256 devices in a mesh: dp: 32 (over x, z), tp: 8 (over y, core).
Axes of the slice: x: 4, y: 4, z: 8, core: 2. Of those that a mesh axis runs over, the one named last changes fastest.
Arguments:
- queries: bfloat16 [512, 128, 576], P('dp', 'tp'), may hold values from -22.5 to 22.5
- new_latent: bfloat16 [512, 576], P('dp'), may hold values from -4.5 to 4.5
- residual: bfloat16 [512, 7168], P('dp', 'tp'), may hold values from -11 to 11
- pool: bfloat16 [4096, 64, 576], P('dp', 'tp'), may hold values from -4.5 to 4.5
- page_owner: int32 [512, 4], P('dp'), may hold values from 0 to 31, as said below
- page_slot: int32 [512, 4], P('dp'), may hold values from 0 to 127, as said below
- lengths: int32 [512], P('dp'), may hold values from 1 to 256, as said below
- resumed: int32 [512], P('dp'), may hold values from 0 to 1, as said below
- value_up: bfloat16 [128, 512, 128], P('tp'), may hold values from -0.25 to 0.25
- out_proj: bfloat16 [16384, 7168], P('dp', 'tp'), may hold values from -0.19921875 to 0.19921875
- norm_gain: float32 [7168], P('tp'), may hold values from 0.1 to 1.9
- gate_weight: bfloat16 [7168, 18432], P('tp', 'dp'), may hold values from -0.0625 to 0.0625
- up_weight: bfloat16 [7168, 18432], P('tp', 'dp'), may hold values from -0.0625 to 0.0625
- down_weight: bfloat16 [18432, 7168], P('dp', 'tp'), may hold values from -0.046875 to 0.046875
Outputs:
- layer_out: bfloat16 [512, 7168], P('dp', 'tp')
The draws below stay inside these ranges and needn't reach their ends.
Inputs may be any that keep to these rules, and one draw needn't show every extreme that they name: `page_owner`: request i is served by rank floor(i / 16). A page p of request i is read when resumed[i] = 1 and p * 64 < lengths[i]. Among the pages of one rank's requests at most 4 have any one owner, and at most 2 of the read ones; in every draw and on every rank some owner holds exactly 4 of them, 2 of them read. `page_slot`: no two pages of any requests share one owner's slot. `lengths`: some request has exactly 256 tokens. `resumed`: the requests of one rank read at most 32 pages in all; some rank reads exactly 32.
All inputs are finite; a program needn't handle non-finite values.
Results may differ from the reference program's by a relative error of at most 0.018.
Values may be sent and summed in bfloat16 or wider, within the bound.
A program may use at most 64 MiB of HBM per device.

```python
from functools import partial
import jax
import jax.numpy as jnp
from jax import lax

D = 7168
FF = 18432
H = 128
KL = 512
KR = 64
VH = 128
PAGE = 64
PAGES = 4
RQ_DEV = 16
REQ = 512
CAPP = 4
CAPU = 2
USED = 32
SLOTS = 128
N_DP = 32


def page_plan(key):
    plan_key = jax.random.fold_in(key, 13)
    count_key, place_key, rank_key = jax.random.split(plan_key, 3)
    cells = RQ_DEV * PAGES
    busy = jax.random.randint(count_key, (N_DP,), USED // 4, USED + 1)
    busy = busy.at[jax.random.randint(place_key, (), 0, N_DP)].set(USED)
    cell_request = jnp.arange(cells, dtype=jnp.int32) // PAGES

    def rank_plan(one_key, rank_busy):
        long_key, perm_key = jax.random.split(one_key)
        longest = jax.random.randint(long_key, (), 0, RQ_DEV)
        shuffle = jax.random.permutation(perm_key, cells).astype(jnp.int32)
        priority = shuffle + jnp.where(cell_request == longest, -cells, 0)
        order = jnp.argsort(jnp.argsort(priority, stable=True), stable=True)
        chosen = (order < rank_busy).astype(jnp.int32)
        return (jnp.sum(chosen.reshape(RQ_DEV, PAGES), axis=1).astype(jnp.int32), longest)
    counts, longest = jax.vmap(rank_plan)(jax.random.split(rank_key, N_DP), busy)
    return (counts, longest)


def route_table(key):
    counts, longest = page_plan(key)
    table_key = jax.random.fold_in(key, 11)
    cells = RQ_DEV * PAGES
    cap_total = N_DP * CAPP
    cap_owner = jnp.arange(cap_total, dtype=jnp.int32) // CAPP
    cap_copy = jnp.arange(cap_total, dtype=jnp.int32) % CAPP
    used_all = (jnp.arange(PAGES, dtype=jnp.int32)[None, None, :] < counts[:, :, None]).reshape(N_DP, cells)

    def rank_routes(rank_key, used_cells):
        chosen_key, shuffle_key, order_key = jax.random.split(rank_key, 3)
        chosen = jax.random.randint(chosen_key, (), 0, N_DP)
        shuffle = jax.random.permutation(shuffle_key, cap_total).astype(jnp.int32)
        base = jnp.where(cap_owner == chosen, 0, cap_total) + shuffle
        first = jnp.argsort(base + jnp.where(cap_copy < CAPU, 0, 2 * cap_total), stable=True)
        second = jnp.argsort(base + jnp.where(cap_copy >= CAPU, 0, 2 * cap_total), stable=True)
        spread = jax.random.permutation(order_key, cells).astype(jnp.int32)
        rank_order = jnp.argsort(jnp.argsort(jnp.where(used_cells, spread, spread + cells), stable=True), stable=True)
        used_total = jnp.sum(used_cells.astype(jnp.int32))
        later = jnp.clip(rank_order - used_total, 0, cap_total - 1)
        picked = jnp.where(used_cells, first[rank_order], second[later])
        return (cap_owner[picked], cap_copy[picked])
    owners, copies = jax.vmap(rank_routes)(jax.random.split(table_key, N_DP), used_all)

    def relabel_owner(slot_key):
        return jax.random.permutation(slot_key, SLOTS).astype(jnp.int32)
    relabel = jax.vmap(relabel_owner)(jax.random.split(jax.random.fold_in(table_key, 5), N_DP))
    rank_ids = jnp.arange(N_DP, dtype=jnp.int32)[:, None]
    slots_used = relabel[owners, rank_ids * CAPP + copies]
    return (owners.reshape(REQ, PAGES).astype(jnp.int32), slots_used.reshape(REQ, PAGES).astype(jnp.int32))


def pool_rows(key, page_rows):
    base_key = jax.random.fold_in(key, 41)

    def single_page(row):
        return jnp.clip(jax.random.normal(jax.random.fold_in(base_key, row), (PAGE, KL + KR), jnp.float32), -4.5, 4.5)
    return jax.vmap(single_page)(page_rows)


def draw_page_owner(key, part):
    owners, slots_used = route_table(key)
    return owners


def draw_page_slot(key, part):
    owners, slots_used = route_table(key)
    return slots_used


def draw_pool(key, part):
    pages_drawn = pool_rows(key, jnp.arange(N_DP * SLOTS, dtype=jnp.int32))
    return pages_drawn.astype(jnp.bfloat16)


def draw_queries(key, part):
    key = jax.random.fold_in(key, 51)
    base_key = jax.random.fold_in(key, 0)
    values = jnp.clip(jax.random.normal(base_key, (REQ, H, KL + KR), jnp.float32), -4.5, 4.5)
    return values.astype(jnp.bfloat16)


def draw_residual(key, part):
    key = jax.random.fold_in(key, 61)
    ramp = jnp.arange(D, dtype=jnp.float32) / D
    values = jnp.clip(jax.random.normal(key, (REQ, D), jnp.float32), -3.5, 3.5) * (0.15 + 3.0 * ramp)
    return values.astype(jnp.bfloat16)


def draw_lengths(key, part):
    counts, longest = page_plan(key)
    key = jax.random.fold_in(key, 21)
    extra_key, free_key = jax.random.split(key)
    extra = jax.random.randint(extra_key, (N_DP, RQ_DEV), 1, PAGE + 1)
    free = jax.random.randint(free_key, (N_DP, RQ_DEV), 1, PAGES * PAGE + 1)
    values = jnp.where(counts > 0, (counts - 1) * PAGE + extra, free)
    is_long = jnp.arange(RQ_DEV, dtype=jnp.int32)[None, :] == longest[:, None]
    values = jnp.where(is_long, PAGES * PAGE, values)
    return values.reshape(REQ).astype(jnp.int32)


def draw_resumed(key, part):
    counts, longest = page_plan(key)
    return (counts > 0).astype(jnp.int32).reshape(REQ)


def shard_levels(key, dims, cuts, smallest, top_value):
    def one(dim, parts):
        draws = jax.random.uniform(jax.random.fold_in(jax.random.fold_in(key, 6), dim), (parts,), jnp.float32, smallest / len(cuts), top_value / len(cuts))
        return jnp.repeat(jnp.exp(draws), dims[dim] // parts).reshape((-1,) + (1,) * (len(dims) - dim - 1))

    loudness = one(*cuts[0])
    for cut in cuts[1:]:
        loudness = loudness * one(*cut)
    return loudness


def centred(own_key, shape, scale, most, pieces=(), kind=jnp.bfloat16):
    values = scale * jax.random.normal(own_key, shape, jnp.float32)
    if pieces:
        values = values * shard_levels(own_key, shape, pieces, -0.22, 0.18)
    return jnp.clip(values, -most, most).astype(kind)


def setup_inputs(seed: int = 0) -> dict:
    splits = jax.random.split(jax.random.key(seed), 15)
    queries = draw_queries(jax.random.fold_in(splits[14], 71), 0)
    new_latent = centred(splits[1], (REQ, KL + KR), 1.0, 4.5, ((0, 32),))
    residual = draw_residual(jax.random.fold_in(splits[14], 71), 0)
    pool = draw_pool(jax.random.fold_in(splits[14], 71), 0)
    page_owner = draw_page_owner(jax.random.fold_in(splits[14], 71), 0)
    page_slot = draw_page_slot(jax.random.fold_in(splits[14], 71), 0)
    lengths = draw_lengths(jax.random.fold_in(splits[14], 71), 0)
    resumed = draw_resumed(jax.random.fold_in(splits[14], 71), 0)
    value_up = centred(splits[8], (H, KL, VH), KL ** -0.5, 0.25, ((0, 8),))
    out_proj = centred(splits[9], (H * VH, D), 0.03125, 0.19921875, ((0, 32), (1, 8)))
    norm_gain = jnp.clip(1.0 + 0.18 * jax.random.normal(splits[10], (D,), jnp.float32), 0.1, 1.9)
    gate_weight = centred(splits[11], (D, FF), D ** -0.5, 0.0625, ((0, 8), (1, 32)))
    up_weight = centred(splits[12], (D, FF), D ** -0.5, 0.0625, ((0, 8), (1, 32)))
    down_weight = centred(splits[13], (FF, D), FF ** -0.5, 0.046875, ((0, 32), (1, 8)))
    return {"queries": queries, "new_latent": new_latent, "residual": residual, "pool": pool, "page_owner": page_owner, "page_slot": page_slot, "lengths": lengths, "resumed": resumed, "value_up": value_up, "out_proj": out_proj, "norm_gain": norm_gain, "gate_weight": gate_weight, "up_weight": up_weight, "down_weight": down_weight}


SCORE_SCALE = 192.0 ** (-0.5)
EPSILON = 1e-06

def rank_attention(pool, rank_parts):
    query_rows, latest_row, owners, slots_used, context, flags = rank_parts
    page_rows = (owners * SLOTS + slots_used).reshape(-1).astype(jnp.int32)
    page_keys = jnp.take(pool, page_rows, axis=0).reshape(RQ_DEV, PAGES * PAGE, KL + KR).astype(jnp.float32)
    query_rows = query_rows.astype(jnp.float32)
    latest_row = latest_row.astype(jnp.float32)
    scores = jnp.einsum('rhc,rtc->rht', query_rows, page_keys) * SCORE_SCALE
    own_score = jnp.einsum('rhc,rc->rh', query_rows, latest_row) * SCORE_SCALE
    position = jnp.arange(PAGES * PAGE, dtype=jnp.int32)
    context_end = jnp.where(flags == 1, context, 0)
    usable = (position[None, :] < context_end[:, None])[:, None, :]
    score_top = jnp.maximum(own_score, lax.optimization_barrier(jnp.max(jnp.where(usable, scores, own_score[:, :, None]), axis=2)))
    weights = jnp.where(usable, jnp.exp(scores - score_top[:, :, None]), 0.0)
    own_weight = jnp.exp(own_score - score_top)
    weight_sum = lax.optimization_barrier(jnp.sum(weights, axis=2)) + own_weight
    rounded = lax.optimization_barrier(weights.astype(jnp.bfloat16))
    latent_sum = jnp.einsum('rht,rtc->rhc', rounded.astype(jnp.float32), page_keys[:, :, :KL])
    latent_sum = latent_sum + own_weight[:, :, None] * latest_row[:, None, :KL]
    return (latent_sum / weight_sum[:, :, None]).astype(jnp.bfloat16)

def reference(queries, new_latent, residual, pool, page_owner, page_slot, lengths, resumed, value_up, out_proj, norm_gain, gate_weight, up_weight, down_weight):
    rank_parts = (queries.reshape(N_DP, RQ_DEV, H, KL + KR), new_latent.reshape(N_DP, RQ_DEV, KL + KR), page_owner.reshape(N_DP, RQ_DEV, PAGES), page_slot.reshape(N_DP, RQ_DEV, PAGES), lengths.reshape(N_DP, RQ_DEV), resumed.reshape(N_DP, RQ_DEV))
    latent_out = lax.map(partial(rank_attention, pool), rank_parts).reshape(REQ, H, KL)
    heads_out = jnp.einsum('rhc,hcv->rhv', latent_out.astype(jnp.float32), value_up.astype(jnp.float32))
    heads_out = heads_out.astype(jnp.bfloat16).reshape(REQ, H * VH)
    attended = jnp.dot(heads_out, out_proj, preferred_element_type=jnp.float32)
    stream = lax.optimization_barrier((residual.astype(jnp.float32) + attended).astype(jnp.bfloat16))
    widened = stream.astype(jnp.float32)
    mean_square = lax.optimization_barrier(jnp.mean(widened * widened, axis=1, keepdims=True))
    normed = (widened * lax.rsqrt(mean_square + EPSILON) * norm_gain).astype(jnp.bfloat16)
    gate_values = jnp.dot(normed, gate_weight, preferred_element_type=jnp.float32)
    up_values = jnp.dot(normed, up_weight, preferred_element_type=jnp.float32)
    hidden = (jax.nn.silu(gate_values) * up_values).astype(jnp.bfloat16)
    lowered = jnp.dot(hidden, down_weight, preferred_element_type=jnp.float32)
    return (widened + lowered).astype(jnp.bfloat16)
```

```python
import functools

import jax
import jax.numpy as jnp
from jax import lax
from jax.experimental import pallas as pl
from jax.experimental.pallas import tpu as pltpu
from jax.sharding import PartitionSpec as P

MESH = pl.DeviceIdType.MESH
F32, BF16, I32 = jnp.float32, jnp.bfloat16, jnp.int32

NX, NY, NZ, NC = 4, 4, 8, 2
REQ_D = 16
HEADS = 16
COLS = 576
KL = 512
VH = 128
TOK = 8
PAGE = 64
PAGES = 4
USED = 32
WIDTH = 896
FFD = 576
D = 7168
SCORE_SCALE = 192.0 ** (-0.5)
EPSILON = 1e-06

FAR_Z = (4, 3, 5, 2, 6, 1, 7)
FAR_X = (2, 1, 3)
FAR_Y = (2, 1, 3)
FAR_DP = sorted(
    ((dx, dz) for dx in range(NX) for dz in range(NZ) if dx or dz),
    key=lambda o: -(min(o[0], NX - o[0]) + min(o[1], NZ - o[1])),
)


def send(src, dst, send_sem, recv_sem, device):
    copy = pltpu.make_async_remote_copy(
        src_ref=src,
        dst_ref=dst,
        send_sem=send_sem,
        recv_sem=recv_sem,
        device_id=device,
        device_id_type=MESH,
    )
    copy.start()


def wait_bytes(ref, sem):
    pltpu.make_async_copy(ref, ref, sem).wait()


def column(row, n):
    rows = lax.broadcasted_iota(I32, (n, n), 0)
    lanes = lax.broadcasted_iota(I32, (n, n), 1)
    return jnp.sum(jnp.where(rows == lanes, row, 0), axis=1, keepdims=True)


def dot(a, b):
    return jnp.dot(a, b, preferred_element_type=F32)


def dot_t(a, b):
    return lax.dot_general(a, b, (((1,), (1,)), ((), ())), preferred_element_type=F32)


def kernel(
    owner_ref, slot_ref, len_ref, res_ref, nl_ref, resid_ref, gain_ref,
    q_hbm, pool_hbm, vup_hbm, wo_hbm, wg_hbm, wu_hbm, wd_hbm,
    out_ref,
    q_v, pool_v, vup_v, wo_v, wg_v, wu_v, wd_v, load_sem,
    want_v, asked_v, asked_s, sel_v, sel_s, limit_v, smem_sem, req_ss, req_rs,
    pg_send, pg_recv, pg_ss, pg_rs,
    keys, key_ss, key_rs, sib_ss, sib_rs,
    qt_v, scores_v,
    hd_send, hd_in, hd_ss, hd_rs,
    hb, hb_ss, hb_rs, hs_ss, hs_rs,
    px_send, px_recv, px_ss, px_rs, pz_own, pz_send, pz_recv, pz_ss, pz_rs,
    stream_v, gat, gz_ss, gz_rs, gx_ss, gx_rs,
    act_v, ssq_send, ssq_recv, ssq_ss, ssq_rs,
    gs_own, gs_send, gs_recv, gs_ss, gs_rs,
    gy_own, gy_send, gy_recv, gy_ss, gy_rs,
    hid, hy_ss, hy_rs, hc_ss, hc_rs,
    dx_send, dx_recv, dx_ss, dx_rs, dz_own, dz_send, dz_recv, dz_ss, dz_rs,
):
    dp, tp = lax.axis_index("dp"), lax.axis_index("tp")
    x, z = dp // NZ, dp % NZ
    y, c = tp // NC, tp % NC

    def at(dx=0, dz=0, dy=0, flip=False):
        core = 1 - c if flip else c
        return (((x + dx) % NX) * NZ + (z + dz) % NZ, ((y + dy) % NY) * NC + core)

    loads = [
        pltpu.make_async_copy(src, dst, load_sem.at[i])
        for i, (src, dst) in enumerate(
            [(pool_hbm, pool_v), (q_hbm, q_v), (vup_hbm, vup_v), (wo_hbm, wo_v),
             (wg_hbm, wg_v), (wu_hbm, wu_v), (wd_hbm, wd_v)]
        )
    ]
    for load in loads:
        load.start()

    barrier = pltpu.get_barrier_semaphore()
    for ox, oz in FAR_DP:
        pl.semaphore_signal(barrier, 1, device_id=at(ox, oz), device_id_type=MESH)
    for oy in FAR_Y:
        pl.semaphore_signal(barrier, 1, device_id=at(dy=oy), device_id_type=MESH)
    pl.semaphore_signal(barrier, 1, device_id=at(flip=True), device_id_type=MESH)
    in_tp = dp // 4
    to_self = jnp.where((tp == in_tp) & (z % 2 == c), 1, 0)

    def greet(k, carry):
        source = 2 * k + c

        @pl.when(jnp.logical_not((source == dp) & (in_tp == tp)))
        def _():
            pl.semaphore_signal(barrier, 1, device_id=(source, in_tp), device_id_type=MESH)

        return carry

    lax.fori_loop(0, 16, greet, 0)

    lengths = column(len_ref[...], REQ_D)
    resumed = column(res_ref[...], REQ_D)
    before = (
        lax.broadcasted_iota(I32, (REQ_D, REQ_D, 1), 1) < lax.broadcasted_iota(I32, (REQ_D, REQ_D, 1), 0)
    ).astype(I32)

    def earlier(v):
        return jnp.sum(before * v[None], axis=1)

    lane = lax.broadcasted_iota(I32, (REQ_D, 128), 1)
    lane_owner = lane % 32
    lane_copy = lane // 32
    page_lane = lax.broadcasted_iota(I32, (REQ_D, USED * TOK), 1) // TOK
    owner_base = jnp.zeros((1, 128), I32)
    read_base = jnp.zeros((1, 128), I32)
    wanted = jnp.zeros((1, 128), I32)
    limit = jnp.zeros((REQ_D, USED * TOK), I32)
    chosen = jnp.zeros((1, USED * TOK), I32)
    for p in range(PAGES):
        owner = owner_ref[:, p : p + 1]
        read = jnp.where((resumed == 1) & (lengths > p * PAGE), 1, 0)
        match = jnp.where(lane_owner == owner, read, 0)
        copy = owner_base + earlier(match)
        owner_base = owner_base + jnp.sum(match, axis=0, keepdims=True)
        wanted = wanted + jnp.sum(
            jnp.where((match > 0) & (copy == lane_copy), slot_ref[:, p : p + 1], 0), axis=0, keepdims=True
        )
        own_copy = jnp.sum(jnp.where(lane < 32, match * copy, 0), axis=1, keepdims=True)
        read_lanes = jnp.broadcast_to(read, (REQ_D, 128))
        place = (read_base + earlier(read_lanes))[:, 0:1]
        read_base = read_base + jnp.sum(read_lanes, axis=0, keepdims=True)
        here = jnp.where(page_lane == place, read, 0)
        limit = limit + here * (lengths - p * PAGE)
        off_x = (x - owner // NZ + NX) % NX
        off_z = (z - owner % NZ + NZ) % NZ
        source = (off_x * NZ + off_z) * 2 + own_copy
        chosen = chosen + jnp.sum(here * source, axis=0, keepdims=True)
    limit_v[...] = limit.astype(F32)
    want_v[0] = wanted
    asked_v[0] = wanted
    sel_v[0] = chosen
    sel_copy = pltpu.make_async_copy(sel_v, sel_s, smem_sem.at[0])
    sel_copy.start()

    pl.semaphore_wait(barrier, 31 + 4 + 16 - to_self)

    for ox, oz in FAR_DP:
        send(want_v.at[0], asked_v.at[ox * NZ + oz], req_ss, req_rs, at(ox, oz))

    loads[1].wait()
    rows = lax.broadcasted_iota(I32, (256, 256), 0)
    lanes = lax.broadcasted_iota(I32, (256, 256), 1)
    swap = jnp.where(lanes == (rows % 16) * 16 + rows // 16, 1.0, 0.0).astype(BF16)
    qt = dot(swap, q_v[...]).astype(BF16)
    qt_v[...] = qt
    own_all = dot_t(qt, nl_ref[...]) * SCORE_SCALE
    own_diag = lax.broadcasted_iota(I32, (256, 16), 1) == lax.broadcasted_iota(I32, (256, 16), 0) % 16
    own_score = jnp.sum(jnp.where(own_diag, own_all, 0.0), axis=1, keepdims=True)
    loads[0].wait()
    sel_copy.wait()

    wait_bytes(asked_v.at[pl.ds(1, 31)], req_rs)
    asked_copy = pltpu.make_async_copy(asked_v, asked_s, smem_sem.at[1])
    asked_copy.start()
    asked_copy.wait()

    def gather(n_in, buffer, n_out):
        pair = [pool_v[jnp.clip(asked_s[n_in, 0, 32 * k + dp], 0, 127)] for k in range(2)]
        buffer[n_out] = jnp.concatenate(pair, axis=0)

    for ox, oz in FAR_DP:
        n_out = ox * NZ + oz
        gather(((NX - ox) % NX) * NZ + (NZ - oz) % NZ, pg_send, n_out)
        send(pg_send.at[n_out], pg_recv.at[n_out], pg_ss, pg_rs, at(ox, oz))
    gather(0, pg_recv, 0)
    wait_bytes(pg_recv.at[pl.ds(1, 31)], pg_rs)

    def pick(u, carry):
        pair = []
        for k in range(2):
            source = jnp.clip(sel_s[0, 0, (2 * u + k) * TOK], 0, 63)
            both = pg_recv[lax.shift_right_logical(source, 1)]
            pair.append(jnp.where(jnp.bitwise_and(source, 1) == 1, both[TOK:], both[:TOK]))
        keys[0, pl.ds(pl.multiple_of(u * 16, 16), 16), :] = jnp.concatenate(pair, axis=0)
        return carry

    lax.fori_loop(0, USED // 2, pick, 0)
    for oy in FAR_Y:
        send(keys.at[0], keys.at[oy], key_ss, key_rs.at[oy], at(dy=oy))
    send(keys.at[0], keys.at[4], sib_ss, sib_rs.at[0], at(flip=True))

    qt = qt_v[...]
    limit = limit_v[...].reshape(1, REQ_D, USED * TOK)
    token = (lax.broadcasted_iota(I32, (1, 1, USED * TOK), 2) % TOK).astype(F32)

    def score_block(n, source_tp):
        block = (dot_t(qt, keys[n]) * SCORE_SCALE).reshape(HEADS, REQ_D, USED * TOK)
        usable = limit > token + (source_tp * TOK).astype(F32)
        block = jnp.where(usable, block, -jnp.inf)
        scores_v[n] = block.reshape(256, USED * TOK)

    def source_of(n):
        core = c if n < 4 else 1 - c
        return ((y + NY - n % 4) % NY) * NC + core

    score_block(0, source_of(0))
    for oy in (1, 3, 2):
        wait_bytes(keys.at[oy], key_rs.at[oy])
        send(keys.at[oy], keys.at[4 + oy], sib_ss, sib_rs.at[oy], at(flip=True))
        score_block(oy, source_of(oy))
    for oy in (0, 1, 3, 2):
        wait_bytes(keys.at[4 + oy], sib_rs.at[oy])
        score_block(4 + oy, source_of(4 + oy))

    peak = scores_v[0]
    for n in range(1, 8):
        peak = jnp.maximum(peak, scores_v[n])
    top = jnp.maximum(own_score, jnp.max(peak, axis=1, keepdims=True))
    own_weight = jnp.exp(own_score - top)
    weight_lanes = jnp.zeros((256, USED * TOK), F32)
    latent = jnp.zeros((256, KL), F32)
    for n in range(8):
        weights = jnp.exp(scores_v[n] - top)
        weight_lanes = weight_lanes + weights
        latent = latent + dot(weights.astype(BF16), keys[n, :, :KL])
    weight_sum = own_weight + jnp.sum(weight_lanes, axis=1, keepdims=True)
    own_latent = nl_ref[:, :KL].astype(F32).reshape(1, REQ_D, KL)
    latent = latent.reshape(HEADS, REQ_D, KL) + own_weight.reshape(HEADS, REQ_D, 1) * own_latent
    latent = (latent / weight_sum.reshape(HEADS, REQ_D, 1)).astype(BF16)

    loads[2].wait()
    for h in range(HEADS):
        hd_send[h] = dot(latent[h], vup_v[h]).astype(BF16)
        target = (4 * tp + h // 4, (h % 4) * NC + z % 2)
        is_me = (target[0] == dp) & (target[1] == tp)

        @pl.when(is_me)
        def _():
            pltpu.make_async_copy(hd_send.at[h], hd_in.at[dp // 2], hd_rs).start()

        @pl.when(jnp.logical_not(is_me))
        def _():
            send(hd_send.at[h], hd_in.at[dp // 2], hd_ss, hd_rs, target)

    wait_bytes(hd_in, hd_rs)
    own_cols = pl.ds(pl.multiple_of(y * VH, VH), VH)
    hb[:, pl.ds(c, 1), :, own_cols] = hd_in[...].reshape(NX, 1, 64, VH)
    own_block = hb.at[:, c, :, own_cols]
    for oy in FAR_Y:
        send(own_block, own_block, hb_ss, hb_rs.at[oy], at(dy=oy))
    send(own_block, own_block, hs_ss, hs_rs.at[0], at(flip=True))
    for oy in (1, 3, 2):
        cols = pl.ds(pl.multiple_of(((y + NY - oy) % NY) * VH, VH), VH)
        block = hb.at[:, c, :, cols]
        wait_bytes(block, hb_rs.at[oy])
        send(block, block, hs_ss, hs_rs.at[oy], at(flip=True))
    for oy in range(4):
        wait_bytes(own_block, hs_rs.at[oy])

    def reduce_scatter(rows_of, weight, place, x_send, x_recv, x_ss, x_rs, z_own, z_send, z_recv, z_ss, z_rs):
        for ox in FAR_X:
            x_send[ox - 1] = dot(rows_of((x + ox) % NX), weight).astype(BF16)
            send(x_send.at[ox - 1], x_recv.at[ox - 1], x_ss, x_rs, at(dx=ox))
        total = dot(rows_of(x), weight)
        wait_bytes(x_recv, x_rs)
        for n in range(3):
            total = total + x_recv[n].astype(F32)
        total = total.reshape(NZ, REQ_D, WIDTH)
        z_own[...] = total
        z_send[...] = total.astype(BF16)
        for oz in FAR_Z:
            send(z_send.at[place((z + oz) % NZ)], z_recv.at[oz - 1], z_ss, z_rs, at(dz=oz))
        mine = z_own[place(z)]
        wait_bytes(z_recv, z_rs)
        for n in range(7):
            mine = mine + z_recv[n].astype(F32)
        return mine

    loads[3].wait()
    attended = reduce_scatter(
        lambda xx: hb[xx].reshape(128, 512), wo_v[...], lambda zz: (zz % 2) * 4 + zz // 2,
        px_send, px_recv, px_ss, px_rs, pz_own, pz_send, pz_recv, pz_ss, pz_rs,
    )
    stream = (resid_ref[...].astype(F32) + attended).astype(BF16)
    stream_v[...] = stream

    gat[x, z] = stream
    for oz in FAR_Z:
        send(gat.at[x, z], gat.at[x, z], gz_ss, gz_rs, at(dz=oz))
    wait_bytes(gat.at[x, pl.ds(0, 7)], gz_rs)
    for ox in FAR_X:
        send(gat.at[x], gat.at[x], gx_ss, gx_rs.at[ox - 1], at(dx=ox))

    def widen(xx):
        block = gat[xx].reshape(128, WIDTH).astype(F32)
        act_v[xx] = (block * gain_ref[...]).astype(BF16)
        square = block * block
        high = square.astype(BF16)
        low = (square - high.astype(F32)).astype(BF16)
        ones = jnp.ones((8, WIDTH), BF16)
        ssq_send[xx] = dot_t(ones, high) + dot_t(ones, low)

    widen(x)
    for ox in (1, 3, 2):
        xx = (x + NX - ox) % NX
        wait_bytes(gat.at[xx], gx_rs.at[ox - 1])
        widen(xx)
    for n, (oy, flip) in enumerate([(2, True), (2, False), (1, True), (3, True), (1, False), (3, False), (0, True)]):
        send(ssq_send, ssq_recv.at[n], ssq_ss, ssq_rs, at(dy=oy, flip=flip))

    loads[4].wait()
    loads[5].wait()

    def products(half):
        act = act_v[pl.ds(half * 2, 2)].reshape(256, WIDTH)
        return dot(act, wg_v[...]), dot(act, wu_v[...])

    gate, up = products(1 - c)
    gs_send[0] = gate.astype(BF16)
    gs_send[1] = up.astype(BF16)
    send(gs_send, gs_recv, gs_ss, gs_rs, at(flip=True))
    gate, up = products(c)
    gs_own[0] = gate.reshape(NY, 64, FFD)
    gs_own[1] = up.reshape(NY, 64, FFD)
    wait_bytes(gs_recv, gs_rs)
    for oy in FAR_Y:
        yy = (y + oy) % NY
        for k in range(2):
            pair = gs_own[k, yy] + gs_recv[k, pl.ds(pl.multiple_of(yy * 64, 64), 64), :].astype(F32)
            gy_send[oy - 1, k] = pair.astype(BF16)
        send(gy_send.at[oy - 1], gy_recv.at[oy - 1], gy_ss, gy_rs, at(dy=oy))
    gate, up = (
        gs_own[k, y] + gs_recv[k, pl.ds(pl.multiple_of(y * 64, 64), 64), :].astype(F32) for k in range(2)
    )
    wait_bytes(ssq_recv, ssq_rs)
    squares = ssq_send[...]
    for n in range(7):
        squares = squares + ssq_recv[n]
    row_id = lax.broadcasted_iota(I32, (64, 128), 0) + c * 256 + y * 64
    lane_id = lax.broadcasted_iota(I32, (64, 128), 1)
    mean = jnp.zeros((64, 1), F32)
    for n in range(NX):
        mean = mean + jnp.sum(
            jnp.where(row_id == lane_id + 128 * n, squares[n, 0:1, :], 0.0), axis=1, keepdims=True
        )
    scale = lax.rsqrt(mean / D + EPSILON)
    wait_bytes(gy_recv, gy_rs)
    for n in range(3):
        gate = gate + gy_recv[n, 0].astype(F32)
        up = up + gy_recv[n, 1].astype(F32)
    gate = gate * scale
    hidden = (gate / (1.0 + jnp.exp(-gate)) * (up * scale)).astype(BF16)

    hid[c, y] = hidden
    for oy in FAR_Y:
        send(hid.at[c, y], hid.at[c, y], hy_ss, hy_rs.at[oy - 1], at(dy=oy))
    send(hid.at[c, y], hid.at[c, y], hc_ss, hc_rs, at(flip=True))
    for oy in (1, 3, 2):
        yy = (y + NY - oy) % NY
        wait_bytes(hid.at[c, yy], hy_rs.at[oy - 1])
        send(hid.at[c, yy], hid.at[c, yy], hc_ss, hc_rs, at(flip=True))
    wait_bytes(hid.at[1 - c], hc_rs)

    loads[6].wait()
    lowered = reduce_scatter(
        lambda xx: hid[xx // 2, pl.ds((xx % 2) * 2, 2)].reshape(128, FFD), wd_v[...], lambda zz: zz,
        dx_send, dx_recv, dx_ss, dx_rs, dz_own, dz_send, dz_recv, dz_ss, dz_rs,
    )
    out_ref[...] = (stream_v[...].astype(F32) + lowered).astype(BF16)

    wait_bytes(asked_v.at[pl.ds(1, 31)], req_ss)
    wait_bytes(pg_send.at[pl.ds(1, 31)], pg_ss)
    wait_bytes(keys.at[pl.ds(0, 3)], key_ss)
    wait_bytes(keys.at[pl.ds(0, 4)], sib_ss)
    wait_bytes(hd_in.at[pl.ds(0, 15)], hd_ss)

    @pl.when(to_self == 0)
    def _():
        wait_bytes(hd_in.at[0], hd_ss)

    for _ in range(3):
        wait_bytes(own_block, hb_ss)
    for _ in range(4):
        wait_bytes(own_block, hs_ss)
    wait_bytes(px_recv, px_ss)
    wait_bytes(pz_recv, pz_ss)
    wait_bytes(gat.at[x, pl.ds(0, 7)], gz_ss)
    wait_bytes(gat.at[pl.ds(0, 3)], gx_ss)
    wait_bytes(ssq_recv, ssq_ss)
    wait_bytes(gs_send, gs_ss)
    wait_bytes(gy_send, gy_ss)
    wait_bytes(hid.at[0, pl.ds(0, 3)], hy_ss)
    wait_bytes(hid.at[0], hc_ss)
    wait_bytes(dx_recv, dx_ss)
    wait_bytes(dz_recv, dz_ss)


def per_device(
    queries, new_latent, residual, pool, page_owner, page_slot, lengths, resumed,
    value_up, out_proj, norm_gain, gate_weight, up_weight, down_weight,
):
    vmem = pl.BlockSpec(memory_space=pltpu.VMEM)
    anywhere = pl.BlockSpec(memory_space=pl.ANY)
    dma, V = pltpu.SemaphoreType.DMA, pltpu.VMEM
    one = dma
    rs_scratch = [
        V((3, 128, WIDTH), BF16), V((3, 128, WIDTH), BF16), one, one,
        V((NZ, REQ_D, WIDTH), F32), V((NZ, REQ_D, WIDTH), BF16), V((7, REQ_D, WIDTH), BF16), one, one,
    ]
    scratch = [
        V((256, COLS), BF16), V((128, TOK, COLS), BF16), V((HEADS, KL, VH), BF16), V((512, WIDTH), BF16),
        V((WIDTH, FFD), BF16), V((WIDTH, FFD), BF16), V((FFD, WIDTH), BF16), dma((7,)),
        V((1, 1, 128), I32), V((32, 1, 128), I32), pltpu.SMEM((32, 1, 128), I32),
        V((1, 1, 256), I32), pltpu.SMEM((1, 1, 256), I32), V((REQ_D, 256), F32), dma((2,)), one, one,
        V((32, 16, COLS), BF16), V((32, 16, COLS), BF16), one, one,
        V((8, 256, COLS), BF16), one, dma((4,)), one, dma((4,)),
        V((256, COLS), BF16), V((8, 256, 256), F32),
        V((HEADS, 16, VH), BF16), V((16, 16, VH), BF16), one, one,
        V((NX, NC, 64, 512), BF16), one, dma((4,)), one, dma((4,)),
        *rs_scratch,
        V((REQ_D, WIDTH), BF16), V((NX, NZ, REQ_D, WIDTH), BF16), one, one, one, dma((3,)),
        V((NX, 128, WIDTH), BF16), V((NX, 8, 128), F32), V((7, NX, 8, 128), F32), one, one,
        V((2, NY, 64, FFD), F32), V((2, 256, FFD), BF16), V((2, 256, FFD), BF16), one, one,
        V((8, 128), F32), V((3, 2, 64, FFD), BF16), V((3, 2, 64, FFD), BF16), one, one,
        V((NC, NY, 64, FFD), BF16), one, dma((3,)), one, one,
        *rs_scratch,
    ]
    return pl.pallas_call(
        kernel,
        out_shape=jax.ShapeDtypeStruct((REQ_D, WIDTH), BF16),
        in_specs=[vmem] * 7 + [anywhere] * 7,
        out_specs=vmem,
        scratch_shapes=scratch,
        compiler_params=pltpu.CompilerParams(
            collective_id=0, has_side_effects=True, vmem_limit_bytes=56 * 1024 * 1024
        ),
        name="layer",
    )(
        page_owner, page_slot, lengths.reshape(1, REQ_D), resumed.reshape(1, REQ_D), new_latent, residual,
        norm_gain.reshape(1, WIDTH), queries.reshape(256, COLS), pool, value_up, out_proj,
        gate_weight, up_weight, down_weight,
    )


def solution(mesh):
    return jax.shard_map(
        per_device,
        mesh=mesh,
        in_specs=(
            P("dp", "tp", None), P("dp", None), P("dp", "tp"), P("dp", "tp", None), P("dp", None), P("dp", None),
            P("dp"), P("dp"), P("tp", None, None), P("dp", "tp"), P("tp"), P("tp", "dp"), P("tp", "dp"),
            P("dp", "tp"),
        ),
        out_specs=P("dp", "tp"),
        check_vma=False,
    )
```

```python
import functools

import jax
import jax.numpy as jnp
from jax import lax
from jax.experimental import pallas as pl
from jax.experimental.pallas import tpu as pltpu
from jax.sharding import PartitionSpec as P

MESH = pl.DeviceIdType.MESH
F32, BF16, I32 = jnp.float32, jnp.bfloat16, jnp.int32

NX, NY, NZ, NC = 4, 4, 8, 2
REQ_D = 16
HEADS = 16
COLS = 576
KL = 512
VH = 128
TOK = 8
PAGE = 64
PAGES = 4
USED = 32
WIDTH = 896
FFD = 576
D = 7168
SCORE_SCALE = 192.0 ** (-0.5)
EPSILON = 1e-06

FAR_Z = (4, 3, 5, 2, 6, 1, 7)
FAR_X = (2, 1, 3)
FAR_Y = (2, 1, 3)
FAR_DP = sorted(
    ((dx, dz) for dx in range(NX) for dz in range(NZ) if dx or dz),
    key=lambda o: -(min(o[0], NX - o[0]) + min(o[1], NZ - o[1])),
)


def send(src, dst, send_sem, recv_sem, device):
    copy = pltpu.make_async_remote_copy(
        src_ref=src,
        dst_ref=dst,
        send_sem=send_sem,
        recv_sem=recv_sem,
        device_id=device,
        device_id_type=MESH,
    )
    copy.start()


def wait_bytes(ref, sem):
    pltpu.make_async_copy(ref, ref, sem).wait()


def column(row, n):
    rows = lax.broadcasted_iota(I32, (n, n), 0)
    lanes = lax.broadcasted_iota(I32, (n, n), 1)
    return jnp.sum(jnp.where(rows == lanes, row, 0), axis=1, keepdims=True)


def dot(a, b):
    return jnp.dot(a, b, preferred_element_type=F32)


def dot_t(a, b):
    return lax.dot_general(a, b, (((1,), (1,)), ((), ())), preferred_element_type=F32)


def kernel(
    owner_ref, slot_ref, len_ref, res_ref, nl_ref, resid_ref, gain_ref,
    q_hbm, pool_hbm, vup_hbm, wo_hbm, wg_hbm, wu_hbm, wd_hbm,
    out_ref,
    q_v, pool_t, pool_v, vup_v, wo_v, wgu_v, wd_v, load_sem,
    want_v, asked_v, asked_s, sel_v, sel_s, limit_v, smem_sem, req_ss, req_rs,
    pg_send, pg_recv, pg_ss, pg_rs,
    keys, key_ss, key_rs, sib_ss, sib_rs,
    qt_v, scores_v,
    hd_send, hd_in, hd_ss, hd_rs,
    hb, hb_ss, hb_rs, hs_ss, hs_rs,
    px_send, px_recv, px_ss, px_rs, pz_own, pz_send, pz_recv, pz_ss, pz_rs,
    stream_v, gat, gz_ss, gz_rs, gx_ss, gx_rs,
    act_v, ssq_send, ssq_recv, ssq_ss, ssq_rs,
    gs_own, gs_send, gs_recv, gs_ss, gs_rs,
    gy_send, gy_recv, gy_ss, gy_rs,
    hid, hy_ss, hy_rs, hc_ss, hc_rs,
    dx_send, dx_recv, dx_ss, dx_rs, dz_own, dz_send, dz_recv, dz_ss, dz_rs,
):
    dp, tp = lax.axis_index("dp"), lax.axis_index("tp")
    x, z = dp // NZ, dp % NZ
    y, c = tp // NC, tp % NC

    def at(dx=0, dz=0, dy=0, flip=False):
        core = 1 - c if flip else c
        return (((x + dx) % NX) * NZ + (z + dz) % NZ, ((y + dy) % NY) * NC + core)

    loads = [
        pltpu.make_async_copy(src, dst, load_sem.at[i])
        for i, (src, dst) in enumerate(
            [(pool_hbm, pool_t), (q_hbm, q_v), (vup_hbm, vup_v), (wo_hbm, wo_v),
             (wg_hbm, wgu_v.at[pl.ds(0, FFD)]), (wu_hbm, wgu_v.at[pl.ds(FFD, FFD)]), (wd_hbm, wd_v)]
        )
    ]
    for load in loads:
        load.start()
    ends = []

    def later(ref, sem):
        ends.append(lambda: wait_bytes(ref, sem))


    barrier = pltpu.get_barrier_semaphore()
    for ox, oz in FAR_DP:
        pl.semaphore_signal(barrier, 1, device_id=at(ox, oz), device_id_type=MESH)
    for oy in FAR_Y:
        pl.semaphore_signal(barrier, 1, device_id=at(dy=oy), device_id_type=MESH)
    pl.semaphore_signal(barrier, 1, device_id=at(flip=True), device_id_type=MESH)
    in_tp = dp // 4
    to_self = jnp.where((tp == in_tp) & (z % 2 == c), 1, 0)

    def greet(k, carry):
        source = 2 * k + c

        @pl.when(jnp.logical_not((source == dp) & (in_tp == tp)))
        def _():
            pl.semaphore_signal(barrier, 1, device_id=(source, in_tp), device_id_type=MESH)

        return carry

    lax.fori_loop(0, 16, greet, 0)

    lengths = column(len_ref[...], REQ_D)
    resumed = column(res_ref[...], REQ_D)
    before = (
        lax.broadcasted_iota(I32, (REQ_D, REQ_D, 1), 1) < lax.broadcasted_iota(I32, (REQ_D, REQ_D, 1), 0)
    ).astype(I32)

    def earlier(v):
        return jnp.sum(before * v[None], axis=1)

    lane = lax.broadcasted_iota(I32, (REQ_D, 128), 1)
    lane_owner = lane % 32
    lane_copy = lane // 32
    page_lane = lax.broadcasted_iota(I32, (REQ_D, USED * TOK), 1) // TOK
    owner_base = jnp.zeros((1, 128), I32)
    read_base = jnp.zeros((1, 128), I32)
    wanted = jnp.zeros((1, 128), I32)
    limit = jnp.zeros((REQ_D, USED * TOK), I32)
    chosen = jnp.zeros((1, USED * TOK), I32)
    for p in range(PAGES):
        owner = column(owner_ref[p : p + 1, :], REQ_D)
        read = jnp.where((resumed == 1) & (lengths > p * PAGE), 1, 0)
        match = jnp.where(lane_owner == owner, read, 0)
        copy = owner_base + earlier(match)
        owner_base = owner_base + jnp.sum(match, axis=0, keepdims=True)
        wanted = wanted + jnp.sum(
            jnp.where((match > 0) & (copy == lane_copy), column(slot_ref[p : p + 1, :], REQ_D), 0),
            axis=0, keepdims=True,
        )
        own_copy = jnp.sum(jnp.where(lane < 32, match * copy, 0), axis=1, keepdims=True)
        read_lanes = jnp.broadcast_to(read, (REQ_D, 128))
        place = (read_base + earlier(read_lanes))[:, 0:1]
        read_base = read_base + jnp.sum(read_lanes, axis=0, keepdims=True)
        here = jnp.where(page_lane == place, read, 0)
        limit = limit + here * (lengths - p * PAGE)
        off_x = (x - owner // NZ + NX) % NX
        off_z = (z - owner % NZ + NZ) % NZ
        source = (off_x * NZ + off_z) * 2 + own_copy
        chosen = chosen + jnp.sum(here * source, axis=0, keepdims=True)
    limit_v[...] = limit.astype(F32)
    want_v[0] = wanted
    asked_v[0] = wanted
    sel_v[0] = chosen
    sel_copy = pltpu.make_async_copy(sel_v, sel_s, smem_sem.at[0])
    sel_copy.start()

    pl.semaphore_wait(barrier, 31 + 4 + 16 - to_self)

    for ox, oz in FAR_DP:
        send(want_v.at[0], asked_v.at[ox * NZ + oz], req_ss, req_rs, at(ox, oz))
    later(asked_v.at[pl.ds(1, 31)], req_ss)

    loads[1].wait()
    rows = lax.broadcasted_iota(I32, (256, 256), 0)
    lanes = lax.broadcasted_iota(I32, (256, 256), 1)
    swap = jnp.where(lanes == (rows % 16) * 16 + rows // 16, 1.0, 0.0).astype(BF16)
    qt = dot(swap, q_v[...]).astype(BF16)
    qt_v[...] = qt
    own_all = dot_t(qt, nl_ref[...]) * SCORE_SCALE
    own_diag = lax.broadcasted_iota(I32, (256, 16), 1) == lax.broadcasted_iota(I32, (256, 16), 0) % 16
    own_score = jnp.sum(jnp.where(own_diag, own_all, 0.0), axis=1, keepdims=True)
    loads[0].wait()
    token_row = lax.broadcasted_iota(I32, (1024, 128), 0)
    slot_lane = lax.broadcasted_iota(I32, (1024, 128), 1)
    pages = jnp.zeros((1024, COLS), F32)
    for j in range(TOK):
        spread = jnp.where(token_row == slot_lane * TOK + j, 1.0, 0.0).astype(BF16)
        pages = pages + dot_t(spread, pool_t[j])
    pool_v[...] = pages.astype(BF16).reshape(128, TOK, COLS)
    sel_copy.wait()

    wait_bytes(asked_v.at[pl.ds(1, 31)], req_rs)
    asked_copy = pltpu.make_async_copy(asked_v, asked_s, smem_sem.at[1])
    asked_copy.start()
    asked_copy.wait()

    def gather(n_in, buffer, n_out):
        pair = [pool_v[jnp.clip(asked_s[n_in, 0, 32 * k + dp], 0, 127)] for k in range(2)]
        buffer[n_out] = jnp.concatenate(pair, axis=0)

    for ox, oz in FAR_DP:
        n_out = ox * NZ + oz
        gather(((NX - ox) % NX) * NZ + (NZ - oz) % NZ, pg_send, n_out)
        send(pg_send.at[n_out], pg_recv.at[n_out], pg_ss, pg_rs, at(ox, oz))
    later(pg_send.at[pl.ds(1, 31)], pg_ss)
    gather(0, pg_recv, 0)
    wait_bytes(pg_recv.at[pl.ds(1, 31)], pg_rs)

    def pick(u, carry):
        pair = []
        for k in range(2):
            source = jnp.clip(sel_s[0, 0, (2 * u + k) * TOK], 0, 63)
            both = pg_recv[lax.shift_right_logical(source, 1)]
            pair.append(jnp.where(jnp.bitwise_and(source, 1) == 1, both[TOK:], both[:TOK]))
        keys[0, pl.ds(pl.multiple_of(u * 16, 16), 16), :] = jnp.concatenate(pair, axis=0)
        return carry

    lax.fori_loop(0, USED // 2, pick, 0)
    for oy in FAR_Y:
        send(keys.at[0], keys.at[oy], key_ss, key_rs.at[oy], at(dy=oy))
    send(keys.at[0], keys.at[4], sib_ss, sib_rs.at[0], at(flip=True))
    later(keys.at[pl.ds(0, 3)], key_ss)
    later(keys.at[pl.ds(0, 4)], sib_ss)

    qt = qt_v[...]
    limit = limit_v[...].reshape(1, REQ_D, USED * TOK)
    token = (lax.broadcasted_iota(I32, (1, 1, USED * TOK), 2) % TOK).astype(F32)

    def score_block(n, source_tp):
        block = (dot_t(qt, keys[n]) * SCORE_SCALE).reshape(HEADS, REQ_D, USED * TOK)
        usable = limit > token + (source_tp * TOK).astype(F32)
        block = jnp.where(usable, block, -jnp.inf)
        scores_v[n] = block.reshape(256, USED * TOK)

    def source_of(n):
        core = c if n < 4 else 1 - c
        return ((y + NY - n % 4) % NY) * NC + core

    score_block(0, source_of(0))
    for oy in (1, 3, 2):
        wait_bytes(keys.at[oy], key_rs.at[oy])
        send(keys.at[oy], keys.at[4 + oy], sib_ss, sib_rs.at[oy], at(flip=True))
        score_block(oy, source_of(oy))
    for oy in (0, 1, 3, 2):
        wait_bytes(keys.at[4 + oy], sib_rs.at[oy])
        score_block(4 + oy, source_of(4 + oy))

    peak = scores_v[0]
    for n in range(1, 8):
        peak = jnp.maximum(peak, scores_v[n])
    top = jnp.maximum(own_score, jnp.max(peak, axis=1, keepdims=True))
    own_weight = jnp.exp(own_score - top)
    weight_lanes = jnp.zeros((256, USED * TOK), F32)
    latent = jnp.zeros((256, KL), F32)
    for n in range(8):
        weights = jnp.exp(scores_v[n] - top)
        weight_lanes = weight_lanes + weights
        latent = latent + dot(weights.astype(BF16), keys[n, :, :KL])
    weight_sum = own_weight + jnp.sum(weight_lanes, axis=1, keepdims=True)
    own_latent = nl_ref[:, :KL].astype(F32).reshape(1, REQ_D, KL)
    latent = latent.reshape(HEADS, REQ_D, KL) + own_weight.reshape(HEADS, REQ_D, 1) * own_latent
    latent = (latent / weight_sum.reshape(HEADS, REQ_D, 1)).astype(BF16)

    loads[2].wait()
    for h in range(HEADS):
        hd_send[h] = dot(latent[h], vup_v[h]).astype(BF16)
        target = (4 * tp + h // 4, (h % 4) * NC + z % 2)
        is_me = (target[0] == dp) & (target[1] == tp)

        @pl.when(is_me)
        def _():
            pltpu.make_async_copy(hd_send.at[h], hd_in.at[dp // 2], hd_rs).start()

        @pl.when(jnp.logical_not(is_me))
        def _():
            send(hd_send.at[h], hd_in.at[dp // 2], hd_ss, hd_rs, target)

    def heads_left():
        wait_bytes(hd_in.at[pl.ds(0, 15)], hd_ss)

        @pl.when(to_self == 0)
        def _():
            wait_bytes(hd_in.at[0], hd_ss)

    ends.append(heads_left)

    wait_bytes(hd_in, hd_rs)
    own_cols = pl.ds(pl.multiple_of(y * VH, VH), VH)
    hb[:, pl.ds(c, 1), :, own_cols] = hd_in[...].reshape(NX, 1, 64, VH)
    own_block = hb.at[:, c, :, own_cols]
    for oy in FAR_Y:
        send(own_block, own_block, hb_ss, hb_rs.at[oy], at(dy=oy))
    send(own_block, own_block, hs_ss, hs_rs.at[0], at(flip=True))
    later(hb.at[:, pl.ds(0, 1), :, pl.ds(0, 3 * VH)], hb_ss)
    later(hb.at[:, 0], hs_ss)
    for oy in (1, 3, 2):
        cols = pl.ds(pl.multiple_of(((y + NY - oy) % NY) * VH, VH), VH)
        block = hb.at[:, c, :, cols]
        wait_bytes(block, hb_rs.at[oy])
        send(block, block, hs_ss, hs_rs.at[oy], at(flip=True))
    for oy in range(4):
        wait_bytes(own_block, hs_rs.at[oy])

    def reduce_scatter(rows_of, weight, place, x_send, x_recv, x_ss, x_rs, z_own, z_send, z_recv, z_ss, z_rs):
        for ox in FAR_X:
            x_send[ox - 1] = dot(rows_of((x + ox) % NX), weight).astype(BF16)
            send(x_send.at[ox - 1], x_recv.at[ox - 1], x_ss, x_rs, at(dx=ox))
        later(x_send, x_ss)
        total = dot(rows_of(x), weight)
        wait_bytes(x_recv, x_rs)
        for n in range(3):
            total = total + x_recv[n].astype(F32)
        total = total.reshape(NZ, REQ_D, WIDTH)
        z_own[...] = total
        z_send[...] = total.astype(BF16)
        for oz in FAR_Z:
            send(z_send.at[place((z + oz) % NZ)], z_recv.at[oz - 1], z_ss, z_rs, at(dz=oz))
        later(z_recv, z_ss)
        mine = z_own[place(z)]
        wait_bytes(z_recv, z_rs)
        for n in range(7):
            mine = mine + z_recv[n].astype(F32)
        return mine

    loads[3].wait()
    attended = reduce_scatter(
        lambda xx: hb[xx].reshape(128, 512), wo_v[...], lambda zz: (zz % 2) * 4 + zz // 2,
        px_send, px_recv, px_ss, px_rs, pz_own, pz_send, pz_recv, pz_ss, pz_rs,
    )
    stream = (resid_ref[...].astype(F32) + attended).astype(BF16)
    stream_v[...] = stream

    gat[x, z] = stream
    for oz in FAR_Z:
        send(gat.at[x, z], gat.at[x, z], gz_ss, gz_rs, at(dz=oz))
    later(gat.at[0, pl.ds(0, 7)], gz_ss)
    wait_bytes(gat.at[x, pl.ds(0, 7)], gz_rs)
    for ox in FAR_X:
        send(gat.at[x], gat.at[x], gx_ss, gx_rs.at[ox - 1], at(dx=ox))
    later(gat.at[pl.ds(0, 3)], gx_ss)

    def widen(xx):
        block = gat[xx].reshape(128, WIDTH).astype(F32)
        act_v[xx] = (block * gain_ref[...].reshape(1, WIDTH)).astype(BF16)
        square = block * block
        high = square.astype(BF16)
        low = (square - high.astype(F32)).astype(BF16)
        ones = jnp.ones((8, WIDTH), BF16)
        ssq_send[xx] = dot_t(ones, high) + dot_t(ones, low)

    widen(x)
    for ox in (1, 3, 2):
        xx = (x + NX - ox) % NX
        wait_bytes(gat.at[xx], gx_rs.at[ox - 1])
        widen(xx)
    for n, (oy, flip) in enumerate([(2, True), (2, False), (1, True), (3, True), (1, False), (3, False), (0, True)]):
        send(ssq_send, ssq_recv.at[n], ssq_ss, ssq_rs, at(dy=oy, flip=flip))
    later(ssq_recv, ssq_ss)

    loads[4].wait()
    loads[5].wait()

    def products(half):
        act = act_v[pl.ds(half * 2, 2)].reshape(256, WIDTH)
        return dot_t(act, wgu_v[...])

    gs_send[...] = products(1 - c).astype(BF16).reshape(NY, 64, 2 * FFD)
    send(gs_send, gs_recv, gs_ss, gs_rs, at(flip=True))
    later(gs_send, gs_ss)
    gs_own[...] = products(c).reshape(NY, 64, 2 * FFD)
    wait_bytes(gs_recv, gs_rs)
    for oy in FAR_Y:
        yy = (y + oy) % NY
        gy_send[oy - 1] = (gs_own[yy] + gs_recv[yy].astype(F32)).astype(BF16)
        send(gy_send.at[oy - 1], gy_recv.at[oy - 1], gy_ss, gy_rs, at(dy=oy))
    later(gy_send, gy_ss)
    both = gs_own[y] + gs_recv[y].astype(F32)
    wait_bytes(ssq_recv, ssq_rs)
    squares = ssq_send[...]
    for n in range(7):
        squares = squares + ssq_recv[n]
    row_id = lax.broadcasted_iota(I32, (64, 128), 0) + c * 256 + y * 64
    lane_id = lax.broadcasted_iota(I32, (64, 128), 1)
    mean = jnp.zeros((64, 1), F32)
    for n in range(NX):
        mean = mean + jnp.sum(
            jnp.where(row_id == lane_id + 128 * n, squares[n, 0:1, :], 0.0), axis=1, keepdims=True
        )
    scale = lax.rsqrt(mean / D + EPSILON)
    wait_bytes(gy_recv, gy_rs)
    for n in range(3):
        both = both + gy_recv[n].astype(F32)
    both = both * scale
    gate, up = both[:, :FFD], both[:, FFD:]
    hidden = (gate / (1.0 + jnp.exp(-gate)) * up).astype(BF16)

    hid[c, y] = hidden
    for oy in FAR_Y:
        send(hid.at[c, y], hid.at[c, y], hy_ss, hy_rs.at[oy - 1], at(dy=oy))
    send(hid.at[c, y], hid.at[c, y], hc_ss, hc_rs, at(flip=True))
    later(hid.at[0, pl.ds(0, 3)], hy_ss)
    later(hid.at[0], hc_ss)
    for oy in (1, 3, 2):
        yy = (y + NY - oy) % NY
        wait_bytes(hid.at[c, yy], hy_rs.at[oy - 1])
        send(hid.at[c, yy], hid.at[c, yy], hc_ss, hc_rs, at(flip=True))
    wait_bytes(hid.at[1 - c], hc_rs)

    loads[6].wait()
    lowered = reduce_scatter(
        lambda xx: hid[xx // 2, pl.ds((xx % 2) * 2, 2)].reshape(128, FFD), wd_v[...], lambda zz: zz,
        dx_send, dx_recv, dx_ss, dx_rs, dz_own, dz_send, dz_recv, dz_ss, dz_rs,
    )
    out_ref[...] = (stream_v[...].astype(F32) + lowered).astype(BF16)

    for end in ends:
        end()


def per_device(
    queries, new_latent, residual, pool, page_owner, page_slot, lengths, resumed,
    value_up, out_proj, norm_gain, gate_weight, up_weight, down_weight,
):
    vmem = pl.BlockSpec(memory_space=pltpu.VMEM)
    anywhere = pl.BlockSpec(memory_space=pl.ANY)
    dma, V = pltpu.SemaphoreType.DMA, pltpu.VMEM
    one = dma
    rs_scratch = [
        V((3, 128, WIDTH), BF16), V((3, 128, WIDTH), BF16), one, one,
        V((NZ, REQ_D, WIDTH), F32), V((NZ, REQ_D, WIDTH), BF16), V((7, REQ_D, WIDTH), BF16), one, one,
    ]
    scratch = [
        V((256, COLS), BF16), V((TOK, COLS, 128), BF16), V((128, TOK, COLS), BF16), V((HEADS, KL, VH), BF16),
        V((512, WIDTH), BF16), V((2 * FFD, WIDTH), BF16), V((FFD, WIDTH), BF16), dma((7,)),
        V((1, 1, 128), I32), V((32, 1, 128), I32), pltpu.SMEM((32, 1, 128), I32),
        V((1, 1, 256), I32), pltpu.SMEM((1, 1, 256), I32), V((REQ_D, 256), F32), dma((2,)), one, one,
        V((32, 16, COLS), BF16), V((32, 16, COLS), BF16), one, one,
        V((8, 256, COLS), BF16), one, dma((4,)), one, dma((4,)),
        V((256, COLS), BF16), V((8, 256, 256), F32),
        V((HEADS, 16, VH), BF16), V((16, 16, VH), BF16), one, one,
        V((NX, NC, 64, 512), BF16), one, dma((4,)), one, dma((4,)),
        *rs_scratch,
        V((REQ_D, WIDTH), BF16), V((NX, NZ, REQ_D, WIDTH), BF16), one, one, one, dma((3,)),
        V((NX, 128, WIDTH), BF16), V((NX, 8, 128), F32), V((7, NX, 8, 128), F32), one, one,
        V((NY, 64, 2 * FFD), F32), V((NY, 64, 2 * FFD), BF16), V((NY, 64, 2 * FFD), BF16), one, one,
        V((3, 64, 2 * FFD), BF16), V((3, 64, 2 * FFD), BF16), one, one,
        V((NC, NY, 64, FFD), BF16), one, dma((3,)), one, one,
        *rs_scratch,
    ]
    return pl.pallas_call(
        kernel,
        out_shape=jax.ShapeDtypeStruct((REQ_D, WIDTH), BF16),
        in_specs=[vmem] * 7 + [anywhere] * 7,
        out_specs=vmem,
        scratch_shapes=scratch,
        compiler_params=pltpu.CompilerParams(
            collective_id=0, has_side_effects=True, vmem_limit_bytes=56 * 1024 * 1024
        ),
        name="layer",
    )(
        page_owner.T, page_slot.T, lengths.reshape(1, REQ_D), resumed.reshape(1, REQ_D), new_latent, residual,
        norm_gain, queries.reshape(256, COLS), pool.transpose(1, 2, 0), value_up, out_proj,
        gate_weight.T, up_weight.T, down_weight,
    )


def solution(mesh):
    return jax.shard_map(
        per_device,
        mesh=mesh,
        in_specs=(
            P("dp", "tp", None), P("dp", None), P("dp", "tp"), P("dp", "tp", None), P("dp", None), P("dp", None),
            P("dp"), P("dp"), P("tp", None, None), P("dp", "tp"), P("tp"), P("tp", "dp"), P("tp", "dp"),
            P("dp", "tp"),
        ),
        out_specs=P("dp", "tp"),
        check_vma=False,
    )
```

```python
import functools

import jax
import jax.numpy as jnp
from jax import lax
from jax.experimental import pallas as pl
from jax.experimental.pallas import tpu as pltpu
from jax.sharding import PartitionSpec as P

MESH = pl.DeviceIdType.MESH
F32, BF16, I32 = jnp.float32, jnp.bfloat16, jnp.int32

NX, NY, NZ, NC = 4, 4, 8, 2
REQ_D = 16
HEADS = 16
COLS = 576
KL = 512
VH = 128
TOK = 8
PAGE = 64
PAGES = 4
USED = 32
WIDTH = 896
WA, WB = 512, 384
PARTS = ((0, 256), (256, 256), (512, 64))
FFD = 576
D = 7168
SCORE_SCALE = 192.0 ** (-0.5)
EPSILON = 1e-06

FAR_Z = (4, 3, 5, 2, 6, 1, 7)
FAR_X = (2, 1, 3)
FAR_Y = (2, 1, 3)
FAR_DP = sorted(
    ((dx, dz) for dx in range(NX) for dz in range(NZ) if dx or dz),
    key=lambda o: -(min(o[0], NX - o[0]) + min(o[1], NZ - o[1])),
)


def send(src, dst, send_sem, recv_sem, device):
    copy = pltpu.make_async_remote_copy(
        src_ref=src,
        dst_ref=dst,
        send_sem=send_sem,
        recv_sem=recv_sem,
        device_id=device,
        device_id_type=MESH,
    )
    copy.start()


def wait_bytes(ref, sem):
    pltpu.make_async_copy(ref, ref, sem).wait()


def column(row, n):
    rows = lax.broadcasted_iota(I32, (n, n), 0)
    lanes = lax.broadcasted_iota(I32, (n, n), 1)
    return jnp.sum(jnp.where(rows == lanes, row, 0), axis=1, keepdims=True)


def dot(a, b):
    return jnp.dot(a, b, preferred_element_type=F32)


def dot_t(a, b):
    return lax.dot_general(a, b, (((1,), (1,)), ((), ())), preferred_element_type=F32)


def kernel(
    owner_ref, slot_ref, len_ref, res_ref, nl_ref, resid_ref, gain_ref,
    q_hbm, pool_hbm, vup_hbm, wo_hbm, wg_hbm, wu_hbm, wd_hbm,
    out_ref,
    q_v, pool_t, pool_v, vup_v, wo_v, wgu_v, wd_v, load_sem,
    want_v, asked_v, asked_s, sel_v, sel_s, limit_v, smem_sem, req_ss, req_rs,
    pg_send, pg_recv, pg_ss, pg_rs,
    keys, key_ss, key_rs, sib_ss, sib_rs,
    qt_v, scores_v,
    hd_send, hd_in, hd_ss, hd_rs,
    hb, hb_ss, hb_rs, hs_ss, hs_rs,
    sums,
    gat_a, ga_ss, ga_rs, gax_ss, gax_rs, gat_b, gb_ss, gb_rs, gbz_ss, gbz_rs,
    act_v, ssq_send, ssq_recv, ssq_ss, ssq_rs,
    gs_own, gs_send, gs_recv, gs_ss, gs_rs,
    gy_send, gy_recv, gy_ss, gy_rs,
    hid, hy_ss, hy_rs, hc_ss, hc_rs,
):
    dp, tp = lax.axis_index("dp"), lax.axis_index("tp")
    x, z = dp // NZ, dp % NZ
    y, c = tp // NC, tp % NC

    def at(dx=0, dz=0, dy=0, flip=False):
        core = 1 - c if flip else c
        return (((x + dx) % NX) * NZ + (z + dz) % NZ, ((y + dy) % NY) * NC + core)

    loads = [
        pltpu.make_async_copy(src, dst, load_sem.at[i])
        for i, (src, dst) in enumerate(
            [(pool_hbm, pool_t), (q_hbm, q_v), (vup_hbm, vup_v), (wo_hbm, wo_v),
             (wg_hbm, wgu_v.at[pl.ds(0, FFD)]), (wu_hbm, wgu_v.at[pl.ds(FFD, FFD)]), (wd_hbm, wd_v)]
        )
    ]
    for load in loads:
        load.start()
    ends = []

    def later(ref, sem):
        ends.append(lambda: wait_bytes(ref, sem))


    barrier = pltpu.get_barrier_semaphore()
    for ox, oz in FAR_DP:
        pl.semaphore_signal(barrier, 1, device_id=at(ox, oz), device_id_type=MESH)
    for oy in FAR_Y:
        pl.semaphore_signal(barrier, 1, device_id=at(dy=oy), device_id_type=MESH)
    pl.semaphore_signal(barrier, 1, device_id=at(flip=True), device_id_type=MESH)
    in_tp = dp // 4
    to_self = jnp.where((tp == in_tp) & (z % 2 == c), 1, 0)

    def greet(k, carry):
        source = 2 * k + c

        @pl.when(jnp.logical_not((source == dp) & (in_tp == tp)))
        def _():
            pl.semaphore_signal(barrier, 1, device_id=(source, in_tp), device_id_type=MESH)

        return carry

    lax.fori_loop(0, 16, greet, 0)

    lengths = column(len_ref[...], REQ_D)
    resumed = column(res_ref[...], REQ_D)
    before = (
        lax.broadcasted_iota(I32, (REQ_D, REQ_D, 1), 1) < lax.broadcasted_iota(I32, (REQ_D, REQ_D, 1), 0)
    ).astype(I32)

    def earlier(v):
        return jnp.sum(before * v[None], axis=1)

    lane = lax.broadcasted_iota(I32, (REQ_D, 128), 1)
    lane_owner = lane % 32
    lane_copy = lane // 32
    page_lane = lax.broadcasted_iota(I32, (REQ_D, USED * TOK), 1) // TOK
    owner_base = jnp.zeros((1, 128), I32)
    read_base = jnp.zeros((1, 128), I32)
    wanted = jnp.zeros((1, 128), I32)
    limit = jnp.zeros((REQ_D, USED * TOK), I32)
    chosen = jnp.zeros((1, USED * TOK), I32)
    for p in range(PAGES):
        owner = column(owner_ref[p : p + 1, :], REQ_D)
        read = jnp.where((resumed == 1) & (lengths > p * PAGE), 1, 0)
        match = jnp.where(lane_owner == owner, read, 0)
        copy = owner_base + earlier(match)
        owner_base = owner_base + jnp.sum(match, axis=0, keepdims=True)
        wanted = wanted + jnp.sum(
            jnp.where((match > 0) & (copy == lane_copy), column(slot_ref[p : p + 1, :], REQ_D), 0),
            axis=0, keepdims=True,
        )
        own_copy = jnp.sum(jnp.where(lane < 32, match * copy, 0), axis=1, keepdims=True)
        read_lanes = jnp.broadcast_to(read, (REQ_D, 128))
        place = (read_base + earlier(read_lanes))[:, 0:1]
        read_base = read_base + jnp.sum(read_lanes, axis=0, keepdims=True)
        here = jnp.where(page_lane == place, read, 0)
        limit = limit + here * (lengths - p * PAGE)
        off_x = (x - owner // NZ + NX) % NX
        off_z = (z - owner % NZ + NZ) % NZ
        source = (off_x * NZ + off_z) * 2 + own_copy
        chosen = chosen + jnp.sum(here * source, axis=0, keepdims=True)
    limit_v[...] = limit.astype(F32)
    want_v[0] = wanted
    asked_v[0] = wanted
    sel_v[0] = chosen
    sel_copy = pltpu.make_async_copy(sel_v, sel_s, smem_sem.at[0])
    sel_copy.start()

    pl.semaphore_wait(barrier, 31 + 4 + 16 - to_self)

    for ox, oz in FAR_DP:
        send(want_v.at[0], asked_v.at[ox * NZ + oz], req_ss, req_rs, at(ox, oz))
    later(asked_v.at[pl.ds(1, 31)], req_ss)

    loads[1].wait()
    rows = lax.broadcasted_iota(I32, (256, 256), 0)
    lanes = lax.broadcasted_iota(I32, (256, 256), 1)
    swap = jnp.where(lanes == (rows % 16) * 16 + rows // 16, 1.0, 0.0).astype(BF16)
    qt = dot(swap, q_v[...]).astype(BF16)
    qt_v[...] = qt
    own_all = dot_t(qt, nl_ref[...]) * SCORE_SCALE
    own_diag = lax.broadcasted_iota(I32, (256, 16), 1) == lax.broadcasted_iota(I32, (256, 16), 0) % 16
    own_score = jnp.sum(jnp.where(own_diag, own_all, 0.0), axis=1, keepdims=True)
    loads[0].wait()
    token_row = lax.broadcasted_iota(I32, (1024, 128), 0)
    slot_lane = lax.broadcasted_iota(I32, (1024, 128), 1)
    pages = jnp.zeros((1024, COLS), F32)
    for j in range(TOK):
        spread = jnp.where(token_row == slot_lane * TOK + j, 1.0, 0.0).astype(BF16)
        pages = pages + dot_t(spread, pool_t[j])
    pool_v[...] = pages.astype(BF16).reshape(128, TOK, COLS)
    sel_copy.wait()

    wait_bytes(asked_v.at[pl.ds(1, 31)], req_rs)
    asked_copy = pltpu.make_async_copy(asked_v, asked_s, smem_sem.at[1])
    asked_copy.start()
    asked_copy.wait()

    def gather(n_in, buffer, n_out, first, width):
        pair = [
            pool_v[jnp.clip(asked_s[n_in, 0, 32 * k + dp], 0, 127), :, first : first + width] for k in range(2)
        ]
        buffer[n_out] = jnp.concatenate(pair, axis=0)

    for i, (first, width) in enumerate(PARTS):
        for ox, oz in FAR_DP:
            n_out = ox * NZ + oz
            gather(((NX - ox) % NX) * NZ + (NZ - oz) % NZ, pg_send[i], n_out, first, width)
            send(pg_send[i].at[n_out], pg_recv[i].at[n_out], pg_ss.at[i], pg_rs.at[i], at(ox, oz))
        later(pg_send[i].at[pl.ds(1, 31)], pg_ss.at[i])
    for i, (first, width) in enumerate(PARTS):
        gather(0, pg_recv[i], 0, first, width)

    for i in range(3):
        wait_bytes(pg_recv[i].at[pl.ds(1, 31)], pg_rs.at[i])

        def pick(u, carry):
            pair = []
            for k in range(2):
                source = jnp.clip(sel_s[0, 0, (2 * u + k) * TOK], 0, 63)
                both = pg_recv[i][lax.shift_right_logical(source, 1)]
                pair.append(jnp.where(jnp.bitwise_and(source, 1) == 1, both[TOK:], both[:TOK]))
            keys[i][0, pl.ds(pl.multiple_of(u * 16, 16), 16), :] = jnp.concatenate(pair, axis=0)
            return carry

        lax.fori_loop(0, USED // 2, pick, 0)
        for oy in FAR_Y:
            send(keys[i].at[0], keys[i].at[oy], key_ss.at[i], key_rs.at[i, oy], at(dy=oy))
        send(keys[i].at[0], keys[i].at[4], sib_ss.at[i], sib_rs.at[i, 0], at(flip=True))
        later(keys[i].at[pl.ds(0, 3)], key_ss.at[i])
        later(keys[i].at[pl.ds(0, 4)], sib_ss.at[i])

    limit = limit_v[...].reshape(1, REQ_D, USED * TOK)
    token = (lax.broadcasted_iota(I32, (1, 1, USED * TOK), 2) % TOK).astype(F32)

    def source_of(n):
        core = c if n < 4 else 1 - c
        return ((y + NY - n % 4) % NY) * NC + core

    def score_block(i, n):
        first, width = PARTS[i]
        block = dot_t(qt_v[:, first : first + width], keys[i][n])
        if i:
            block = scores_v[n] + block
        if i == 2:
            usable = limit > token + (source_of(n) * TOK).astype(F32)
            block = (block * SCORE_SCALE).reshape(HEADS, REQ_D, USED * TOK)
            block = jnp.where(usable, block, -jnp.inf).reshape(256, USED * TOK)
        scores_v[n] = block

    for i in range(3):
        for oy in (1, 3, 2):
            wait_bytes(keys[i].at[oy], key_rs.at[i, oy])
            send(keys[i].at[oy], keys[i].at[4 + oy], sib_ss.at[i], sib_rs.at[i, oy], at(flip=True))
        for n in range(4):
            score_block(i, n)
        for oy in (0, 1, 3, 2):
            wait_bytes(keys[i].at[4 + oy], sib_rs.at[i, oy])
            score_block(i, 4 + oy)

    peak = scores_v[0]
    for n in range(1, 8):
        peak = jnp.maximum(peak, scores_v[n])
    top = jnp.maximum(own_score, jnp.max(peak, axis=1, keepdims=True))
    own_weight = jnp.exp(own_score - top)
    weight_lanes = jnp.zeros((256, USED * TOK), F32)
    halves = [jnp.zeros((256, 256), F32)] * 2
    for n in range(8):
        weights = jnp.exp(scores_v[n] - top)
        weight_lanes = weight_lanes + weights
        weights = weights.astype(BF16)
        halves = [half + dot(weights, keys[i][n]) for i, half in enumerate(halves)]
    latent = jnp.concatenate(halves, axis=1)
    weight_sum = own_weight + jnp.sum(weight_lanes, axis=1, keepdims=True)
    own_latent = nl_ref[:, :KL].astype(F32).reshape(1, REQ_D, KL)
    latent = latent.reshape(HEADS, REQ_D, KL) + own_weight.reshape(HEADS, REQ_D, 1) * own_latent
    latent = (latent / weight_sum.reshape(HEADS, REQ_D, 1)).astype(BF16)

    loads[2].wait()
    for h in range(HEADS):
        hd_send[h] = dot(latent[h], vup_v[h]).astype(BF16)
        target = (4 * tp + h // 4, (h % 4) * NC + z % 2)
        is_me = (target[0] == dp) & (target[1] == tp)

        @pl.when(is_me)
        def _():
            pltpu.make_async_copy(hd_send.at[h], hd_in.at[dp // 2], hd_rs).start()

        @pl.when(jnp.logical_not(is_me))
        def _():
            send(hd_send.at[h], hd_in.at[dp // 2], hd_ss, hd_rs, target)

    def heads_left():
        wait_bytes(hd_in.at[pl.ds(0, 15)], hd_ss)

        @pl.when(to_self == 0)
        def _():
            wait_bytes(hd_in.at[0], hd_ss)

    ends.append(heads_left)

    wait_bytes(hd_in, hd_rs)
    own_cols = pl.ds(pl.multiple_of(y * VH, VH), VH)
    hb[:, pl.ds(c, 1), :, own_cols] = hd_in[...].reshape(NX, 1, 64, VH)
    own_block = hb.at[:, c, :, own_cols]
    for oy in FAR_Y:
        send(own_block, own_block, hb_ss, hb_rs.at[oy], at(dy=oy))
    send(own_block, own_block, hs_ss, hs_rs.at[0], at(flip=True))
    later(hb.at[:, pl.ds(0, 1), :, pl.ds(0, 3 * VH)], hb_ss)
    later(hb.at[:, 0], hs_ss)
    for oy in (1, 3, 2):
        cols = pl.ds(pl.multiple_of(((y + NY - oy) % NY) * VH, VH), VH)
        block = hb.at[:, c, :, cols]
        wait_bytes(block, hb_rs.at[oy])
        send(block, block, hs_ss, hs_rs.at[oy], at(flip=True))
    for oy in range(4):
        wait_bytes(own_block, hs_rs.at[oy])

    def sum_over_dp(rows_x, rows_all, weight, place, bufs, ready_a, ready_b):
        (a_send, a_recv, a_ss, a_rs, a_own, a_mid, am_recv, am_ss, am_rs,
         b_send, b_recv, b_ss, b_rs, b_own, b_mid, bm_recv, bm_ss, bm_rs) = bufs
        for ox in FAR_X:
            a_send[ox - 1] = dot(rows_x((x + ox) % NX), weight[:, :WA]).astype(BF16)
            send(a_send.at[ox - 1], a_recv.at[ox - 1], a_ss, a_rs, at(dx=ox))
        later(a_send, a_ss)
        b_send[...] = dot(rows_all(), weight[:, WA:]).astype(BF16).reshape(NX, NZ, REQ_D, WB)
        for oz in FAR_Z:
            send(b_send.at[:, place((z + oz) % NZ)], b_recv.at[oz - 1], b_ss, b_rs, at(dz=oz))
        later(b_recv, b_ss)
        total = dot(rows_x(x), weight[:, :WA])
        wait_bytes(a_recv, a_rs)
        for n in range(3):
            total = total + a_recv[n].astype(F32)
        total = total.reshape(NZ, REQ_D, WA)
        a_own[...] = total
        a_mid[...] = total.astype(BF16)
        for oz in FAR_Z:
            send(a_mid.at[place((z + oz) % NZ)], am_recv.at[oz - 1], am_ss, am_rs, at(dz=oz))
        later(am_recv, am_ss)
        total = b_send[:, place(z)].astype(F32)
        wait_bytes(b_recv, b_rs)
        for n in range(7):
            total = total + b_recv[n].astype(F32)
        b_own[...] = total
        b_mid[...] = total.astype(BF16)
        for ox in FAR_X:
            send(b_mid.at[(x + ox) % NX], bm_recv.at[ox - 1], bm_ss, bm_rs, at(dx=ox))
        later(bm_recv, bm_ss)
        mine = a_own[place(z)]
        wait_bytes(am_recv, am_rs)
        for n in range(7):
            mine = mine + am_recv[n].astype(F32)
        ready_a(mine)
        mine = b_own[x]
        wait_bytes(bm_recv, bm_rs)
        for n in range(3):
            mine = mine + bm_recv[n].astype(F32)
        ready_b(mine)

    def stream_a(attended):
        stream = (resid_ref[:, :WA].astype(F32) + attended).astype(BF16)
        gat_a[x, z] = stream
        for oz in FAR_Z:
            send(gat_a.at[x, z], gat_a.at[x, z], ga_ss, ga_rs, at(dz=oz))
        later(gat_a.at[0, pl.ds(0, 7)], ga_ss)

    def stream_b(attended):
        stream = (resid_ref[:, WA:].astype(F32) + attended).astype(BF16)
        gat_b[x, z] = stream
        for ox in FAR_X:
            send(gat_b.at[x, z], gat_b.at[x, z], gb_ss, gb_rs, at(dx=ox))
        later(gat_b.at[0, pl.ds(0, 3)], gb_ss)

    loads[3].wait()
    sum_over_dp(
        lambda xx: hb[xx].reshape(128, 512), lambda: hb[...].reshape(512, 512), wo_v,
        lambda zz: (zz % 2) * 4 + zz // 2, sums[0], stream_a, stream_b,
    )
    wait_bytes(gat_a.at[0, pl.ds(0, 7)], ga_rs)
    for ox in FAR_X:
        send(gat_a.at[x], gat_a.at[x], gax_ss, gax_rs.at[ox - 1], at(dx=ox))
    later(gat_a.at[pl.ds(0, 3)], gax_ss)
    wait_bytes(gat_b.at[0, pl.ds(0, 3)], gb_rs)
    for oz in FAR_Z:
        send(gat_b.at[:, z], gat_b.at[:, z], gbz_ss, gbz_rs, at(dz=oz))
    later(gat_b.at[:, pl.ds(0, 7)], gbz_ss)

    def widen(block, gain):
        block = block.astype(F32)
        square = block * block
        high = square.astype(BF16)
        low = (square - high.astype(F32)).astype(BF16)
        ones = jnp.ones((8, block.shape[1]), BF16)
        return (block * gain).astype(BF16), (dot_t(ones, high) + dot_t(ones, low))[0:1]

    gain = gain_ref[...].reshape(1, WIDTH)

    def widen_a(xx):
        act, squares = widen(gat_a[xx].reshape(128, WA), gain[:, :WA])
        act_v[pl.ds(xx * 2, 2), :, :WA] = act.reshape(2, 64, WA)
        ssq_send[xx] = squares

    widen_a(x)
    for ox in (1, 3, 2):
        xx = (x + NX - ox) % NX
        wait_bytes(gat_a.at[xx], gax_rs.at[ox - 1])
        widen_a(xx)
    wait_bytes(gat_b.at[:, pl.ds(0, 7)], gbz_rs)
    for xx in range(NX):
        act, squares = widen(gat_b[xx].reshape(128, WB), gain[:, WA:])
        act_v[2 * xx : 2 * xx + 2, :, WA:] = act.reshape(2, 64, WB)
        ssq_send[xx] = ssq_send[xx] + squares
    for n, (oy, flip) in enumerate([(2, True), (2, False), (1, True), (3, True), (1, False), (3, False), (0, True)]):
        send(ssq_send, ssq_recv.at[n], ssq_ss, ssq_rs, at(dy=oy, flip=flip))
    later(ssq_recv, ssq_ss)

    loads[4].wait()
    loads[5].wait()

    def products(half, pair):
        act = jnp.concatenate([act_v[half * 4 + (y + oy) % NY] for oy in pair], axis=0)
        return dot_t(act, wgu_v[...]).reshape(2, 64, 2 * FFD)

    def to_core(k, pair):
        gs_send[k] = products(1 - c, pair).astype(BF16)
        send(gs_send.at[k], gs_recv.at[k], gs_ss, gs_rs.at[k], at(flip=True))

    pairs = ((2, 1), (3, 0))
    to_core(0, pairs[0])
    gs_own[0] = products(c, pairs[0])
    to_core(1, pairs[1])
    later(gs_send, gs_ss)
    gs_own[1] = products(c, pairs[1])
    for k, pair in enumerate(pairs):
        wait_bytes(gs_recv.at[k], gs_rs.at[k])
        for n, oy in enumerate(pair):
            both = gs_own[k, n] + gs_recv[k, n].astype(F32)
            if oy:
                gy_send[oy - 1] = both.astype(BF16)
                send(gy_send.at[oy - 1], gy_recv.at[oy - 1], gy_ss, gy_rs, at(dy=oy))
    later(gy_send, gy_ss)
    wait_bytes(ssq_recv, ssq_rs)
    squares = ssq_send[...]
    for n in range(7):
        squares = squares + ssq_recv[n]
    row_id = lax.broadcasted_iota(I32, (64, 128), 0) + c * 256 + y * 64
    lane_id = lax.broadcasted_iota(I32, (64, 128), 1)
    mean = jnp.zeros((64, 1), F32)
    for n in range(NX):
        mean = mean + jnp.sum(
            jnp.where(row_id == lane_id + 128 * n, squares[n], 0.0), axis=1, keepdims=True
        )
    scale = lax.rsqrt(mean / D + EPSILON)
    wait_bytes(gy_recv, gy_rs)
    for n in range(3):
        both = both + gy_recv[n].astype(F32)
    both = both * scale
    gate, up = both[:, :FFD], both[:, FFD:]
    hidden = (gate / (1.0 + jnp.exp(-gate)) * up).astype(BF16)

    hid[c, y] = hidden
    for oy in FAR_Y:
        send(hid.at[c, y], hid.at[c, y], hy_ss, hy_rs.at[oy - 1], at(dy=oy))
    send(hid.at[c, y], hid.at[c, y], hc_ss, hc_rs, at(flip=True))
    later(hid.at[0, pl.ds(0, 3)], hy_ss)
    later(hid.at[0], hc_ss)
    for oy in (1, 3, 2):
        yy = (y + NY - oy) % NY
        wait_bytes(hid.at[c, yy], hy_rs.at[oy - 1])
        send(hid.at[c, yy], hid.at[c, yy], hc_ss, hc_rs, at(flip=True))
    wait_bytes(hid.at[1 - c], hc_rs)

    loads[6].wait()

    def out_a(lowered):
        out_ref[:, :WA] = (gat_a[x, z].astype(F32) + lowered).astype(BF16)

    def out_b(lowered):
        out_ref[:, WA:] = (gat_b[x, z].astype(F32) + lowered).astype(BF16)

    sum_over_dp(
        lambda xx: hid[xx // 2, pl.ds((xx % 2) * 2, 2)].reshape(128, FFD), lambda: hid[...].reshape(512, FFD), wd_v,
        lambda zz: zz, sums[1], out_a, out_b,
    )
    for end in ends:
        end()


def per_device(
    queries, new_latent, residual, pool, page_owner, page_slot, lengths, resumed,
    value_up, out_proj, norm_gain, gate_weight, up_weight, down_weight,
):
    vmem = pl.BlockSpec(memory_space=pltpu.VMEM)
    anywhere = pl.BlockSpec(memory_space=pl.ANY)
    dma, V = pltpu.SemaphoreType.DMA, pltpu.VMEM
    one = dma
    sum_scratch = [
        V((3, 128, WA), BF16), V((3, 128, WA), BF16), one, one,
        V((NZ, REQ_D, WA), F32), V((NZ, REQ_D, WA), BF16), V((7, REQ_D, WA), BF16), one, one,
        V((NX, NZ, REQ_D, WB), BF16), V((7, NX, REQ_D, WB), BF16), one, one,
        V((NX, REQ_D, WB), F32), V((NX, REQ_D, WB), BF16), V((3, REQ_D, WB), BF16), one, one,
    ]
    scratch = [
        V((256, COLS), BF16), V((TOK, COLS, 128), BF16), V((128, TOK, COLS), BF16), V((HEADS, KL, VH), BF16),
        V((512, WIDTH), BF16), V((2 * FFD, WIDTH), BF16), V((FFD, WIDTH), BF16), dma((7,)),
        V((1, 1, 128), I32), V((32, 1, 128), I32), pltpu.SMEM((32, 1, 128), I32),
        V((1, 1, 256), I32), pltpu.SMEM((1, 1, 256), I32), V((REQ_D, 256), F32), dma((2,)), one, one,
        [V((32, 16, w), BF16) for _, w in PARTS], [V((32, 16, w), BF16) for _, w in PARTS], dma((3,)), dma((3,)),
        [V((8, 256, w), BF16) for _, w in PARTS], dma((3,)), dma((3, 4)), dma((3,)), dma((3, 4)),
        V((256, COLS), BF16), V((8, 256, 256), F32),
        V((HEADS, 16, VH), BF16), V((16, 16, VH), BF16), one, one,
        V((NX, NC, 64, 512), BF16), one, dma((4,)), one, dma((4,)),
        [sum_scratch, sum_scratch],
        V((NX, NZ, REQ_D, WA), BF16), one, one, one, dma((3,)),
        V((NX, NZ, REQ_D, WB), BF16), one, one, one, one,
        V((8, 64, WIDTH), BF16), V((NX, 1, 128), F32), V((7, NX, 1, 128), F32), one, one,
        V((2, 2, 64, 2 * FFD), F32), V((2, 2, 64, 2 * FFD), BF16), V((2, 2, 64, 2 * FFD), BF16), one, dma((2,)),
        V((3, 64, 2 * FFD), BF16), V((3, 64, 2 * FFD), BF16), one, one,
        V((NC, NY, 64, FFD), BF16), one, dma((3,)), one, one,
    ]
    return pl.pallas_call(
        kernel,
        out_shape=jax.ShapeDtypeStruct((REQ_D, WIDTH), BF16),
        in_specs=[vmem] * 7 + [anywhere] * 7,
        out_specs=vmem,
        scratch_shapes=scratch,
        compiler_params=pltpu.CompilerParams(
            collective_id=0, has_side_effects=True, vmem_limit_bytes=56 * 1024 * 1024
        ),
        name="layer",
    )(
        page_owner.T, page_slot.T, lengths.reshape(1, REQ_D), resumed.reshape(1, REQ_D), new_latent, residual,
        norm_gain, queries.reshape(256, COLS), pool.transpose(1, 2, 0), value_up, out_proj,
        gate_weight.T, up_weight.T, down_weight,
    )


def solution(mesh):
    return jax.shard_map(
        per_device,
        mesh=mesh,
        in_specs=(
            P("dp", "tp", None), P("dp", None), P("dp", "tp"), P("dp", "tp", None), P("dp", None), P("dp", None),
            P("dp"), P("dp"), P("tp", None, None), P("dp", "tp"), P("tp"), P("tp", "dp"), P("tp", "dp"),
            P("dp", "tp"),
        ),
        out_specs=P("dp", "tp"),
        check_vma=False,
    )
```

```python
import functools

import jax
import jax.numpy as jnp
from jax import lax
from jax.experimental import pallas as pl
from jax.experimental.pallas import tpu as pltpu
from jax.sharding import PartitionSpec as P

MESH = pl.DeviceIdType.MESH
F32, BF16, I32 = jnp.float32, jnp.bfloat16, jnp.int32

NX, NY, NZ, NC = 4, 4, 8, 2
REQ_D = 16
HEADS = 16
COLS = 576
KL = 512
VH = 128
TOK = 8
PAGE = 64
PAGES = 4
USED = 32
WIDTH = 896
PARTS_A, FIRST_B = ((0, 384), (384, 256)), 640
WB = WIDTH - FIRST_B
PARTS = ((0, 256), (256, 256), (512, 64))
FFD = 576
D = 7168
SCORE_SCALE = 192.0 ** (-0.5)
EPSILON = 1e-06

FAR_Z = (4, 3, 5, 2, 6, 1, 7)
FAR_X = (2, 1, 3)
FAR_Y = (2, 1, 3)
FAR_DP = sorted(
    ((dx, dz) for dx in range(NX) for dz in range(NZ) if dx or dz),
    key=lambda o: -(min(o[0], NX - o[0]) + min(o[1], NZ - o[1])),
)


def send(src, dst, send_sem, recv_sem, device):
    copy = pltpu.make_async_remote_copy(
        src_ref=src,
        dst_ref=dst,
        send_sem=send_sem,
        recv_sem=recv_sem,
        device_id=device,
        device_id_type=MESH,
    )
    copy.start()


def wait_bytes(ref, sem):
    pltpu.make_async_copy(ref, ref, sem).wait()


def column(row, n):
    rows = lax.broadcasted_iota(I32, (n, n), 0)
    lanes = lax.broadcasted_iota(I32, (n, n), 1)
    return jnp.sum(jnp.where(rows == lanes, row, 0), axis=1, keepdims=True)


def dot(a, b):
    return jnp.dot(a, b, preferred_element_type=F32)


def dot_t(a, b):
    return lax.dot_general(a, b, (((1,), (1,)), ((), ())), preferred_element_type=F32)


def kernel(
    owner_ref, slot_ref, len_ref, res_ref, nl_ref, resid_ref, gain_ref,
    q_hbm, pool_hbm, vup_hbm, wo_hbm, wg_hbm, wu_hbm, wd_hbm,
    out_ref,
    q_v, pool_t, pool_v, vup_v, wo_v, wgu_v, wt_v, wd_v, load_sem,
    want_v, asked_v, asked_s, sel_v, sel_s, limit_v, smem_sem, req_ss, req_rs,
    pg_send, pg_recv, pg_ss, pg_rs,
    keys, key_ss, key_rs, sib_ss, sib_rs,
    qt_v, scores_v,
    hd_send, hd_in, hd_ss, hd_rs,
    hb, hb_ss, hb_rs, hs_ss, hs_rs,
    sums,
    gat_a, gat_b, gbz_ss, gbz_rs, resid_b, rb_ss, rb_rs,
    act_v, ssq_send, ssq_recv, ssq_ss, ssq_rs,
    gs_own, gs_send, gs_recv, gs_ss, gs_rs,
    gy_send, gy_recv, gy_ss, gy_rs,
    hid, hy_ss, hy_rs, hc_ss, hc_rs,
):
    dp, tp = lax.axis_index("dp"), lax.axis_index("tp")
    x, z = dp // NZ, dp % NZ
    y, c = tp // NC, tp % NC

    def at(dx=0, dz=0, dy=0, flip=False):
        core = 1 - c if flip else c
        return (((x + dx) % NX) * NZ + (z + dz) % NZ, ((y + dy) % NY) * NC + core)

    loads = [
        pltpu.make_async_copy(src, dst, load_sem.at[i])
        for i, (src, dst) in enumerate(
            [(pool_hbm, pool_t), (q_hbm, q_v), (vup_hbm, vup_v), (wo_hbm, wo_v),
             (wg_hbm, wgu_v.at[pl.ds(0, FFD)]), (wu_hbm, wgu_v.at[pl.ds(FFD, FFD)]), (wd_hbm, wd_v)]
        )
    ]
    for load in loads:
        load.start()
    ends = []

    def later(ref, sem):
        ends.append(lambda: wait_bytes(ref, sem))


    barrier = pltpu.get_barrier_semaphore()
    for ox, oz in FAR_DP:
        pl.semaphore_signal(barrier, 1, device_id=at(ox, oz), device_id_type=MESH)
    for oy in FAR_Y:
        pl.semaphore_signal(barrier, 1, device_id=at(dy=oy), device_id_type=MESH)
    pl.semaphore_signal(barrier, 1, device_id=at(flip=True), device_id_type=MESH)
    in_tp = dp // 4
    to_self = jnp.where((tp == in_tp) & (z % 2 == c), 1, 0)

    def greet(k, carry):
        source = 2 * k + c

        @pl.when(jnp.logical_not((source == dp) & (in_tp == tp)))
        def _():
            pl.semaphore_signal(barrier, 1, device_id=(source, in_tp), device_id_type=MESH)

        return carry

    lax.fori_loop(0, 16, greet, 0)

    lengths = column(len_ref[...], REQ_D)
    resumed = column(res_ref[...], REQ_D)
    before = (
        lax.broadcasted_iota(I32, (REQ_D, REQ_D, 1), 1) < lax.broadcasted_iota(I32, (REQ_D, REQ_D, 1), 0)
    ).astype(I32)

    def earlier(v):
        return jnp.sum(before * v[None], axis=1)

    lane = lax.broadcasted_iota(I32, (REQ_D, 128), 1)
    lane_owner = lane % 32
    lane_copy = lane // 32
    page_lane = lax.broadcasted_iota(I32, (REQ_D, USED * TOK), 1) // TOK
    owner_base = jnp.zeros((1, 128), I32)
    read_base = jnp.zeros((1, 128), I32)
    wanted = jnp.zeros((1, 128), I32)
    limit = jnp.zeros((REQ_D, USED * TOK), I32)
    chosen = jnp.zeros((1, USED * TOK), I32)
    for p in range(PAGES):
        owner = column(owner_ref[p : p + 1, :], REQ_D)
        read = jnp.where((resumed == 1) & (lengths > p * PAGE), 1, 0)
        match = jnp.where(lane_owner == owner, read, 0)
        copy = owner_base + earlier(match)
        owner_base = owner_base + jnp.sum(match, axis=0, keepdims=True)
        wanted = wanted + jnp.sum(
            jnp.where((match > 0) & (copy == lane_copy), column(slot_ref[p : p + 1, :], REQ_D), 0),
            axis=0, keepdims=True,
        )
        own_copy = jnp.sum(jnp.where(lane < 32, match * copy, 0), axis=1, keepdims=True)
        read_lanes = jnp.broadcast_to(read, (REQ_D, 128))
        place = (read_base + earlier(read_lanes))[:, 0:1]
        read_base = read_base + jnp.sum(read_lanes, axis=0, keepdims=True)
        here = jnp.where(page_lane == place, read, 0)
        limit = limit + here * (lengths - p * PAGE)
        off_x = (x - owner // NZ + NX) % NX
        off_z = (z - owner % NZ + NZ) % NZ
        source = (off_x * NZ + off_z) * 2 + own_copy
        chosen = chosen + jnp.sum(here * source, axis=0, keepdims=True)
    limit_v[...] = limit.astype(F32)
    want_v[0] = wanted
    asked_v[0] = wanted
    sel_v[0] = chosen
    sel_copy = pltpu.make_async_copy(sel_v, sel_s, smem_sem.at[0])
    sel_copy.start()

    pl.semaphore_wait(barrier, 31 + 4 + 16 - to_self)

    for ox, oz in FAR_DP:
        send(want_v.at[0], asked_v.at[ox * NZ + oz], req_ss, req_rs, at(ox, oz))
    later(asked_v.at[pl.ds(1, 31)], req_ss)

    resid_b[pl.ds(x, 1)] = resid_ref[:, FIRST_B:].reshape(1, REQ_D, WB)
    for ox in FAR_X:
        send(resid_b.at[x], resid_b.at[x], rb_ss, rb_rs, at(dx=ox))
    later(resid_b.at[pl.ds(0, 3)], rb_ss)

    loads[1].wait()
    rows = lax.broadcasted_iota(I32, (256, 256), 0)
    lanes = lax.broadcasted_iota(I32, (256, 256), 1)
    swap = jnp.where(lanes == (rows % 16) * 16 + rows // 16, 1.0, 0.0).astype(BF16)
    qt = dot(swap, q_v[...]).astype(BF16)
    qt_v[...] = qt
    own_all = dot_t(qt, nl_ref[...]) * SCORE_SCALE
    own_diag = lax.broadcasted_iota(I32, (256, 16), 1) == lax.broadcasted_iota(I32, (256, 16), 0) % 16
    own_score = jnp.sum(jnp.where(own_diag, own_all, 0.0), axis=1, keepdims=True)
    loads[0].wait()
    token_row = lax.broadcasted_iota(I32, (1024, 128), 0)
    slot_lane = lax.broadcasted_iota(I32, (1024, 128), 1)
    pages = jnp.zeros((1024, COLS), F32)
    for j in range(TOK):
        spread = jnp.where(token_row == slot_lane * TOK + j, 1.0, 0.0).astype(BF16)
        pages = pages + dot_t(spread, pool_t[j])
    pool_v[...] = pages.astype(BF16).reshape(128, TOK, COLS)
    sel_copy.wait()

    wait_bytes(asked_v.at[pl.ds(1, 31)], req_rs)
    asked_copy = pltpu.make_async_copy(asked_v, asked_s, smem_sem.at[1])
    asked_copy.start()
    asked_copy.wait()

    def gather(n_in, buffer, n_out, first, width):
        pair = [
            pool_v[jnp.clip(asked_s[n_in, 0, 32 * k + dp], 0, 127), :, first : first + width] for k in range(2)
        ]
        buffer[n_out] = jnp.concatenate(pair, axis=0)

    for i, (first, width) in enumerate(PARTS):
        for ox, oz in FAR_DP:
            n_out = ox * NZ + oz
            gather(((NX - ox) % NX) * NZ + (NZ - oz) % NZ, pg_send[i], n_out, first, width)
            send(pg_send[i].at[n_out], pg_recv[i].at[n_out], pg_ss.at[i], pg_rs.at[i], at(ox, oz))
        later(pg_send[i].at[pl.ds(1, 31)], pg_ss.at[i])
    for i, (first, width) in enumerate(PARTS):
        gather(0, pg_recv[i], 0, first, width)

    loads[4].wait()
    loads[5].wait()
    same = lax.broadcasted_iota(I32, (128, 128), 0) == lax.broadcasted_iota(I32, (128, 128), 1)
    same = jnp.where(same, 1.0, 0.0).astype(BF16)
    for first in range(0, WIDTH, 128):
        wt_v[first : first + 128] = dot_t(same, wgu_v[:, first : first + 128]).astype(BF16)

    def pass_on(i):
        upper, lower = pl.ds(0, 128), pl.ds(128, 128)
        wait_bytes(keys[i].at[1], key_rs.at[i, 1])
        send(keys[i].at[1, upper], keys[i].at[2, upper], key_ss.at[i], key_rs.at[i, 2], at(dy=1))
        send(keys[i].at[1], keys[i].at[5], sib_ss.at[i], sib_rs.at[i, 1], at(flip=True))
        wait_bytes(keys[i].at[3], key_rs.at[i, 3])
        send(keys[i].at[3, lower], keys[i].at[2, lower], key_ss.at[i], key_rs.at[i, 0], at(dy=3))
        send(keys[i].at[3], keys[i].at[7], sib_ss.at[i], sib_rs.at[i, 3], at(flip=True))

    for i in range(len(PARTS)):
        wait_bytes(pg_recv[i].at[pl.ds(1, 31)], pg_rs.at[i])

        def pick(u, carry):
            pair = []
            for k in range(2):
                source = jnp.clip(sel_s[0, 0, (2 * u + k) * TOK], 0, 63)
                both = pg_recv[i][lax.shift_right_logical(source, 1)]
                pair.append(jnp.where(jnp.bitwise_and(source, 1) == 1, both[TOK:], both[:TOK]))
            keys[i][0, pl.ds(pl.multiple_of(u * 16, 16), 16), :] = jnp.concatenate(pair, axis=0)
            return carry

        lax.fori_loop(0, USED // 2, pick, 0)
        for oy in FAR_Y if i == len(PARTS) - 1 else (1, 3):
            send(keys[i].at[0], keys[i].at[oy], key_ss.at[i], key_rs.at[i, oy], at(dy=oy))
        send(keys[i].at[0], keys[i].at[4], sib_ss.at[i], sib_rs.at[i, 0], at(flip=True))
        later(keys[i].at[pl.ds(0, 3)], key_ss.at[i])
        later(keys[i].at[pl.ds(0, 4)], sib_ss.at[i])
        if i:
            pass_on(i - 1)

    limit = limit_v[...].reshape(1, REQ_D, USED * TOK)
    token = (lax.broadcasted_iota(I32, (1, 1, USED * TOK), 2) % TOK).astype(F32)

    def source_of(n):
        core = c if n < 4 else 1 - c
        return ((y + NY - n % 4) % NY) * NC + core

    def score_block(i, n):
        first, width = PARTS[i]
        block = dot_t(qt_v[:, first : first + width], keys[i][n])
        if i:
            block = scores_v[n] + block
        if i == len(PARTS) - 1:
            usable = limit > token + (source_of(n) * TOK).astype(F32)
            block = (block * SCORE_SCALE).reshape(HEADS, REQ_D, USED * TOK)
            block = jnp.where(usable, block, -jnp.inf).reshape(256, USED * TOK)
        scores_v[n] = block

    for i in range(len(PARTS)):
        if i < len(PARTS) - 1:
            wait_bytes(keys[i].at[2, pl.ds(0, 128)], key_rs.at[i, 2])
            wait_bytes(keys[i].at[2, pl.ds(128, 128)], key_rs.at[i, 0])
            send(keys[i].at[2], keys[i].at[6], sib_ss.at[i], sib_rs.at[i, 2], at(flip=True))
        else:
            for oy in (1, 3, 2):
                wait_bytes(keys[i].at[oy], key_rs.at[i, oy])
                send(keys[i].at[oy], keys[i].at[4 + oy], sib_ss.at[i], sib_rs.at[i, oy], at(flip=True))
        for n in range(4):
            score_block(i, n)
        for oy in (0, 1, 3, 2):
            wait_bytes(keys[i].at[4 + oy], sib_rs.at[i, oy])
            score_block(i, 4 + oy)

    peak = scores_v[0]
    for n in range(1, 8):
        peak = jnp.maximum(peak, scores_v[n])
    top = jnp.maximum(own_score, jnp.max(peak, axis=1, keepdims=True))
    own_weight = jnp.exp(own_score - top)
    weight_lanes = jnp.zeros((256, USED * TOK), F32)
    pieces = [jnp.zeros((256, width), F32) for _, width in PARTS[:-1]]
    for n in range(8):
        weights = jnp.exp(scores_v[n] - top)
        weight_lanes = weight_lanes + weights
        weights = weights.astype(BF16)
        pieces = [piece + dot(weights, keys[i][n]) for i, piece in enumerate(pieces)]
    latent = jnp.concatenate(pieces, axis=1)
    weight_sum = own_weight + jnp.sum(weight_lanes, axis=1, keepdims=True)
    own_latent = nl_ref[:, :KL].astype(F32).reshape(1, REQ_D, KL)
    latent = latent.reshape(HEADS, REQ_D, KL) + own_weight.reshape(HEADS, REQ_D, 1) * own_latent
    latent = (latent / weight_sum.reshape(HEADS, REQ_D, 1)).astype(BF16)

    loads[2].wait()
    for h in range(HEADS):
        hd_send[h] = dot(latent[h], vup_v[h]).astype(BF16)
        target = (4 * tp + h // 4, (h % 4) * NC + z % 2)
        is_me = (target[0] == dp) & (target[1] == tp)

        @pl.when(is_me)
        def _():
            pltpu.make_async_copy(hd_send.at[h], hd_in.at[dp // 2], hd_rs).start()

        @pl.when(jnp.logical_not(is_me))
        def _():
            send(hd_send.at[h], hd_in.at[dp // 2], hd_ss, hd_rs, target)

    def heads_left():
        wait_bytes(hd_in.at[pl.ds(0, 15)], hd_ss)

        @pl.when(to_self == 0)
        def _():
            wait_bytes(hd_in.at[0], hd_ss)

    ends.append(heads_left)

    wait_bytes(hd_in, hd_rs)
    own_cols = pl.ds(pl.multiple_of(y * VH, VH), VH)
    hb[:, pl.ds(c, 1), :, own_cols] = hd_in[...].reshape(NX, 1, 64, VH)
    own_block = hb.at[:, c, :, own_cols]
    for oy in FAR_Y:
        send(own_block, own_block, hb_ss, hb_rs.at[oy], at(dy=oy))
    send(own_block, own_block, hs_ss, hs_rs.at[0], at(flip=True))
    later(hb.at[:, pl.ds(0, 1), :, pl.ds(0, 3 * VH)], hb_ss)
    later(hb.at[:, 0], hs_ss)
    for oy in (1, 3, 2):
        cols = pl.ds(pl.multiple_of(((y + NY - oy) % NY) * VH, VH), VH)
        block = hb.at[:, c, :, cols]
        wait_bytes(block, hb_rs.at[oy])
        send(block, block, hs_ss, hs_rs.at[oy], at(flip=True))
    for oy in range(4):
        wait_bytes(own_block, hs_rs.at[oy])

    def sum_over_dp(rows_x, rows_all, weight, place, bufs, ready_a, gather_b, ready_b):
        parts_a, (b_send, b_recv, b_ss, b_rs, b_own, b_mid, bm_recv, bm_ss, bm_rs) = bufs
        for (first, width), (a_send, a_recv, a_ss, a_rs, *_) in zip(PARTS_A, parts_a):
            for ox in FAR_X:
                a_send[ox - 1] = dot(rows_x((x + ox) % NX), weight[:, first : first + width]).astype(BF16)
                send(a_send.at[ox - 1], a_recv.at[ox - 1], a_ss, a_rs, at(dx=ox))
            later(a_send, a_ss)
        b_send[...] = dot(rows_all(), weight[:, FIRST_B:]).astype(BF16).reshape(NX, NZ, REQ_D, WB)
        for oz in FAR_Z:
            send(b_send.at[:, place((z + oz) % NZ)], b_recv.at[oz - 1], b_ss, b_rs, at(dz=oz))
        later(b_recv, b_ss)
        own = dot(rows_x(x), weight[:, :FIRST_B])
        for (first, width), (a_send, a_recv, a_ss, a_rs, a_own, a_mid, am_recv, am_ss, am_rs) in zip(PARTS_A, parts_a):
            total = own[:, first : first + width]
            wait_bytes(a_recv, a_rs)
            for n in range(3):
                total = total + a_recv[n].astype(F32)
            total = total.reshape(NZ, REQ_D, width)
            a_own[...] = total
            a_mid[...] = total.astype(BF16)
            for oz in FAR_Z:
                send(a_mid.at[place((z + oz) % NZ)], am_recv.at[oz - 1], am_ss, am_rs, at(dz=oz))
            later(am_recv, am_ss)
        total = b_send[:, place(z)].astype(F32)
        wait_bytes(b_recv, b_rs)
        for n in range(7):
            total = total + b_recv[n].astype(F32)
        if gather_b:
            bm_recv[x] = total.astype(BF16)
            for ox in FAR_X:
                send(bm_recv.at[x], bm_recv.at[x], bm_ss, bm_rs, at(dx=ox))
            later(bm_recv.at[pl.ds(0, 3)], bm_ss)
        else:
            b_own[...] = total
            b_mid[...] = total.astype(BF16)
            for ox in FAR_X:
                send(b_mid.at[(x + ox) % NX], bm_recv.at[ox - 1], bm_ss, bm_rs, at(dx=ox))
            later(bm_recv, bm_ss)
        for part, (_, _, _, _, a_own, _, am_recv, _, am_rs) in enumerate(parts_a):
            mine = a_own[place(z)]
            wait_bytes(am_recv, am_rs)
            for n in range(7):
                mine = mine + am_recv[n].astype(F32)
            ready_a(part, mine)
        if gather_b:
            wait_bytes(bm_recv.at[pl.ds(0, 3)], bm_rs)
            mine = bm_recv[0].astype(F32)
            for n in range(1, NX):
                mine = mine + bm_recv[n].astype(F32)
        else:
            mine = b_own[x]
            wait_bytes(bm_recv, bm_rs)
            for n in range(3):
                mine = mine + bm_recv[n].astype(F32)
        ready_b(mine)

    def stream_a(part, attended):
        first, width = PARTS_A[part]
        gat, z_ss, z_rs, _, _ = gat_a[part]
        gat[x, z] = (resid_ref[:, first : first + width].astype(F32) + attended).astype(BF16)
        for oz in FAR_Z:
            send(gat.at[x, z], gat.at[x, z], z_ss, z_rs, at(dz=oz))
        later(gat.at[0, pl.ds(0, 7)], z_ss)

    def stream_b(attended):
        wait_bytes(resid_b.at[pl.ds(0, 3)], rb_rs)
        gat_b[:, z] = (resid_b[...].astype(F32) + attended).astype(BF16)
        for oz in FAR_Z:
            send(gat_b.at[:, z], gat_b.at[:, z], gbz_ss, gbz_rs, at(dz=oz))
        later(gat_b.at[:, pl.ds(0, 7)], gbz_ss)

    loads[3].wait()
    sum_over_dp(
        lambda xx: hb[xx].reshape(128, 512), lambda: hb[...].reshape(512, 512), wo_v,
        lambda zz: (zz % 2) * 4 + zz // 2, sums[0], stream_a, True, stream_b,
    )
    for gat, _, z_rs, x_ss, x_rs in gat_a:
        wait_bytes(gat.at[0, pl.ds(0, 7)], z_rs)
        for ox in FAR_X:
            send(gat.at[x], gat.at[x], x_ss, x_rs.at[ox - 1], at(dx=ox))
        later(gat.at[pl.ds(0, 3)], x_ss)

    def widen(block, gain):
        block = block.astype(F32)
        square = block * block
        high = square.astype(BF16)
        low = (square - high.astype(F32)).astype(BF16)
        ones = jnp.ones((8, block.shape[1]), BF16)
        return (block * gain).astype(BF16), (dot_t(ones, high) + dot_t(ones, low))[0:1]

    gain = gain_ref[...].reshape(1, WIDTH)

    for part, ((first, width), (gat, _, _, _, x_rs)) in enumerate(zip(PARTS_A, gat_a)):
        for ox in (0, 1, 3, 2):
            xx = (x + NX - ox) % NX
            if ox:
                wait_bytes(gat.at[xx], x_rs.at[ox - 1])
            act, squares = widen(gat[xx].reshape(128, width), gain[:, first : first + width])
            act_v[pl.ds(xx * 2, 2), :, first : first + width] = act.reshape(2, 64, width)
            ssq_send[xx] = ssq_send[xx] + squares if part else squares
    wait_bytes(gat_b.at[:, pl.ds(0, 7)], gbz_rs)
    for xx in range(NX):
        act, squares = widen(gat_b[xx].reshape(128, WB), gain[:, FIRST_B:])
        act_v[2 * xx : 2 * xx + 2, :, FIRST_B:] = act.reshape(2, 64, WB)
        ssq_send[xx] = ssq_send[xx] + squares
    for n, (oy, flip) in enumerate([(2, True), (2, False), (1, True), (3, True), (1, False), (3, False), (0, True)]):
        send(ssq_send, ssq_recv.at[n], ssq_ss, ssq_rs, at(dy=oy, flip=flip))
    later(ssq_recv, ssq_ss)

    def products(half, pair):
        act = jnp.concatenate([act_v[half * 4 + (y + oy) % NY] for oy in pair], axis=0)
        return dot(act, wt_v[...]).reshape(2, 64, 2 * FFD)

    def to_core(k, pair):
        gs_send[k] = products(1 - c, pair).astype(BF16)
        send(gs_send.at[k], gs_recv.at[k], gs_ss, gs_rs.at[k], at(flip=True))

    pairs = ((2, 1), (3, 0))
    to_core(0, pairs[0])
    gs_own[0] = products(c, pairs[0])
    to_core(1, pairs[1])
    later(gs_send, gs_ss)
    gs_own[1] = products(c, pairs[1])
    for k, pair in enumerate(pairs):
        wait_bytes(gs_recv.at[k], gs_rs.at[k])
        for n, oy in enumerate(pair):
            both = gs_own[k, n] + gs_recv[k, n].astype(F32)
            if oy:
                gy_send[oy - 1] = both.astype(BF16)
                send(gy_send.at[oy - 1], gy_recv.at[oy - 1], gy_ss, gy_rs, at(dy=oy))
    later(gy_send, gy_ss)
    wait_bytes(ssq_recv, ssq_rs)
    squares = ssq_send[...]
    for n in range(7):
        squares = squares + ssq_recv[n]
    row_id = lax.broadcasted_iota(I32, (64, 128), 0) + c * 256 + y * 64
    lane_id = lax.broadcasted_iota(I32, (64, 128), 1)
    mean = jnp.zeros((64, 1), F32)
    for n in range(NX):
        mean = mean + jnp.sum(
            jnp.where(row_id == lane_id + 128 * n, squares[n], 0.0), axis=1, keepdims=True
        )
    scale = lax.rsqrt(mean / D + EPSILON)
    wait_bytes(gy_recv, gy_rs)
    for n in range(3):
        both = both + gy_recv[n].astype(F32)
    both = both * scale
    gate, up = both[:, :FFD], both[:, FFD:]
    hidden = (gate / (1.0 + jnp.exp(-gate)) * up).astype(BF16)

    hid[c, y] = hidden
    for oy in FAR_Y:
        send(hid.at[c, y], hid.at[c, y], hy_ss, hy_rs.at[oy - 1], at(dy=oy))
    send(hid.at[c, y], hid.at[c, y], hc_ss, hc_rs, at(flip=True))
    later(hid.at[0, pl.ds(0, 3)], hy_ss)
    later(hid.at[0], hc_ss)
    for oy in (1, 3, 2):
        yy = (y + NY - oy) % NY
        wait_bytes(hid.at[c, yy], hy_rs.at[oy - 1])
        send(hid.at[c, yy], hid.at[c, yy], hc_ss, hc_rs, at(flip=True))
    wait_bytes(hid.at[1 - c], hc_rs)

    loads[6].wait()

    def out_a(part, lowered):
        first, width = PARTS_A[part]
        out_ref[:, first : first + width] = (gat_a[part][0][x, z].astype(F32) + lowered).astype(BF16)

    def out_b(lowered):
        out_ref[:, FIRST_B:] = (gat_b[x, z].astype(F32) + lowered).astype(BF16)

    sum_over_dp(
        lambda xx: hid[xx // 2, pl.ds((xx % 2) * 2, 2)].reshape(128, FFD), lambda: hid[...].reshape(512, FFD), wd_v,
        lambda zz: zz, sums[1], out_a, False, out_b,
    )
    for end in ends:
        end()


def per_device(
    queries, new_latent, residual, pool, page_owner, page_slot, lengths, resumed,
    value_up, out_proj, norm_gain, gate_weight, up_weight, down_weight,
):
    vmem = pl.BlockSpec(memory_space=pltpu.VMEM)
    anywhere = pl.BlockSpec(memory_space=pl.ANY)
    dma, V = pltpu.SemaphoreType.DMA, pltpu.VMEM
    one, n = dma, len(PARTS)
    def sum_scratch(gather_b):
        return [
            [
                [V((3, 128, w), BF16), V((3, 128, w), BF16), one, one,
                 V((NZ, REQ_D, w), F32), V((NZ, REQ_D, w), BF16), V((7, REQ_D, w), BF16), one, one]
                for _, w in PARTS_A
            ],
            [V((NX, NZ, REQ_D, WB), BF16), V((7, NX, REQ_D, WB), BF16), one, one,
             V((NX, REQ_D, WB), F32), V((NX, REQ_D, WB), BF16),
             V((NX, NX, REQ_D, WB) if gather_b else (3, REQ_D, WB), BF16), one, one],
        ]

    scratch = [
        V((256, COLS), BF16), V((TOK, COLS, 128), BF16), V((128, TOK, COLS), BF16), V((HEADS, KL, VH), BF16),
        V((512, WIDTH), BF16), V((2 * FFD, WIDTH), BF16), V((WIDTH, 2 * FFD), BF16), V((FFD, WIDTH), BF16), dma((7,)),
        V((1, 1, 128), I32), V((32, 1, 128), I32), pltpu.SMEM((32, 1, 128), I32),
        V((1, 1, 256), I32), pltpu.SMEM((1, 1, 256), I32), V((REQ_D, 256), F32), dma((2,)), one, one,
        [V((32, 16, w), BF16) for _, w in PARTS], [V((32, 16, w), BF16) for _, w in PARTS], dma((n,)), dma((n,)),
        [V((8, 256, w), BF16) for _, w in PARTS], dma((n,)), dma((n, 4)), dma((n,)), dma((n, 4)),
        V((256, COLS), BF16), V((8, 256, 256), F32),
        V((HEADS, 16, VH), BF16), V((16, 16, VH), BF16), one, one,
        V((NX, NC, 64, 512), BF16), one, dma((4,)), one, dma((4,)),
        [sum_scratch(True), sum_scratch(False)],
        [[V((NX, NZ, REQ_D, w), BF16), one, one, one, dma((3,))] for _, w in PARTS_A],
        V((NX, NZ, REQ_D, WB), BF16), one, one, V((NX, REQ_D, WB), BF16), one, one,
        V((8, 64, WIDTH), BF16), V((NX, 1, 128), F32), V((7, NX, 1, 128), F32), one, one,
        V((2, 2, 64, 2 * FFD), F32), V((2, 2, 64, 2 * FFD), BF16), V((2, 2, 64, 2 * FFD), BF16), one, dma((2,)),
        V((3, 64, 2 * FFD), BF16), V((3, 64, 2 * FFD), BF16), one, one,
        V((NC, NY, 64, FFD), BF16), one, dma((3,)), one, one,
    ]
    return pl.pallas_call(
        kernel,
        out_shape=jax.ShapeDtypeStruct((REQ_D, WIDTH), BF16),
        in_specs=[vmem] * 7 + [anywhere] * 7,
        out_specs=vmem,
        scratch_shapes=scratch,
        compiler_params=pltpu.CompilerParams(
            collective_id=0, has_side_effects=True, vmem_limit_bytes=56 * 1024 * 1024
        ),
        name="layer",
    )(
        page_owner.T, page_slot.T, lengths.reshape(1, REQ_D), resumed.reshape(1, REQ_D), new_latent, residual,
        norm_gain, queries.reshape(256, COLS), pool.transpose(1, 2, 0), value_up, out_proj,
        gate_weight.T, up_weight.T, down_weight,
    )


def solution(mesh):
    return jax.shard_map(
        per_device,
        mesh=mesh,
        in_specs=(
            P("dp", "tp", None), P("dp", None), P("dp", "tp"), P("dp", "tp", None), P("dp", None), P("dp", None),
            P("dp"), P("dp"), P("tp", None, None), P("dp", "tp"), P("tp"), P("tp", "dp"), P("tp", "dp"),
            P("dp", "tp"),
        ),
        out_specs=P("dp", "tp"),
        check_vma=False,
    )
```

```python
import functools

import jax
import jax.numpy as jnp
from jax import lax
from jax.experimental import pallas as pl
from jax.experimental.pallas import tpu as pltpu
from jax.sharding import PartitionSpec as P

MESH = pl.DeviceIdType.MESH
F32, BF16, I32 = jnp.float32, jnp.bfloat16, jnp.int32

NX, NY, NZ, NC = 4, 4, 8, 2
REQ_D = 16
HEADS = 16
COLS = 576
KL = 512
VH = 128
TOK = 8
PAGE = 64
PAGES = 4
USED = 32
WIDTH = 896
PARTS_A, FIRST_B = ((0, 384), (384, 256)), 640
WB = WIDTH - FIRST_B
UNITS = ((0, 256), (256, 320))
PARTS = ((0, 256), (256, 256), (512, 64))
FFD = 576
D = 7168
SCORE_SCALE = 192.0 ** (-0.5)
EPSILON = 1e-06

FAR_Z = (4, 3, 5, 2, 6, 1, 7)
FAR_X = (2, 1, 3)
FAR_Y = (2, 1, 3)
FAR_DP = sorted(
    ((dx, dz) for dx in range(NX) for dz in range(NZ) if dx or dz),
    key=lambda o: -(min(o[0], NX - o[0]) + min(o[1], NZ - o[1])),
)


def send(src, dst, send_sem, recv_sem, device):
    copy = pltpu.make_async_remote_copy(
        src_ref=src,
        dst_ref=dst,
        send_sem=send_sem,
        recv_sem=recv_sem,
        device_id=device,
        device_id_type=MESH,
    )
    copy.start()


def wait_bytes(ref, sem):
    pltpu.make_async_copy(ref, ref, sem).wait()


def column(row, n):
    rows = lax.broadcasted_iota(I32, (n, n), 0)
    lanes = lax.broadcasted_iota(I32, (n, n), 1)
    return jnp.sum(jnp.where(rows == lanes, row, 0), axis=1, keepdims=True)


def dot(a, b):
    return jnp.dot(a, b, preferred_element_type=F32)


def dot_t(a, b):
    return lax.dot_general(a, b, (((1,), (1,)), ((), ())), preferred_element_type=F32)


def kernel(
    owner_ref, slot_ref, len_ref, res_ref, nl_ref, resid_ref, gain_ref,
    q_hbm, pool_hbm, vup_hbm, wo_hbm, wg_hbm, wu_hbm, wd_hbm,
    out_ref,
    q_v, pool_t, pool_v, vup_v, wo_v, wgu_v, wt_v, wd_v, load_sem,
    want_v, asked_v, asked_s, sel_v, sel_s, limit_v, smem_sem, req_ss, req_rs,
    pg_send, pg_recv, pg_ss, pg_rs,
    keys, key_ss, key_rs, sib_ss, sib_rs,
    qt_v, scores_v,
    hd_send, hd_in, hd_ss, hd_rs,
    hb, hb_ss, hb_rs, hs_ss, hs_rs,
    sums,
    gat_a, gat_b, gbz_ss, gbz_rs, resid_b, rb_ss, rb_rs,
    act_v, ssq_send, ssq_recv, ssq_ss, ssq_rs,
    units, hids,
):
    dp, tp = lax.axis_index("dp"), lax.axis_index("tp")
    x, z = dp // NZ, dp % NZ
    y, c = tp // NC, tp % NC

    def at(dx=0, dz=0, dy=0, flip=False):
        core = 1 - c if flip else c
        return (((x + dx) % NX) * NZ + (z + dz) % NZ, ((y + dy) % NY) * NC + core)

    unit_loads = [
        (hbm.at[pl.ds(first, width)], wgu_v.at[pl.ds(2 * first + k * width, width)])
        for first, width in UNITS
        for k, hbm in enumerate((wg_hbm, wu_hbm))
    ]
    loads = [
        pltpu.make_async_copy(src, dst, load_sem.at[i])
        for i, (src, dst) in enumerate(
            [(pool_hbm, pool_t), (q_hbm, q_v), (vup_hbm, vup_v), (wo_hbm, wo_v), (wd_hbm, wd_v), *unit_loads]
        )
    ]
    for load in loads:
        load.start()
    ends = []

    def later(ref, sem):
        ends.append(lambda: wait_bytes(ref, sem))


    barrier = pltpu.get_barrier_semaphore()
    for ox, oz in FAR_DP:
        pl.semaphore_signal(barrier, 1, device_id=at(ox, oz), device_id_type=MESH)
    for oy in FAR_Y:
        pl.semaphore_signal(barrier, 1, device_id=at(dy=oy), device_id_type=MESH)
    pl.semaphore_signal(barrier, 1, device_id=at(flip=True), device_id_type=MESH)
    in_tp = dp // 4
    to_self = jnp.where((tp == in_tp) & (z % 2 == c), 1, 0)

    def greet(k, carry):
        source = 2 * k + c

        @pl.when(jnp.logical_not((source == dp) & (in_tp == tp)))
        def _():
            pl.semaphore_signal(barrier, 1, device_id=(source, in_tp), device_id_type=MESH)

        return carry

    lax.fori_loop(0, 16, greet, 0)

    lengths = column(len_ref[...], REQ_D)
    resumed = column(res_ref[...], REQ_D)
    before = (
        lax.broadcasted_iota(I32, (REQ_D, REQ_D, 1), 1) < lax.broadcasted_iota(I32, (REQ_D, REQ_D, 1), 0)
    ).astype(I32)

    def earlier(v):
        return jnp.sum(before * v[None], axis=1)

    lane = lax.broadcasted_iota(I32, (REQ_D, 128), 1)
    lane_owner = lane % 32
    lane_copy = lane // 32
    page_lane = lax.broadcasted_iota(I32, (REQ_D, USED * TOK), 1) // TOK
    owner_base = jnp.zeros((1, 128), I32)
    read_base = jnp.zeros((1, 128), I32)
    wanted = jnp.zeros((1, 128), I32)
    limit = jnp.zeros((REQ_D, USED * TOK), I32)
    chosen = jnp.zeros((1, USED * TOK), I32)
    for p in range(PAGES):
        owner = column(owner_ref[p : p + 1, :], REQ_D)
        read = jnp.where((resumed == 1) & (lengths > p * PAGE), 1, 0)
        match = jnp.where(lane_owner == owner, read, 0)
        copy = owner_base + earlier(match)
        owner_base = owner_base + jnp.sum(match, axis=0, keepdims=True)
        wanted = wanted + jnp.sum(
            jnp.where((match > 0) & (copy == lane_copy), column(slot_ref[p : p + 1, :], REQ_D), 0),
            axis=0, keepdims=True,
        )
        own_copy = jnp.sum(jnp.where(lane < 32, match * copy, 0), axis=1, keepdims=True)
        read_lanes = jnp.broadcast_to(read, (REQ_D, 128))
        place = (read_base + earlier(read_lanes))[:, 0:1]
        read_base = read_base + jnp.sum(read_lanes, axis=0, keepdims=True)
        here = jnp.where(page_lane == place, read, 0)
        limit = limit + here * (lengths - p * PAGE)
        off_x = (x - owner // NZ + NX) % NX
        off_z = (z - owner % NZ + NZ) % NZ
        source = (off_x * NZ + off_z) * 2 + own_copy
        chosen = chosen + jnp.sum(here * source, axis=0, keepdims=True)
    limit_v[...] = limit.astype(F32)
    want_v[0] = wanted
    asked_v[0] = wanted
    sel_v[0] = chosen
    sel_copy = pltpu.make_async_copy(sel_v, sel_s, smem_sem.at[0])
    sel_copy.start()

    pl.semaphore_wait(barrier, 31 + 4 + 16 - to_self)

    for ox, oz in FAR_DP:
        send(want_v.at[0], asked_v.at[ox * NZ + oz], req_ss, req_rs, at(ox, oz))
    later(asked_v.at[pl.ds(1, 31)], req_ss)

    resid_b[pl.ds(x, 1)] = resid_ref[:, FIRST_B:].reshape(1, REQ_D, WB)
    for ox in FAR_X:
        send(resid_b.at[x], resid_b.at[x], rb_ss, rb_rs, at(dx=ox))
    later(resid_b.at[pl.ds(0, 3)], rb_ss)

    loads[1].wait()
    rows = lax.broadcasted_iota(I32, (256, 256), 0)
    lanes = lax.broadcasted_iota(I32, (256, 256), 1)
    swap = jnp.where(lanes == (rows % 16) * 16 + rows // 16, 1.0, 0.0).astype(BF16)
    qt = dot(swap, q_v[...]).astype(BF16)
    qt_v[...] = qt
    own_all = dot_t(qt, nl_ref[...]) * SCORE_SCALE
    own_diag = lax.broadcasted_iota(I32, (256, 16), 1) == lax.broadcasted_iota(I32, (256, 16), 0) % 16
    own_score = jnp.sum(jnp.where(own_diag, own_all, 0.0), axis=1, keepdims=True)
    loads[0].wait()
    token_row = lax.broadcasted_iota(I32, (1024, 128), 0)
    slot_lane = lax.broadcasted_iota(I32, (1024, 128), 1)
    pages = jnp.zeros((1024, COLS), F32)
    for j in range(TOK):
        spread = jnp.where(token_row == slot_lane * TOK + j, 1.0, 0.0).astype(BF16)
        pages = pages + dot_t(spread, pool_t[j])
    pool_v[...] = pages.astype(BF16).reshape(128, TOK, COLS)
    sel_copy.wait()

    wait_bytes(asked_v.at[pl.ds(1, 31)], req_rs)
    asked_copy = pltpu.make_async_copy(asked_v, asked_s, smem_sem.at[1])
    asked_copy.start()
    asked_copy.wait()

    def gather(n_in, buffer, n_out, first, width):
        pair = [
            pool_v[jnp.clip(asked_s[n_in, 0, 32 * k + dp], 0, 127), :, first : first + width] for k in range(2)
        ]
        buffer[n_out] = jnp.concatenate(pair, axis=0)

    for i, (first, width) in enumerate(PARTS):
        for ox, oz in FAR_DP:
            n_out = ox * NZ + oz
            gather(((NX - ox) % NX) * NZ + (NZ - oz) % NZ, pg_send[i], n_out, first, width)
            send(pg_send[i].at[n_out], pg_recv[i].at[n_out], pg_ss.at[i], pg_rs.at[i], at(ox, oz))
        later(pg_send[i].at[pl.ds(1, 31)], pg_ss.at[i])
    for i, (first, width) in enumerate(PARTS):
        gather(0, pg_recv[i], 0, first, width)

    for load in loads[5:]:
        load.wait()
    same = lax.broadcasted_iota(I32, (128, 128), 0) == lax.broadcasted_iota(I32, (128, 128), 1)
    same = jnp.where(same, 1.0, 0.0).astype(BF16)
    for first in range(0, WIDTH, 128):
        wt_v[first : first + 128] = dot_t(same, wgu_v[:, first : first + 128]).astype(BF16)

    def pass_on(i):
        upper, lower = pl.ds(0, 128), pl.ds(128, 128)
        wait_bytes(keys[i].at[1], key_rs.at[i, 1])
        send(keys[i].at[1, upper], keys[i].at[2, upper], key_ss.at[i], key_rs.at[i, 2], at(dy=1))
        send(keys[i].at[1], keys[i].at[5], sib_ss.at[i], sib_rs.at[i, 1], at(flip=True))
        wait_bytes(keys[i].at[3], key_rs.at[i, 3])
        send(keys[i].at[3, lower], keys[i].at[2, lower], key_ss.at[i], key_rs.at[i, 0], at(dy=3))
        send(keys[i].at[3], keys[i].at[7], sib_ss.at[i], sib_rs.at[i, 3], at(flip=True))

    for i in range(len(PARTS)):
        wait_bytes(pg_recv[i].at[pl.ds(1, 31)], pg_rs.at[i])

        def pick(u, carry):
            pair = []
            for k in range(2):
                source = jnp.clip(sel_s[0, 0, (2 * u + k) * TOK], 0, 63)
                both = pg_recv[i][lax.shift_right_logical(source, 1)]
                pair.append(jnp.where(jnp.bitwise_and(source, 1) == 1, both[TOK:], both[:TOK]))
            keys[i][0, pl.ds(pl.multiple_of(u * 16, 16), 16), :] = jnp.concatenate(pair, axis=0)
            return carry

        lax.fori_loop(0, USED // 2, pick, 0)
        for oy in FAR_Y if i == len(PARTS) - 1 else (1, 3):
            send(keys[i].at[0], keys[i].at[oy], key_ss.at[i], key_rs.at[i, oy], at(dy=oy))
        send(keys[i].at[0], keys[i].at[4], sib_ss.at[i], sib_rs.at[i, 0], at(flip=True))
        later(keys[i].at[pl.ds(0, 3)], key_ss.at[i])
        later(keys[i].at[pl.ds(0, 4)], sib_ss.at[i])
        if i:
            pass_on(i - 1)

    limit = limit_v[...].reshape(1, REQ_D, USED * TOK)
    token = (lax.broadcasted_iota(I32, (1, 1, USED * TOK), 2) % TOK).astype(F32)

    def source_of(n):
        core = c if n < 4 else 1 - c
        return ((y + NY - n % 4) % NY) * NC + core

    def score_block(i, n):
        first, width = PARTS[i]
        block = dot_t(qt_v[:, first : first + width], keys[i][n])
        if i:
            block = scores_v[n] + block
        if i == len(PARTS) - 1:
            usable = limit > token + (source_of(n) * TOK).astype(F32)
            block = (block * SCORE_SCALE).reshape(HEADS, REQ_D, USED * TOK)
            block = jnp.where(usable, block, -jnp.inf).reshape(256, USED * TOK)
        scores_v[n] = block

    for i in range(len(PARTS)):
        if i < len(PARTS) - 1:
            wait_bytes(keys[i].at[2, pl.ds(0, 128)], key_rs.at[i, 2])
            wait_bytes(keys[i].at[2, pl.ds(128, 128)], key_rs.at[i, 0])
            send(keys[i].at[2], keys[i].at[6], sib_ss.at[i], sib_rs.at[i, 2], at(flip=True))
        else:
            for oy in (1, 3, 2):
                wait_bytes(keys[i].at[oy], key_rs.at[i, oy])
                send(keys[i].at[oy], keys[i].at[4 + oy], sib_ss.at[i], sib_rs.at[i, oy], at(flip=True))
        for n in range(4):
            score_block(i, n)
        for oy in (0, 1, 3, 2):
            wait_bytes(keys[i].at[4 + oy], sib_rs.at[i, oy])
            score_block(i, 4 + oy)

    peak = scores_v[0]
    for n in range(1, 8):
        peak = jnp.maximum(peak, scores_v[n])
    top = jnp.maximum(own_score, jnp.max(peak, axis=1, keepdims=True))
    own_weight = jnp.exp(own_score - top)
    weight_lanes = jnp.zeros((256, USED * TOK), F32)
    pieces = [jnp.zeros((256, width), F32) for _, width in PARTS[:-1]]
    for n in range(8):
        weights = jnp.exp(scores_v[n] - top)
        weight_lanes = weight_lanes + weights
        weights = weights.astype(BF16)
        pieces = [piece + dot(weights, keys[i][n]) for i, piece in enumerate(pieces)]
    latent = jnp.concatenate(pieces, axis=1)
    weight_sum = own_weight + jnp.sum(weight_lanes, axis=1, keepdims=True)
    own_latent = nl_ref[:, :KL].astype(F32).reshape(1, REQ_D, KL)
    latent = latent.reshape(HEADS, REQ_D, KL) + own_weight.reshape(HEADS, REQ_D, 1) * own_latent
    latent = (latent / weight_sum.reshape(HEADS, REQ_D, 1)).astype(BF16)

    loads[2].wait()
    for h in range(HEADS):
        hd_send[h] = dot(latent[h], vup_v[h]).astype(BF16)
        target = (4 * tp + h // 4, (h % 4) * NC + z % 2)
        is_me = (target[0] == dp) & (target[1] == tp)

        @pl.when(is_me)
        def _():
            pltpu.make_async_copy(hd_send.at[h], hd_in.at[dp // 2], hd_rs).start()

        @pl.when(jnp.logical_not(is_me))
        def _():
            send(hd_send.at[h], hd_in.at[dp // 2], hd_ss, hd_rs, target)

    def heads_left():
        wait_bytes(hd_in.at[pl.ds(0, 15)], hd_ss)

        @pl.when(to_self == 0)
        def _():
            wait_bytes(hd_in.at[0], hd_ss)

    ends.append(heads_left)

    wait_bytes(hd_in, hd_rs)
    own_cols = pl.ds(pl.multiple_of(y * VH, VH), VH)
    hb[:, pl.ds(c, 1), :, own_cols] = hd_in[...].reshape(NX, 1, 64, VH)
    own_block = hb.at[:, c, :, own_cols]
    for oy in FAR_Y:
        send(own_block, own_block, hb_ss, hb_rs.at[oy], at(dy=oy))
    send(own_block, own_block, hs_ss, hs_rs.at[0], at(flip=True))
    later(hb.at[:, pl.ds(0, 1), :, pl.ds(0, 3 * VH)], hb_ss)
    later(hb.at[:, 0], hs_ss)
    for oy in (1, 3, 2):
        cols = pl.ds(pl.multiple_of(((y + NY - oy) % NY) * VH, VH), VH)
        block = hb.at[:, c, :, cols]
        wait_bytes(block, hb_rs.at[oy])
        send(block, block, hs_ss, hs_rs.at[oy], at(flip=True))
    for oy in range(4):
        wait_bytes(own_block, hs_rs.at[oy])

    def sum_over_dp(rows_x, rows_all, weight, place, bufs, ready_a, gather_b, ready_b):
        parts_a, (b_send, b_recv, b_ss, b_rs, b_own, b_mid, bm_recv, bm_ss, bm_rs) = bufs
        for (first, width), (a_send, a_recv, a_ss, a_rs, *_) in zip(PARTS_A, parts_a):
            for ox in FAR_X:
                a_send[ox - 1] = dot(rows_x((x + ox) % NX), weight[:, first : first + width]).astype(BF16)
                send(a_send.at[ox - 1], a_recv.at[ox - 1], a_ss, a_rs, at(dx=ox))
            later(a_send, a_ss)
        b_send[...] = dot(rows_all(), weight[:, FIRST_B:]).astype(BF16).reshape(NX, NZ, REQ_D, WB)
        for oz in FAR_Z:
            send(b_send.at[:, place((z + oz) % NZ)], b_recv.at[oz - 1], b_ss, b_rs, at(dz=oz))
        later(b_recv, b_ss)
        own = dot(rows_x(x), weight[:, :FIRST_B])
        for (first, width), (a_send, a_recv, a_ss, a_rs, a_own, a_mid, am_recv, am_ss, am_rs) in zip(PARTS_A, parts_a):
            total = own[:, first : first + width]
            wait_bytes(a_recv, a_rs)
            for n in range(3):
                total = total + a_recv[n].astype(F32)
            total = total.reshape(NZ, REQ_D, width)
            a_own[...] = total
            a_mid[...] = total.astype(BF16)
            for oz in FAR_Z:
                send(a_mid.at[place((z + oz) % NZ)], am_recv.at[oz - 1], am_ss, am_rs, at(dz=oz))
            later(am_recv, am_ss)
        total = b_send[:, place(z)].astype(F32)
        wait_bytes(b_recv, b_rs)
        for n in range(7):
            total = total + b_recv[n].astype(F32)
        if gather_b:
            bm_recv[x] = total.astype(BF16)
            for ox in FAR_X:
                send(bm_recv.at[x], bm_recv.at[x], bm_ss, bm_rs, at(dx=ox))
            later(bm_recv.at[pl.ds(0, 3)], bm_ss)
        else:
            b_own[...] = total
            b_mid[...] = total.astype(BF16)
            for ox in FAR_X:
                send(b_mid.at[(x + ox) % NX], bm_recv.at[ox - 1], bm_ss, bm_rs, at(dx=ox))
            later(bm_recv, bm_ss)
        for part, (_, _, _, _, a_own, _, am_recv, _, am_rs) in enumerate(parts_a):
            mine = a_own[place(z)]
            wait_bytes(am_recv, am_rs)
            for n in range(7):
                mine = mine + am_recv[n].astype(F32)
            ready_a(part, mine)
        if gather_b:
            wait_bytes(bm_recv.at[pl.ds(0, 3)], bm_rs)
            mine = bm_recv[0].astype(F32)
            for n in range(1, NX):
                mine = mine + bm_recv[n].astype(F32)
        else:
            mine = b_own[x]
            wait_bytes(bm_recv, bm_rs)
            for n in range(3):
                mine = mine + bm_recv[n].astype(F32)
        ready_b(mine)

    def stream_a(part, attended):
        first, width = PARTS_A[part]
        gat, z_ss, z_rs, _, _ = gat_a[part]
        gat[x, z] = (resid_ref[:, first : first + width].astype(F32) + attended).astype(BF16)
        for oz in FAR_Z:
            send(gat.at[x, z], gat.at[x, z], z_ss, z_rs, at(dz=oz))
        later(gat.at[0, pl.ds(0, 7)], z_ss)

    def stream_b(attended):
        wait_bytes(resid_b.at[pl.ds(0, 3)], rb_rs)
        gat_b[:, z] = (resid_b[...].astype(F32) + attended).astype(BF16)
        for oz in FAR_Z:
            send(gat_b.at[:, z], gat_b.at[:, z], gbz_ss, gbz_rs, at(dz=oz))
        later(gat_b.at[:, pl.ds(0, 7)], gbz_ss)

    loads[3].wait()
    sum_over_dp(
        lambda xx: hb[xx].reshape(128, 512), lambda: hb[...].reshape(512, 512), wo_v,
        lambda zz: (zz % 2) * 4 + zz // 2, sums[0], stream_a, True, stream_b,
    )
    for gat, _, z_rs, x_ss, x_rs in gat_a:
        wait_bytes(gat.at[0, pl.ds(0, 7)], z_rs)
        for ox in FAR_X:
            send(gat.at[x], gat.at[x], x_ss, x_rs.at[ox - 1], at(dx=ox))
        later(gat.at[pl.ds(0, 3)], x_ss)

    def widen(block, gain):
        block = block.astype(F32)
        square = block * block
        high = square.astype(BF16)
        low = (square - high.astype(F32)).astype(BF16)
        ones = jnp.ones((8, block.shape[1]), BF16)
        return (block * gain).astype(BF16), (dot_t(ones, high) + dot_t(ones, low))[0:1]

    gain = gain_ref[...].reshape(1, WIDTH)

    for part, ((first, width), (gat, _, _, _, x_rs)) in enumerate(zip(PARTS_A, gat_a)):
        for ox in (0, 1, 3, 2):
            xx = (x + NX - ox) % NX
            if ox:
                wait_bytes(gat.at[xx], x_rs.at[ox - 1])
            act, squares = widen(gat[xx].reshape(128, width), gain[:, first : first + width])
            act_v[pl.ds(xx * 2, 2), :, first : first + width] = act.reshape(2, 64, width)
            ssq_send[xx] = ssq_send[xx] + squares if part else squares
    wait_bytes(gat_b.at[:, pl.ds(0, 7)], gbz_rs)
    for xx in range(NX):
        act, squares = widen(gat_b[xx].reshape(128, WB), gain[:, FIRST_B:])
        act_v[2 * xx : 2 * xx + 2, :, FIRST_B:] = act.reshape(2, 64, WB)
        ssq_send[xx] = ssq_send[xx] + squares
    for n, (oy, flip) in enumerate([(2, True), (2, False), (1, True), (3, True), (1, False), (3, False), (0, True)]):
        send(ssq_send, ssq_recv.at[n], ssq_ss, ssq_rs, at(dy=oy, flip=flip))
    later(ssq_recv, ssq_ss)

    ways = (2, 1, 3, 0)

    def products(half, part):
        first, width = UNITS[part]
        act = jnp.concatenate([act_v[half * 4 + (y + oy) % NY] for oy in ways], axis=0)
        return dot(act, wt_v[:, 2 * first : 2 * (first + width)]).reshape(NY, 64, 2 * width)

    for part, (own, to_core, from_core, core_ss, core_rs, to_y, from_y, y_ss, y_rs) in enumerate(units):
        to_core[...] = products(1 - c, part).astype(BF16)
        send(to_core, from_core, core_ss, core_rs, at(flip=True))
        later(to_core, core_ss)
        own[...] = products(c, part)
        wait_bytes(from_core, core_rs)
        for n in range(3):
            to_y[n] = (own[n] + from_core[n].astype(F32)).astype(BF16)
            send(to_y.at[n], from_y.at[n], y_ss, y_rs, at(dy=ways[n]))
        later(to_y, y_ss)
    wait_bytes(ssq_recv, ssq_rs)
    squares = ssq_send[...]
    for n in range(7):
        squares = squares + ssq_recv[n]
    row_id = lax.broadcasted_iota(I32, (64, 128), 0) + c * 256 + y * 64
    lane_id = lax.broadcasted_iota(I32, (64, 128), 1)
    mean = jnp.zeros((64, 1), F32)
    for n in range(NX):
        mean = mean + jnp.sum(
            jnp.where(row_id == lane_id + 128 * n, squares[n], 0.0), axis=1, keepdims=True
        )
    scale = lax.rsqrt(mean / D + EPSILON)
    for (_, width), (own, _, from_core, _, _, _, from_y, _, y_rs), (hid, hy_ss, hy_rs, hc_ss, hc_rs) in zip(
        UNITS, units, hids
    ):
        both = own[3] + from_core[3].astype(F32)
        wait_bytes(from_y, y_rs)
        for n in range(3):
            both = both + from_y[n].astype(F32)
        both = both * scale
        gate, up = both[:, :width], both[:, width:]
        hid[c, y] = (gate / (1.0 + jnp.exp(-gate)) * up).astype(BF16)
        for oy in FAR_Y:
            send(hid.at[c, y], hid.at[c, y], hy_ss, hy_rs.at[oy - 1], at(dy=oy))
        send(hid.at[c, y], hid.at[c, y], hc_ss, hc_rs, at(flip=True))
        later(hid.at[0, pl.ds(0, 3)], hy_ss)
        later(hid.at[0], hc_ss)
    for hid, _, hy_rs, hc_ss, hc_rs in hids:
        for oy in (1, 3, 2):
            yy = (y + NY - oy) % NY
            wait_bytes(hid.at[c, yy], hy_rs.at[oy - 1])
            send(hid.at[c, yy], hid.at[c, yy], hc_ss, hc_rs, at(flip=True))
    for hid, _, _, _, hc_rs in hids:
        wait_bytes(hid.at[1 - c], hc_rs)

    loads[4].wait()

    def out_a(part, lowered):
        first, width = PARTS_A[part]
        out_ref[:, first : first + width] = (gat_a[part][0][x, z].astype(F32) + lowered).astype(BF16)

    def out_b(lowered):
        out_ref[:, FIRST_B:] = (gat_b[x, z].astype(F32) + lowered).astype(BF16)

    sum_over_dp(
        lambda xx: jnp.concatenate(
            [hid[0][xx // 2, pl.ds((xx % 2) * 2, 2)].reshape(128, -1) for hid in hids], axis=1
        ),
        lambda: jnp.concatenate([hid[0][...].reshape(512, -1) for hid in hids], axis=1), wd_v,
        lambda zz: zz, sums[1], out_a, False, out_b,
    )
    for end in ends:
        end()


def per_device(
    queries, new_latent, residual, pool, page_owner, page_slot, lengths, resumed,
    value_up, out_proj, norm_gain, gate_weight, up_weight, down_weight,
):
    vmem = pl.BlockSpec(memory_space=pltpu.VMEM)
    anywhere = pl.BlockSpec(memory_space=pl.ANY)
    dma, V = pltpu.SemaphoreType.DMA, pltpu.VMEM
    one, n = dma, len(PARTS)
    def sum_scratch(gather_b):
        return [
            [
                [V((3, 128, w), BF16), V((3, 128, w), BF16), one, one,
                 V((NZ, REQ_D, w), F32), V((NZ, REQ_D, w), BF16), V((7, REQ_D, w), BF16), one, one]
                for _, w in PARTS_A
            ],
            [V((NX, NZ, REQ_D, WB), BF16), V((7, NX, REQ_D, WB), BF16), one, one,
             V((NX, REQ_D, WB), F32), V((NX, REQ_D, WB), BF16),
             V((NX, NX, REQ_D, WB) if gather_b else (3, REQ_D, WB), BF16), one, one],
        ]

    scratch = [
        V((256, COLS), BF16), V((TOK, COLS, 128), BF16), V((128, TOK, COLS), BF16), V((HEADS, KL, VH), BF16),
        V((512, WIDTH), BF16), V((2 * FFD, WIDTH), BF16), V((WIDTH, 2 * FFD), BF16), V((FFD, WIDTH), BF16), dma((9,)),
        V((1, 1, 128), I32), V((32, 1, 128), I32), pltpu.SMEM((32, 1, 128), I32),
        V((1, 1, 256), I32), pltpu.SMEM((1, 1, 256), I32), V((REQ_D, 256), F32), dma((2,)), one, one,
        [V((32, 16, w), BF16) for _, w in PARTS], [V((32, 16, w), BF16) for _, w in PARTS], dma((n,)), dma((n,)),
        [V((8, 256, w), BF16) for _, w in PARTS], dma((n,)), dma((n, 4)), dma((n,)), dma((n, 4)),
        V((256, COLS), BF16), V((8, 256, 256), F32),
        V((HEADS, 16, VH), BF16), V((16, 16, VH), BF16), one, one,
        V((NX, NC, 64, 512), BF16), one, dma((4,)), one, dma((4,)),
        [sum_scratch(True), sum_scratch(False)],
        [[V((NX, NZ, REQ_D, w), BF16), one, one, one, dma((3,))] for _, w in PARTS_A],
        V((NX, NZ, REQ_D, WB), BF16), one, one, V((NX, REQ_D, WB), BF16), one, one,
        V((8, 64, WIDTH), BF16), V((NX, 1, 128), F32), V((7, NX, 1, 128), F32), one, one,
        [
            [V((NY, 64, 2 * w), F32), V((NY, 64, 2 * w), BF16), V((NY, 64, 2 * w), BF16), one, one,
             V((3, 64, 2 * w), BF16), V((3, 64, 2 * w), BF16), one, one]
            for _, w in UNITS
        ],
        [[V((NC, NY, 64, w), BF16), one, dma((3,)), one, one] for _, w in UNITS],
    ]
    return pl.pallas_call(
        kernel,
        out_shape=jax.ShapeDtypeStruct((REQ_D, WIDTH), BF16),
        in_specs=[vmem] * 7 + [anywhere] * 7,
        out_specs=vmem,
        scratch_shapes=scratch,
        compiler_params=pltpu.CompilerParams(
            collective_id=0, has_side_effects=True, vmem_limit_bytes=56 * 1024 * 1024
        ),
        name="layer",
    )(
        page_owner.T, page_slot.T, lengths.reshape(1, REQ_D), resumed.reshape(1, REQ_D), new_latent, residual,
        norm_gain, queries.reshape(256, COLS), pool.transpose(1, 2, 0), value_up, out_proj,
        gate_weight.T, up_weight.T, down_weight,
    )


def solution(mesh):
    return jax.shard_map(
        per_device,
        mesh=mesh,
        in_specs=(
            P("dp", "tp", None), P("dp", None), P("dp", "tp"), P("dp", "tp", None), P("dp", None), P("dp", None),
            P("dp"), P("dp"), P("tp", None, None), P("dp", "tp"), P("tp"), P("tp", "dp"), P("tp", "dp"),
            P("dp", "tp"),
        ),
        out_specs=P("dp", "tp"),
        check_vma=False,
    )
```

```python
import functools

import jax
import jax.numpy as jnp
from jax import lax
from jax.experimental import pallas as pl
from jax.experimental.pallas import tpu as pltpu
from jax.sharding import PartitionSpec as P

MESH = pl.DeviceIdType.MESH
F32, BF16, I32 = jnp.float32, jnp.bfloat16, jnp.int32

NX, NY, NZ, NC = 4, 4, 8, 2
REQ_D = 16
HEADS = 16
COLS = 576
KL = 512
VH = 128
TOK = 8
PAGE = 64
PAGES = 4
USED = 32
WIDTH = 896
PARTS_A, FIRST_B = ((0, 384), (384, 256)), 640
WB = WIDTH - FIRST_B
UNITS = ((0, 256), (256, 256), (512, 64))
PARTS = ((0, 256), (256, 256), (512, 64))
FFD = 576
D = 7168
SCORE_SCALE = 192.0 ** (-0.5)
EPSILON = 1e-06

FAR_Z = (4, 3, 5, 2, 6, 1, 7)
FAR_X = (2, 1, 3)
FAR_Y = (2, 1, 3)
FAR_DP = sorted(
    ((dx, dz) for dx in range(NX) for dz in range(NZ) if dx or dz),
    key=lambda o: -(min(o[0], NX - o[0]) + min(o[1], NZ - o[1])),
)


def send(src, dst, send_sem, recv_sem, device):
    copy = pltpu.make_async_remote_copy(
        src_ref=src,
        dst_ref=dst,
        send_sem=send_sem,
        recv_sem=recv_sem,
        device_id=device,
        device_id_type=MESH,
    )
    copy.start()


def wait_bytes(ref, sem):
    pltpu.make_async_copy(ref, ref, sem).wait()


def column(row, n):
    rows = lax.broadcasted_iota(I32, (n, n), 0)
    lanes = lax.broadcasted_iota(I32, (n, n), 1)
    return jnp.sum(jnp.where(rows == lanes, row, 0), axis=1, keepdims=True)


def dot(a, b):
    return jnp.dot(a, b, preferred_element_type=F32)


def dot_t(a, b):
    return lax.dot_general(a, b, (((1,), (1,)), ((), ())), preferred_element_type=F32)


def kernel(
    owner_ref, slot_ref, len_ref, res_ref, nl_ref, resid_ref, gain_ref,
    q_hbm, pool_hbm, vup_hbm, wo_hbm, wg_hbm, wu_hbm, wd_hbm,
    out_ref,
    q_v, pool_t, pool_v, vup_v, wo_v, wgu_v, wt_v, wd_v, load_sem,
    want_v, asked_v, asked_s, sel_v, sel_s, limit_v, smem_sem, req_ss, req_rs,
    pg_send, pg_recv, pg_ss, pg_rs,
    keys, key_ss, key_rs, sib_ss, sib_rs,
    qt_v, scores_v,
    hd_send, hd_in, hd_ss, hd_rs,
    hb, hb_ss, hb_rs, hs_ss, hs_rs,
    sums,
    gat_a, gat_b, gbz_ss, gbz_rs, resid_b, rb_ss, rb_rs,
    act_v, ssq_send, ssq_recv, ssq_ss, ssq_rs,
    units, hids,
):
    dp, tp = lax.axis_index("dp"), lax.axis_index("tp")
    x, z = dp // NZ, dp % NZ
    y, c = tp // NC, tp % NC

    def at(dx=0, dz=0, dy=0, flip=False):
        core = 1 - c if flip else c
        return (((x + dx) % NX) * NZ + (z + dz) % NZ, ((y + dy) % NY) * NC + core)

    unit_loads = [
        (hbm.at[pl.ds(first, width)], wgu_v.at[pl.ds(2 * first + k * width, width)])
        for first, width in UNITS
        for k, hbm in enumerate((wg_hbm, wu_hbm))
    ]
    loads = [
        pltpu.make_async_copy(src, dst, load_sem.at[i])
        for i, (src, dst) in enumerate(
            [(pool_hbm, pool_t), (q_hbm, q_v), (vup_hbm, vup_v), (wo_hbm, wo_v), (wd_hbm, wd_v), *unit_loads]
        )
    ]
    for load in loads:
        load.start()
    ends = []

    def later(ref, sem):
        ends.append(lambda: wait_bytes(ref, sem))


    barrier = pltpu.get_barrier_semaphore()
    for ox, oz in FAR_DP:
        pl.semaphore_signal(barrier, 1, device_id=at(ox, oz), device_id_type=MESH)
    for oy in FAR_Y:
        pl.semaphore_signal(barrier, 1, device_id=at(dy=oy), device_id_type=MESH)
    pl.semaphore_signal(barrier, 1, device_id=at(flip=True), device_id_type=MESH)
    in_tp = dp // 4
    to_self = jnp.where((tp == in_tp) & (z % 2 == c), 1, 0)

    def greet(k, carry):
        source = 2 * k + c

        @pl.when(jnp.logical_not((source == dp) & (in_tp == tp)))
        def _():
            pl.semaphore_signal(barrier, 1, device_id=(source, in_tp), device_id_type=MESH)

        return carry

    lax.fori_loop(0, 16, greet, 0)

    lengths = column(len_ref[...], REQ_D)
    resumed = column(res_ref[...], REQ_D)
    before = (
        lax.broadcasted_iota(I32, (REQ_D, REQ_D, 1), 1) < lax.broadcasted_iota(I32, (REQ_D, REQ_D, 1), 0)
    ).astype(I32)

    def earlier(v):
        return jnp.sum(before * v[None], axis=1)

    lane = lax.broadcasted_iota(I32, (REQ_D, 128), 1)
    lane_owner = lane % 32
    lane_copy = lane // 32
    page_lane = lax.broadcasted_iota(I32, (REQ_D, USED * TOK), 1) // TOK
    owner_base = jnp.zeros((1, 128), I32)
    read_base = jnp.zeros((1, 128), I32)
    wanted = jnp.zeros((1, 128), I32)
    limit = jnp.zeros((REQ_D, USED * TOK), I32)
    chosen = jnp.zeros((1, USED * TOK), I32)
    for p in range(PAGES):
        owner = column(owner_ref[p : p + 1, :], REQ_D)
        read = jnp.where((resumed == 1) & (lengths > p * PAGE), 1, 0)
        match = jnp.where(lane_owner == owner, read, 0)
        copy = owner_base + earlier(match)
        owner_base = owner_base + jnp.sum(match, axis=0, keepdims=True)
        wanted = wanted + jnp.sum(
            jnp.where((match > 0) & (copy == lane_copy), column(slot_ref[p : p + 1, :], REQ_D), 0),
            axis=0, keepdims=True,
        )
        own_copy = jnp.sum(jnp.where(lane < 32, match * copy, 0), axis=1, keepdims=True)
        read_lanes = jnp.broadcast_to(read, (REQ_D, 128))
        place = (read_base + earlier(read_lanes))[:, 0:1]
        read_base = read_base + jnp.sum(read_lanes, axis=0, keepdims=True)
        here = jnp.where(page_lane == place, read, 0)
        limit = limit + here * (lengths - p * PAGE)
        off_x = (x - owner // NZ + NX) % NX
        off_z = (z - owner % NZ + NZ) % NZ
        source = (off_x * NZ + off_z) * 2 + own_copy
        chosen = chosen + jnp.sum(here * source, axis=0, keepdims=True)
    limit_v[...] = limit.astype(F32)
    want_v[0] = wanted
    asked_v[0] = wanted
    sel_v[0] = chosen
    sel_copy = pltpu.make_async_copy(sel_v, sel_s, smem_sem.at[0])
    sel_copy.start()

    pl.semaphore_wait(barrier, 31 + 4 + 16 - to_self)

    for ox, oz in FAR_DP:
        send(want_v.at[0], asked_v.at[ox * NZ + oz], req_ss, req_rs, at(ox, oz))
    later(asked_v.at[pl.ds(1, 31)], req_ss)

    resid_b[pl.ds(x, 1)] = resid_ref[:, FIRST_B:].reshape(1, REQ_D, WB)
    for ox in FAR_X:
        send(resid_b.at[x], resid_b.at[x], rb_ss, rb_rs, at(dx=ox))
    later(resid_b.at[pl.ds(0, 3)], rb_ss)

    loads[1].wait()
    rows = lax.broadcasted_iota(I32, (256, 256), 0)
    lanes = lax.broadcasted_iota(I32, (256, 256), 1)
    swap = jnp.where(lanes == (rows % 16) * 16 + rows // 16, 1.0, 0.0).astype(BF16)
    qt = dot(swap, q_v[...]).astype(BF16)
    qt_v[...] = qt
    own_all = dot_t(qt, nl_ref[...]) * SCORE_SCALE
    own_diag = lax.broadcasted_iota(I32, (256, 16), 1) == lax.broadcasted_iota(I32, (256, 16), 0) % 16
    own_score = jnp.sum(jnp.where(own_diag, own_all, 0.0), axis=1, keepdims=True)
    loads[0].wait()
    token_row = lax.broadcasted_iota(I32, (1024, 128), 0)
    slot_lane = lax.broadcasted_iota(I32, (1024, 128), 1)
    pages = jnp.zeros((1024, COLS), F32)
    for j in range(TOK):
        spread = jnp.where(token_row == slot_lane * TOK + j, 1.0, 0.0).astype(BF16)
        pages = pages + dot_t(spread, pool_t[j])
    pool_v[...] = pages.astype(BF16).reshape(128, TOK, COLS)
    sel_copy.wait()

    wait_bytes(asked_v.at[pl.ds(1, 31)], req_rs)
    asked_copy = pltpu.make_async_copy(asked_v, asked_s, smem_sem.at[1])
    asked_copy.start()
    asked_copy.wait()

    def gather(n_in, buffer, n_out, first, width):
        pair = [
            pool_v[jnp.clip(asked_s[n_in, 0, 32 * k + dp], 0, 127), :, first : first + width] for k in range(2)
        ]
        buffer[n_out] = jnp.concatenate(pair, axis=0)

    for i, (first, width) in enumerate(PARTS):
        for ox, oz in FAR_DP:
            n_out = ox * NZ + oz
            gather(((NX - ox) % NX) * NZ + (NZ - oz) % NZ, pg_send[i], n_out, first, width)
            send(pg_send[i].at[n_out], pg_recv[i].at[n_out], pg_ss.at[i], pg_rs.at[i], at(ox, oz))
        later(pg_send[i].at[pl.ds(1, 31)], pg_ss.at[i])
    for i, (first, width) in enumerate(PARTS):
        gather(0, pg_recv[i], 0, first, width)

    for load in loads[5:]:
        load.wait()
    same = lax.broadcasted_iota(I32, (128, 128), 0) == lax.broadcasted_iota(I32, (128, 128), 1)
    same = jnp.where(same, 1.0, 0.0).astype(BF16)
    for first in range(0, WIDTH, 128):
        wt_v[first : first + 128] = dot_t(same, wgu_v[:, first : first + 128]).astype(BF16)

    def pass_on(i):
        upper, lower = pl.ds(0, 128), pl.ds(128, 128)
        wait_bytes(keys[i].at[1], key_rs.at[i, 1])
        send(keys[i].at[1, upper], keys[i].at[2, upper], key_ss.at[i], key_rs.at[i, 2], at(dy=1))
        send(keys[i].at[1], keys[i].at[5], sib_ss.at[i], sib_rs.at[i, 1], at(flip=True))
        wait_bytes(keys[i].at[3], key_rs.at[i, 3])
        send(keys[i].at[3, lower], keys[i].at[2, lower], key_ss.at[i], key_rs.at[i, 0], at(dy=3))
        send(keys[i].at[3], keys[i].at[7], sib_ss.at[i], sib_rs.at[i, 3], at(flip=True))

    for i in range(len(PARTS)):
        wait_bytes(pg_recv[i].at[pl.ds(1, 31)], pg_rs.at[i])

        def pick(u, carry):
            pair = []
            for k in range(2):
                source = jnp.clip(sel_s[0, 0, (2 * u + k) * TOK], 0, 63)
                both = pg_recv[i][lax.shift_right_logical(source, 1)]
                pair.append(jnp.where(jnp.bitwise_and(source, 1) == 1, both[TOK:], both[:TOK]))
            keys[i][0, pl.ds(pl.multiple_of(u * 16, 16), 16), :] = jnp.concatenate(pair, axis=0)
            return carry

        lax.fori_loop(0, USED // 2, pick, 0)
        for oy in FAR_Y if i == len(PARTS) - 1 else (1, 3):
            send(keys[i].at[0], keys[i].at[oy], key_ss.at[i], key_rs.at[i, oy], at(dy=oy))
        send(keys[i].at[0], keys[i].at[4], sib_ss.at[i], sib_rs.at[i, 0], at(flip=True))
        later(keys[i].at[pl.ds(0, 3)], key_ss.at[i])
        later(keys[i].at[pl.ds(0, 4)], sib_ss.at[i])
        if i:
            pass_on(i - 1)

    limit = limit_v[...].reshape(1, REQ_D, USED * TOK)
    token = (lax.broadcasted_iota(I32, (1, 1, USED * TOK), 2) % TOK).astype(F32)

    def source_of(n):
        core = c if n < 4 else 1 - c
        return ((y + NY - n % 4) % NY) * NC + core

    def score_block(i, n):
        first, width = PARTS[i]
        block = dot_t(qt_v[:, first : first + width], keys[i][n])
        if i:
            block = scores_v[n] + block
        if i == len(PARTS) - 1:
            usable = limit > token + (source_of(n) * TOK).astype(F32)
            block = (block * SCORE_SCALE).reshape(HEADS, REQ_D, USED * TOK)
            block = jnp.where(usable, block, -jnp.inf).reshape(256, USED * TOK)
        scores_v[n] = block

    for i in range(len(PARTS)):
        if i < len(PARTS) - 1:
            wait_bytes(keys[i].at[2, pl.ds(0, 128)], key_rs.at[i, 2])
            wait_bytes(keys[i].at[2, pl.ds(128, 128)], key_rs.at[i, 0])
            send(keys[i].at[2], keys[i].at[6], sib_ss.at[i], sib_rs.at[i, 2], at(flip=True))
        else:
            for oy in (1, 3, 2):
                wait_bytes(keys[i].at[oy], key_rs.at[i, oy])
                send(keys[i].at[oy], keys[i].at[4 + oy], sib_ss.at[i], sib_rs.at[i, oy], at(flip=True))
        for n in range(4):
            score_block(i, n)
        for oy in (0, 1, 3, 2):
            wait_bytes(keys[i].at[4 + oy], sib_rs.at[i, oy])
            score_block(i, 4 + oy)

    peak = scores_v[0]
    for n in range(1, 8):
        peak = jnp.maximum(peak, scores_v[n])
    top = jnp.maximum(own_score, jnp.max(peak, axis=1, keepdims=True))
    own_weight = jnp.exp(own_score - top)
    weight_lanes = jnp.zeros((256, USED * TOK), F32)
    pieces = [jnp.zeros((256, width), F32) for _, width in PARTS[:-1]]
    for n in range(8):
        weights = jnp.exp(scores_v[n] - top)
        weight_lanes = weight_lanes + weights
        weights = weights.astype(BF16)
        pieces = [piece + dot(weights, keys[i][n]) for i, piece in enumerate(pieces)]
    latent = jnp.concatenate(pieces, axis=1)
    weight_sum = own_weight + jnp.sum(weight_lanes, axis=1, keepdims=True)
    own_latent = nl_ref[:, :KL].astype(F32).reshape(1, REQ_D, KL)
    latent = latent.reshape(HEADS, REQ_D, KL) + own_weight.reshape(HEADS, REQ_D, 1) * own_latent
    latent = (latent / weight_sum.reshape(HEADS, REQ_D, 1)).astype(BF16)

    loads[2].wait()
    for h in range(HEADS):
        hd_send[h] = dot(latent[h], vup_v[h]).astype(BF16)
        target = (4 * tp + h // 4, (h % 4) * NC + z % 2)
        is_me = (target[0] == dp) & (target[1] == tp)

        @pl.when(is_me)
        def _():
            pltpu.make_async_copy(hd_send.at[h], hd_in.at[dp // 2], hd_rs).start()

        @pl.when(jnp.logical_not(is_me))
        def _():
            send(hd_send.at[h], hd_in.at[dp // 2], hd_ss, hd_rs, target)

    def heads_left():
        wait_bytes(hd_in.at[pl.ds(0, 15)], hd_ss)

        @pl.when(to_self == 0)
        def _():
            wait_bytes(hd_in.at[0], hd_ss)

    ends.append(heads_left)

    wait_bytes(hd_in, hd_rs)
    own_cols = pl.ds(pl.multiple_of(y * VH, VH), VH)
    hb[:, pl.ds(c, 1), :, own_cols] = hd_in[...].reshape(NX, 1, 64, VH)
    own_block = hb.at[:, c, :, own_cols]
    for oy in FAR_Y:
        send(own_block, own_block, hb_ss, hb_rs.at[oy], at(dy=oy))
    send(own_block, own_block, hs_ss, hs_rs.at[0], at(flip=True))
    later(hb.at[:, pl.ds(0, 1), :, pl.ds(0, 3 * VH)], hb_ss)
    later(hb.at[:, 0], hs_ss)
    for oy in (1, 3, 2):
        cols = pl.ds(pl.multiple_of(((y + NY - oy) % NY) * VH, VH), VH)
        block = hb.at[:, c, :, cols]
        wait_bytes(block, hb_rs.at[oy])
        send(block, block, hs_ss, hs_rs.at[oy], at(flip=True))
    for oy in range(4):
        wait_bytes(own_block, hs_rs.at[oy])

    def sum_over_dp(rows_x, rows_all, weight, place, bufs, ready_a, gather_b, ready_b):
        parts_a, (b_send, b_recv, b_ss, b_rs, b_own, b_mid, bm_recv, bm_ss, bm_rs) = bufs
        for (first, width), (a_send, a_recv, a_ss, a_rs, *_) in zip(PARTS_A, parts_a):
            for ox in FAR_X:
                a_send[ox - 1] = dot(rows_x((x + ox) % NX), weight[:, first : first + width]).astype(BF16)
                send(a_send.at[ox - 1], a_recv.at[ox - 1], a_ss, a_rs, at(dx=ox))
            later(a_send, a_ss)
        b_send[...] = dot(rows_all(), weight[:, FIRST_B:]).astype(BF16).reshape(NX, NZ, REQ_D, WB)
        for oz in FAR_Z:
            send(b_send.at[:, place((z + oz) % NZ)], b_recv.at[oz - 1], b_ss, b_rs, at(dz=oz))
        later(b_recv, b_ss)
        own = dot(rows_x(x), weight[:, :FIRST_B])
        for (first, width), (a_send, a_recv, a_ss, a_rs, a_own, a_mid, am_recv, am_ss, am_rs) in zip(PARTS_A, parts_a):
            total = own[:, first : first + width]
            wait_bytes(a_recv, a_rs)
            for n in range(3):
                total = total + a_recv[n].astype(F32)
            total = total.reshape(NZ, REQ_D, width)
            a_own[...] = total
            a_mid[...] = total.astype(BF16)
            for oz in FAR_Z:
                send(a_mid.at[place((z + oz) % NZ)], am_recv.at[oz - 1], am_ss, am_rs, at(dz=oz))
            later(am_recv, am_ss)
        total = b_send[:, place(z)].astype(F32)
        wait_bytes(b_recv, b_rs)
        for n in range(7):
            total = total + b_recv[n].astype(F32)
        if gather_b:
            bm_recv[x] = total.astype(BF16)
            for ox in FAR_X:
                send(bm_recv.at[x], bm_recv.at[x], bm_ss, bm_rs, at(dx=ox))
            later(bm_recv.at[pl.ds(0, 3)], bm_ss)
        else:
            b_own[...] = total
            b_mid[...] = total.astype(BF16)
            for ox in FAR_X:
                send(b_mid.at[(x + ox) % NX], bm_recv.at[ox - 1], bm_ss, bm_rs, at(dx=ox))
            later(bm_recv, bm_ss)
        for part, (_, _, _, _, a_own, _, am_recv, _, am_rs) in enumerate(parts_a):
            mine = a_own[place(z)]
            wait_bytes(am_recv, am_rs)
            for n in range(7):
                mine = mine + am_recv[n].astype(F32)
            ready_a(part, mine)
        if gather_b:
            wait_bytes(bm_recv.at[pl.ds(0, 3)], bm_rs)
            mine = bm_recv[0].astype(F32)
            for n in range(1, NX):
                mine = mine + bm_recv[n].astype(F32)
        else:
            mine = b_own[x]
            wait_bytes(bm_recv, bm_rs)
            for n in range(3):
                mine = mine + bm_recv[n].astype(F32)
        ready_b(mine)

    def stream_a(part, attended):
        first, width = PARTS_A[part]
        gat, z_ss, z_rs, _, _ = gat_a[part]
        gat[x, z] = (resid_ref[:, first : first + width].astype(F32) + attended).astype(BF16)
        for oz in FAR_Z:
            send(gat.at[x, z], gat.at[x, z], z_ss, z_rs, at(dz=oz))
        later(gat.at[0, pl.ds(0, 7)], z_ss)

    def stream_b(attended):
        wait_bytes(resid_b.at[pl.ds(0, 3)], rb_rs)
        gat_b[:, z] = (resid_b[...].astype(F32) + attended).astype(BF16)
        for oz in FAR_Z:
            send(gat_b.at[:, z], gat_b.at[:, z], gbz_ss, gbz_rs, at(dz=oz))
        later(gat_b.at[:, pl.ds(0, 7)], gbz_ss)

    loads[3].wait()
    sum_over_dp(
        lambda xx: hb[xx].reshape(128, 512), lambda: hb[...].reshape(512, 512), wo_v,
        lambda zz: (zz % 2) * 4 + zz // 2, sums[0], stream_a, True, stream_b,
    )
    for gat, _, z_rs, x_ss, x_rs in gat_a:
        wait_bytes(gat.at[0, pl.ds(0, 7)], z_rs)
        for ox in FAR_X:
            send(gat.at[x], gat.at[x], x_ss, x_rs.at[ox - 1], at(dx=ox))
        later(gat.at[pl.ds(0, 3)], x_ss)

    def widen(block, gain):
        return (block.astype(F32) * gain).astype(BF16)

    def square_sums():
        for xx in range(NX):
            total = jnp.zeros((8, 128), F32)
            for gat in [gat[0] for gat in gat_a] + [gat_b]:
                block = gat[xx].reshape(128, -1).astype(F32)
                square = block * block
                high = square.astype(BF16)
                low = (square - high.astype(F32)).astype(BF16)
                ones = jnp.ones((8, block.shape[1]), BF16)
                total = total + dot_t(ones, high) + dot_t(ones, low)
            ssq_send[xx] = total[0:1]
        tp_others = [(2, True), (2, False), (1, True), (3, True), (1, False), (3, False), (0, True)]
        for n, (oy, flip) in enumerate(tp_others):
            send(ssq_send, ssq_recv.at[n], ssq_ss, ssq_rs, at(dy=oy, flip=flip))
        later(ssq_recv, ssq_ss)

    gain = gain_ref[...].reshape(1, WIDTH)

    for (first, width), (gat, _, _, _, x_rs) in zip(PARTS_A, gat_a):
        for ox in (0, 1, 3, 2):
            xx = (x + NX - ox) % NX
            if ox:
                wait_bytes(gat.at[xx], x_rs.at[ox - 1])
            act = widen(gat[xx].reshape(128, width), gain[:, first : first + width])
            act_v[pl.ds(xx * 2, 2), :, first : first + width] = act.reshape(2, 64, width)
    wait_bytes(gat_b.at[:, pl.ds(0, 7)], gbz_rs)
    for xx in range(NX):
        act = widen(gat_b[xx].reshape(128, WB), gain[:, FIRST_B:])
        act_v[2 * xx : 2 * xx + 2, :, FIRST_B:] = act.reshape(2, 64, WB)

    ways = (2, 1, 3, 0)

    def products(half, part):
        first, width = UNITS[part]
        act = jnp.concatenate([act_v[half * 4 + (y + oy) % NY] for oy in ways], axis=0)
        return dot(act, wt_v[:, 2 * first : 2 * (first + width)]).reshape(NY, 64, 2 * width)

    for part, (own, to_core, from_core, core_ss, core_rs, to_y, from_y, y_ss, y_rs) in enumerate(units):
        to_core[...] = products(1 - c, part).astype(BF16)
        send(to_core, from_core, core_ss, core_rs, at(flip=True))
        later(to_core, core_ss)
        own[...] = products(c, part)
        if part == 1:
            square_sums()
        wait_bytes(from_core, core_rs)
        for n in range(3):
            to_y[n] = (own[n] + from_core[n].astype(F32)).astype(BF16)
            send(to_y.at[n], from_y.at[n], y_ss, y_rs, at(dy=ways[n]))
        later(to_y, y_ss)
    wait_bytes(ssq_recv, ssq_rs)
    squares = ssq_send[...]
    for n in range(7):
        squares = squares + ssq_recv[n]
    row_id = lax.broadcasted_iota(I32, (64, 128), 0) + c * 256 + y * 64
    lane_id = lax.broadcasted_iota(I32, (64, 128), 1)
    mean = jnp.zeros((64, 1), F32)
    for n in range(NX):
        mean = mean + jnp.sum(
            jnp.where(row_id == lane_id + 128 * n, squares[n], 0.0), axis=1, keepdims=True
        )
    scale = lax.rsqrt(mean / D + EPSILON)
    for (_, width), (own, _, from_core, _, _, _, from_y, _, y_rs), (hid, hy_ss, hy_rs, hc_ss, hc_rs) in zip(
        UNITS, units, hids
    ):
        both = own[3] + from_core[3].astype(F32)
        wait_bytes(from_y, y_rs)
        for n in range(3):
            both = both + from_y[n].astype(F32)
        both = both * scale
        gate, up = both[:, :width], both[:, width:]
        hid[c, y] = (gate / (1.0 + jnp.exp(-gate)) * up).astype(BF16)
        for oy in FAR_Y:
            send(hid.at[c, y], hid.at[c, y], hy_ss, hy_rs.at[oy - 1], at(dy=oy))
        send(hid.at[c, y], hid.at[c, y], hc_ss, hc_rs, at(flip=True))
        later(hid.at[0, pl.ds(0, 3)], hy_ss)
        later(hid.at[0], hc_ss)
    for hid, _, hy_rs, hc_ss, hc_rs in hids:
        for oy in (1, 3, 2):
            yy = (y + NY - oy) % NY
            wait_bytes(hid.at[c, yy], hy_rs.at[oy - 1])
            send(hid.at[c, yy], hid.at[c, yy], hc_ss, hc_rs, at(flip=True))
    for hid, _, _, _, hc_rs in hids:
        wait_bytes(hid.at[1 - c], hc_rs)

    loads[4].wait()

    def out_a(part, lowered):
        first, width = PARTS_A[part]
        out_ref[:, first : first + width] = (gat_a[part][0][x, z].astype(F32) + lowered).astype(BF16)

    def out_b(lowered):
        out_ref[:, FIRST_B:] = (gat_b[x, z].astype(F32) + lowered).astype(BF16)

    sum_over_dp(
        lambda xx: jnp.concatenate(
            [hid[0][xx // 2, pl.ds((xx % 2) * 2, 2)].reshape(128, -1) for hid in hids], axis=1
        ),
        lambda: jnp.concatenate([hid[0][...].reshape(512, -1) for hid in hids], axis=1), wd_v,
        lambda zz: zz, sums[1], out_a, False, out_b,
    )
    for end in ends:
        end()


def per_device(
    queries, new_latent, residual, pool, page_owner, page_slot, lengths, resumed,
    value_up, out_proj, norm_gain, gate_weight, up_weight, down_weight,
):
    vmem = pl.BlockSpec(memory_space=pltpu.VMEM)
    anywhere = pl.BlockSpec(memory_space=pl.ANY)
    dma, V = pltpu.SemaphoreType.DMA, pltpu.VMEM
    one, n = dma, len(PARTS)
    def sum_scratch(gather_b):
        return [
            [
                [V((3, 128, w), BF16), V((3, 128, w), BF16), one, one,
                 V((NZ, REQ_D, w), F32), V((NZ, REQ_D, w), BF16), V((7, REQ_D, w), BF16), one, one]
                for _, w in PARTS_A
            ],
            [V((NX, NZ, REQ_D, WB), BF16), V((7, NX, REQ_D, WB), BF16), one, one,
             V((NX, REQ_D, WB), F32), V((NX, REQ_D, WB), BF16),
             V((NX, NX, REQ_D, WB) if gather_b else (3, REQ_D, WB), BF16), one, one],
        ]

    scratch = [
        V((256, COLS), BF16), V((TOK, COLS, 128), BF16), V((128, TOK, COLS), BF16), V((HEADS, KL, VH), BF16),
        V((512, WIDTH), BF16), V((2 * FFD, WIDTH), BF16), V((WIDTH, 2 * FFD), BF16), V((FFD, WIDTH), BF16), dma((5 + 2 * len(UNITS),)),
        V((1, 1, 128), I32), V((32, 1, 128), I32), pltpu.SMEM((32, 1, 128), I32),
        V((1, 1, 256), I32), pltpu.SMEM((1, 1, 256), I32), V((REQ_D, 256), F32), dma((2,)), one, one,
        [V((32, 16, w), BF16) for _, w in PARTS], [V((32, 16, w), BF16) for _, w in PARTS], dma((n,)), dma((n,)),
        [V((8, 256, w), BF16) for _, w in PARTS], dma((n,)), dma((n, 4)), dma((n,)), dma((n, 4)),
        V((256, COLS), BF16), V((8, 256, 256), F32),
        V((HEADS, 16, VH), BF16), V((16, 16, VH), BF16), one, one,
        V((NX, NC, 64, 512), BF16), one, dma((4,)), one, dma((4,)),
        [sum_scratch(True), sum_scratch(False)],
        [[V((NX, NZ, REQ_D, w), BF16), one, one, one, dma((3,))] for _, w in PARTS_A],
        V((NX, NZ, REQ_D, WB), BF16), one, one, V((NX, REQ_D, WB), BF16), one, one,
        V((8, 64, WIDTH), BF16), V((NX, 1, 128), F32), V((7, NX, 1, 128), F32), one, one,
        [
            [V((NY, 64, 2 * w), F32), V((NY, 64, 2 * w), BF16), V((NY, 64, 2 * w), BF16), one, one,
             V((3, 64, 2 * w), BF16), V((3, 64, 2 * w), BF16), one, one]
            for _, w in UNITS
        ],
        [[V((NC, NY, 64, w), BF16), one, dma((3,)), one, one] for _, w in UNITS],
    ]
    return pl.pallas_call(
        kernel,
        out_shape=jax.ShapeDtypeStruct((REQ_D, WIDTH), BF16),
        in_specs=[vmem] * 7 + [anywhere] * 7,
        out_specs=vmem,
        scratch_shapes=scratch,
        compiler_params=pltpu.CompilerParams(
            collective_id=0, has_side_effects=True, vmem_limit_bytes=56 * 1024 * 1024
        ),
        name="layer",
    )(
        page_owner.T, page_slot.T, lengths.reshape(1, REQ_D), resumed.reshape(1, REQ_D), new_latent, residual,
        norm_gain, queries.reshape(256, COLS), pool.transpose(1, 2, 0), value_up, out_proj,
        gate_weight.T, up_weight.T, down_weight,
    )


def solution(mesh):
    return jax.shard_map(
        per_device,
        mesh=mesh,
        in_specs=(
            P("dp", "tp", None), P("dp", None), P("dp", "tp"), P("dp", "tp", None), P("dp", None), P("dp", None),
            P("dp"), P("dp"), P("tp", None, None), P("dp", "tp"), P("tp"), P("tp", "dp"), P("tp", "dp"),
            P("dp", "tp"),
        ),
        out_specs=P("dp", "tp"),
        check_vma=False,
    )
```

```python
import functools

import jax
import jax.numpy as jnp
from jax import lax
from jax.experimental import pallas as pl
from jax.experimental.pallas import tpu as pltpu
from jax.sharding import PartitionSpec as P

MESH = pl.DeviceIdType.MESH
F32, BF16, I32 = jnp.float32, jnp.bfloat16, jnp.int32

NX, NY, NZ, NC = 4, 4, 8, 2
REQ_D = 16
HEADS = 16
COLS = 576
KL = 512
VH = 128
TOK = 8
PAGE = 64
PAGES = 4
USED = 32
WIDTH = 896
PARTS_A, FIRST_B = ((0, 384), (384, 256)), 640
WB = WIDTH - FIRST_B
UNITS = ((0, 256), (256, 256), (512, 64))
PARTS = ((0, 256), (256, 256), (512, 64))
FFD = 576
D = 7168
SCORE_SCALE = 192.0 ** (-0.5)
EPSILON = 1e-06

FAR_Z = (4, 3, 5, 2, 6, 1, 7)
FAR_X = (2, 1, 3)
FAR_Y = (2, 1, 3)
FAR_DP = sorted(
    ((dx, dz) for dx in range(NX) for dz in range(NZ) if dx or dz),
    key=lambda o: -(min(o[0], NX - o[0]) + min(o[1], NZ - o[1])),
)


def send(src, dst, send_sem, recv_sem, device):
    copy = pltpu.make_async_remote_copy(
        src_ref=src,
        dst_ref=dst,
        send_sem=send_sem,
        recv_sem=recv_sem,
        device_id=device,
        device_id_type=MESH,
    )
    copy.start()


def wait_bytes(ref, sem):
    pltpu.make_async_copy(ref, ref, sem).wait()


def column(row, n):
    rows = lax.broadcasted_iota(I32, (n, n), 0)
    lanes = lax.broadcasted_iota(I32, (n, n), 1)
    return jnp.sum(jnp.where(rows == lanes, row, 0), axis=1, keepdims=True)


def dot(a, b):
    return jnp.dot(a, b, preferred_element_type=F32)


def dot_t(a, b):
    return lax.dot_general(a, b, (((1,), (1,)), ((), ())), preferred_element_type=F32)


def kernel(
    owner_ref, slot_ref, len_ref, res_ref, nl_ref, resid_ref, gain_ref,
    q_hbm, pool_hbm, vup_hbm, wo_hbm, wg_hbm, wu_hbm, wd_hbm,
    out_ref,
    q_v, pool_t, pool_v, vup_v, wo_v, wgu_v, wt_v, wd_v, load_sem,
    want_v, asked_v, asked_s, sel_v, sel_s, limit_v, smem_sem, req_ss, req_rs,
    pg_send, pg_recv, pg_ss, pg_rs,
    keys, key_ss, key_rs, sib_ss, sib_rs,
    qt_v, scores_v,
    hd_send, hd_in, hd_ss, hd_rs,
    hb, hb_ss, hb_rs, hs_ss, hs_rs,
    sums,
    gat_a, gat_b, gbz_ss, gbz_rs, resid_b, rb_ss, rb_rs,
    act_v, ssq_send, ssq_recv, ssq_ss, ssq_rs,
    units, hids,
):
    dp, tp = lax.axis_index("dp"), lax.axis_index("tp")
    x, z = dp // NZ, dp % NZ
    y, c = tp // NC, tp % NC

    def at(dx=0, dz=0, dy=0, flip=False):
        core = 1 - c if flip else c
        return (((x + dx) % NX) * NZ + (z + dz) % NZ, ((y + dy) % NY) * NC + core)

    unit_loads = [
        (hbm.at[pl.ds(first, width)], wgu_v.at[pl.ds(2 * first + k * width, width)])
        for first, width in UNITS
        for k, hbm in enumerate((wg_hbm, wu_hbm))
    ]
    loads = [
        pltpu.make_async_copy(src, dst, load_sem.at[i])
        for i, (src, dst) in enumerate(
            [(pool_hbm, pool_t), (q_hbm, q_v), (vup_hbm, vup_v), (wo_hbm, wo_v), (wd_hbm, wd_v), *unit_loads]
        )
    ]
    for load in loads:
        load.start()
    ends = []

    def later(ref, sem):
        ends.append(lambda: wait_bytes(ref, sem))


    barrier = pltpu.get_barrier_semaphore()
    for ox, oz in FAR_DP:
        pl.semaphore_signal(barrier, 1, device_id=at(ox, oz), device_id_type=MESH)
    for oy in FAR_Y:
        pl.semaphore_signal(barrier, 1, device_id=at(dy=oy), device_id_type=MESH)
    pl.semaphore_signal(barrier, 1, device_id=at(flip=True), device_id_type=MESH)
    in_tp = dp // 4
    to_self = jnp.where((tp == in_tp) & (z % 2 == c), 1, 0)

    def greet(k, carry):
        source = 2 * k + c

        @pl.when(jnp.logical_not((source == dp) & (in_tp == tp)))
        def _():
            pl.semaphore_signal(barrier, 1, device_id=(source, in_tp), device_id_type=MESH)

        return carry

    lax.fori_loop(0, 16, greet, 0)

    lengths = column(len_ref[...], REQ_D)
    resumed = column(res_ref[...], REQ_D)
    before = (
        lax.broadcasted_iota(I32, (REQ_D, REQ_D, 1), 1) < lax.broadcasted_iota(I32, (REQ_D, REQ_D, 1), 0)
    ).astype(I32)

    def earlier(v):
        return jnp.sum(before * v[None], axis=1)

    lane = lax.broadcasted_iota(I32, (REQ_D, 128), 1)
    lane_owner = lane % 32
    lane_copy = lane // 32
    page_lane = lax.broadcasted_iota(I32, (REQ_D, USED * TOK), 1) // TOK
    owner_base = jnp.zeros((1, 128), I32)
    read_base = jnp.zeros((1, 128), I32)
    wanted = jnp.zeros((1, 128), I32)
    limit = jnp.zeros((REQ_D, USED * TOK), I32)
    chosen = jnp.zeros((1, USED * TOK), I32)
    for p in range(PAGES):
        owner = column(owner_ref[p : p + 1, :], REQ_D)
        read = jnp.where((resumed == 1) & (lengths > p * PAGE), 1, 0)
        match = jnp.where(lane_owner == owner, read, 0)
        copy = owner_base + earlier(match)
        owner_base = owner_base + jnp.sum(match, axis=0, keepdims=True)
        wanted = wanted + jnp.sum(
            jnp.where((match > 0) & (copy == lane_copy), column(slot_ref[p : p + 1, :], REQ_D), 0),
            axis=0, keepdims=True,
        )
        own_copy = jnp.sum(jnp.where(lane < 32, match * copy, 0), axis=1, keepdims=True)
        read_lanes = jnp.broadcast_to(read, (REQ_D, 128))
        place = (read_base + earlier(read_lanes))[:, 0:1]
        read_base = read_base + jnp.sum(read_lanes, axis=0, keepdims=True)
        here = jnp.where(page_lane == place, read, 0)
        limit = limit + here * (lengths - p * PAGE)
        off_x = (x - owner // NZ + NX) % NX
        off_z = (z - owner % NZ + NZ) % NZ
        source = (off_x * NZ + off_z) * 2 + own_copy
        chosen = chosen + jnp.sum(here * source, axis=0, keepdims=True)
    limit_v[...] = limit.astype(F32)
    want_v[0] = wanted
    asked_v[0] = wanted
    sel_v[0] = chosen
    sel_copy = pltpu.make_async_copy(sel_v, sel_s, smem_sem.at[0])
    sel_copy.start()

    pl.semaphore_wait(barrier, 31 + 4 + 16 - to_self)

    for ox, oz in FAR_DP:
        send(want_v.at[0], asked_v.at[ox * NZ + oz], req_ss, req_rs, at(ox, oz))
    later(asked_v.at[pl.ds(1, 31)], req_ss)

    resid_b[pl.ds(x, 1)] = resid_ref[:, FIRST_B:].reshape(1, REQ_D, WB)
    for ox in FAR_X:
        send(resid_b.at[x], resid_b.at[x], rb_ss, rb_rs, at(dx=ox))
    later(resid_b.at[pl.ds(0, 3)], rb_ss)

    loads[1].wait()
    rows = lax.broadcasted_iota(I32, (256, 256), 0)
    lanes = lax.broadcasted_iota(I32, (256, 256), 1)
    swap = jnp.where(lanes == (rows % 16) * 16 + rows // 16, 1.0, 0.0).astype(BF16)
    qt = dot(swap, q_v[...]).astype(BF16)
    qt_v[...] = qt
    own_all = dot_t(qt, nl_ref[...]) * SCORE_SCALE
    own_diag = lax.broadcasted_iota(I32, (256, 16), 1) == lax.broadcasted_iota(I32, (256, 16), 0) % 16
    own_score = jnp.sum(jnp.where(own_diag, own_all, 0.0), axis=1, keepdims=True)
    loads[0].wait()
    token_row = lax.broadcasted_iota(I32, (1024, 128), 0)
    slot_lane = lax.broadcasted_iota(I32, (1024, 128), 1)
    pages = jnp.zeros((1024, COLS), F32)
    for j in range(TOK):
        spread = jnp.where(token_row == slot_lane * TOK + j, 1.0, 0.0).astype(BF16)
        pages = pages + dot_t(spread, pool_t[j])
    pool_v[...] = pages.astype(BF16).reshape(128, TOK, COLS)
    sel_copy.wait()

    wait_bytes(asked_v.at[pl.ds(1, 31)], req_rs)
    asked_copy = pltpu.make_async_copy(asked_v, asked_s, smem_sem.at[1])
    asked_copy.start()
    asked_copy.wait()

    def gather(n_in, buffer, n_out, first, width):
        pair = [
            pool_v[jnp.clip(asked_s[n_in, 0, 32 * k + dp], 0, 127), :, first : first + width] for k in range(2)
        ]
        buffer[n_out] = jnp.concatenate(pair, axis=0)

    for i, (first, width) in enumerate(PARTS):
        for ox, oz in FAR_DP:
            n_out = ox * NZ + oz
            gather(((NX - ox) % NX) * NZ + (NZ - oz) % NZ, pg_send[i], n_out, first, width)
            send(pg_send[i].at[n_out], pg_recv[i].at[n_out], pg_ss.at[i], pg_rs.at[i], at(ox, oz))
        later(pg_send[i].at[pl.ds(1, 31)], pg_ss.at[i])
    for i, (first, width) in enumerate(PARTS):
        gather(0, pg_recv[i], 0, first, width)

    for load in loads[5:]:
        load.wait()
    same = lax.broadcasted_iota(I32, (128, 128), 0) == lax.broadcasted_iota(I32, (128, 128), 1)
    same = jnp.where(same, 1.0, 0.0).astype(BF16)
    for first in range(0, WIDTH, 128):
        wt_v[first : first + 128] = dot_t(same, wgu_v[:, first : first + 128]).astype(BF16)

    def pass_on(i):
        upper, lower = pl.ds(0, 128), pl.ds(128, 128)
        wait_bytes(keys[i].at[1], key_rs.at[i, 1])
        send(keys[i].at[1, upper], keys[i].at[2, upper], key_ss.at[i], key_rs.at[i, 2], at(dy=1))
        send(keys[i].at[1], keys[i].at[5], sib_ss.at[i], sib_rs.at[i, 1], at(flip=True))
        wait_bytes(keys[i].at[3], key_rs.at[i, 3])
        send(keys[i].at[3, lower], keys[i].at[2, lower], key_ss.at[i], key_rs.at[i, 0], at(dy=3))
        send(keys[i].at[3], keys[i].at[7], sib_ss.at[i], sib_rs.at[i, 3], at(flip=True))

    for i in range(len(PARTS)):
        wait_bytes(pg_recv[i].at[pl.ds(1, 31)], pg_rs.at[i])

        def pick(u, carry):
            pair = []
            for k in range(2):
                source = jnp.clip(sel_s[0, 0, (2 * u + k) * TOK], 0, 63)
                both = pg_recv[i][lax.shift_right_logical(source, 1)]
                pair.append(jnp.where(jnp.bitwise_and(source, 1) == 1, both[TOK:], both[:TOK]))
            keys[i][0, pl.ds(pl.multiple_of(u * 16, 16), 16), :] = jnp.concatenate(pair, axis=0)
            return carry

        lax.fori_loop(0, USED // 2, pick, 0)
        for oy in FAR_Y if i == len(PARTS) - 1 else (1, 3):
            send(keys[i].at[0], keys[i].at[oy], key_ss.at[i], key_rs.at[i, oy], at(dy=oy))
        send(keys[i].at[0], keys[i].at[4], sib_ss.at[i], sib_rs.at[i, 0], at(flip=True))
        later(keys[i].at[pl.ds(0, 3)], key_ss.at[i])
        later(keys[i].at[pl.ds(0, 4)], sib_ss.at[i])
        if i:
            pass_on(i - 1)

    limit = limit_v[...].reshape(1, REQ_D, USED * TOK)
    token = (lax.broadcasted_iota(I32, (1, 1, USED * TOK), 2) % TOK).astype(F32)

    def source_of(n):
        core = c if n < 4 else 1 - c
        return ((y + NY - n % 4) % NY) * NC + core

    def score_block(i, n):
        first, width = PARTS[i]
        block = dot_t(qt_v[:, first : first + width], keys[i][n])
        if i:
            block = scores_v[n] + block
        if i == len(PARTS) - 1:
            usable = limit > token + (source_of(n) * TOK).astype(F32)
            block = (block * SCORE_SCALE).reshape(HEADS, REQ_D, USED * TOK)
            block = jnp.where(usable, block, -jnp.inf).reshape(256, USED * TOK)
        scores_v[n] = block

    for i in range(len(PARTS)):
        if i < len(PARTS) - 1:
            wait_bytes(keys[i].at[2, pl.ds(0, 128)], key_rs.at[i, 2])
            wait_bytes(keys[i].at[2, pl.ds(128, 128)], key_rs.at[i, 0])
            send(keys[i].at[2], keys[i].at[6], sib_ss.at[i], sib_rs.at[i, 2], at(flip=True))
        else:
            for oy in (1, 3, 2):
                wait_bytes(keys[i].at[oy], key_rs.at[i, oy])
                send(keys[i].at[oy], keys[i].at[4 + oy], sib_ss.at[i], sib_rs.at[i, oy], at(flip=True))
        for n in range(4):
            score_block(i, n)
        for oy in (0, 1, 3, 2):
            wait_bytes(keys[i].at[4 + oy], sib_rs.at[i, oy])
            score_block(i, 4 + oy)

    peak = scores_v[0]
    for n in range(1, 8):
        peak = jnp.maximum(peak, scores_v[n])
    top = jnp.maximum(own_score, jnp.max(peak, axis=1, keepdims=True))
    own_weight = jnp.exp(own_score - top)
    weight_lanes = jnp.zeros((256, USED * TOK), F32)
    pieces = [jnp.zeros((256, width), F32) for _, width in PARTS[:-1]]
    for n in range(8):
        weights = jnp.exp(scores_v[n] - top)
        weight_lanes = weight_lanes + weights
        weights = weights.astype(BF16)
        pieces = [piece + dot(weights, keys[i][n]) for i, piece in enumerate(pieces)]
    latent = jnp.concatenate(pieces, axis=1)
    weight_sum = own_weight + jnp.sum(weight_lanes, axis=1, keepdims=True)
    own_latent = nl_ref[:, :KL].astype(F32).reshape(1, REQ_D, KL)
    latent = latent.reshape(HEADS, REQ_D, KL) + own_weight.reshape(HEADS, REQ_D, 1) * own_latent
    latent = (latent / weight_sum.reshape(HEADS, REQ_D, 1)).astype(BF16)

    loads[2].wait()
    for h in range(HEADS):
        hd_send[h] = dot(latent[h], vup_v[h]).astype(BF16)
        target = (4 * tp + h // 4, (h % 4) * NC + z % 2)
        is_me = (target[0] == dp) & (target[1] == tp)

        @pl.when(is_me)
        def _():
            pltpu.make_async_copy(hd_send.at[h], hd_in.at[dp // 2], hd_rs).start()

        @pl.when(jnp.logical_not(is_me))
        def _():
            send(hd_send.at[h], hd_in.at[dp // 2], hd_ss, hd_rs, target)

    def heads_left():
        wait_bytes(hd_in.at[pl.ds(0, 15)], hd_ss)

        @pl.when(to_self == 0)
        def _():
            wait_bytes(hd_in.at[0], hd_ss)

    ends.append(heads_left)

    wait_bytes(hd_in, hd_rs)
    own_cols = pl.ds(pl.multiple_of(y * VH, VH), VH)
    hb[:, pl.ds(c, 1), :, own_cols] = hd_in[...].reshape(NX, 1, 64, VH)
    own_block = hb.at[:, c, :, own_cols]
    for oy in FAR_Y:
        send(own_block, own_block, hb_ss, hb_rs.at[oy], at(dy=oy))
    send(own_block, own_block, hs_ss, hs_rs.at[0], at(flip=True))
    later(hb.at[:, pl.ds(0, 1), :, pl.ds(0, 3 * VH)], hb_ss)
    later(hb.at[:, 0], hs_ss)
    for oy in (1, 3, 2):
        cols = pl.ds(pl.multiple_of(((y + NY - oy) % NY) * VH, VH), VH)
        block = hb.at[:, c, :, cols]
        wait_bytes(block, hb_rs.at[oy])
        send(block, block, hs_ss, hs_rs.at[oy], at(flip=True))
    for oy in range(4):
        wait_bytes(own_block, hs_rs.at[oy])

    def sum_over_dp(rows_x, rows_all, weight, place, bufs, ready_a, gather_b, ready_b):
        parts_a, (b_send, b_recv, b_ss, b_rs, b_own, b_mid, bm_recv, bm_ss, bm_rs) = bufs
        for (first, width), (a_send, a_recv, a_ss, a_rs, *_) in zip(PARTS_A, parts_a):
            for ox in FAR_X:
                a_send[ox - 1] = dot(rows_x((x + ox) % NX), weight[:, first : first + width]).astype(BF16)
                send(a_send.at[ox - 1], a_recv.at[ox - 1], a_ss, a_rs, at(dx=ox))
            later(a_send, a_ss)
        b_send[...] = dot(rows_all(), weight[:, FIRST_B:]).astype(BF16).reshape(NX, NZ, REQ_D, WB)
        for oz in FAR_Z:
            send(b_send.at[:, place((z + oz) % NZ)], b_recv.at[oz - 1], b_ss, b_rs, at(dz=oz))
        later(b_recv, b_ss)
        own = dot(rows_x(x), weight[:, :FIRST_B])
        for (first, width), (a_send, a_recv, a_ss, a_rs, a_own, a_mid, am_recv, am_ss, am_rs) in zip(PARTS_A, parts_a):
            total = own[:, first : first + width]
            wait_bytes(a_recv, a_rs)
            for n in range(3):
                total = total + a_recv[n].astype(F32)
            total = total.reshape(NZ, REQ_D, width)
            a_own[...] = total
            a_mid[...] = total.astype(BF16)
            for oz in FAR_Z:
                send(a_mid.at[place((z + oz) % NZ)], am_recv.at[oz - 1], am_ss, am_rs, at(dz=oz))
            later(am_recv, am_ss)
        total = b_send[:, place(z)].astype(F32)
        wait_bytes(b_recv, b_rs)
        for n in range(7):
            total = total + b_recv[n].astype(F32)
        if gather_b:
            bm_recv[x] = total.astype(BF16)
            for ox in FAR_X:
                send(bm_recv.at[x], bm_recv.at[x], bm_ss, bm_rs, at(dx=ox))
            later(bm_recv.at[pl.ds(0, 3)], bm_ss)
        else:
            b_own[...] = total
            b_mid[...] = total.astype(BF16)
            for ox in FAR_X:
                send(b_mid.at[(x + ox) % NX], bm_recv.at[ox - 1], bm_ss, bm_rs, at(dx=ox))
            later(bm_recv, bm_ss)
        for part, (_, _, _, _, a_own, _, am_recv, _, am_rs) in enumerate(parts_a):
            mine = a_own[place(z)]
            wait_bytes(am_recv, am_rs)
            for n in range(7):
                mine = mine + am_recv[n].astype(F32)
            ready_a(part, mine)
        if gather_b:
            wait_bytes(bm_recv.at[pl.ds(0, 3)], bm_rs)
            mine = bm_recv[0].astype(F32)
            for n in range(1, NX):
                mine = mine + bm_recv[n].astype(F32)
        else:
            mine = b_own[x]
            wait_bytes(bm_recv, bm_rs)
            for n in range(3):
                mine = mine + bm_recv[n].astype(F32)
        ready_b(mine)

    def stream_a(part, attended):
        first, width = PARTS_A[part]
        gat, z_ss, z_rs, _, _ = gat_a[part]
        gat[x, z] = (resid_ref[:, first : first + width].astype(F32) + attended).astype(BF16)
        for oz in FAR_Z:
            send(gat.at[x, z], gat.at[x, z], z_ss, z_rs, at(dz=oz))
        later(gat.at[0, pl.ds(0, 7)], z_ss)

    def stream_b(attended):
        wait_bytes(resid_b.at[pl.ds(0, 3)], rb_rs)
        gat_b[:, z] = (resid_b[...].astype(F32) + attended).astype(BF16)
        for oz in FAR_Z:
            send(gat_b.at[:, z], gat_b.at[:, z], gbz_ss, gbz_rs, at(dz=oz))
        later(gat_b.at[:, pl.ds(0, 7)], gbz_ss)

    loads[3].wait()
    sum_over_dp(
        lambda xx: hb[xx].reshape(128, 512), lambda: hb[...].reshape(512, 512), wo_v,
        lambda zz: (zz % 2) * 4 + zz // 2, sums[0], stream_a, True, stream_b,
    )
    for gat, _, z_rs, x_ss, x_rs in gat_a:
        wait_bytes(gat.at[0, pl.ds(0, 7)], z_rs)
        for ox in FAR_X:
            send(gat.at[x], gat.at[x], x_ss, x_rs.at[ox - 1], at(dx=ox))
        later(gat.at[pl.ds(0, 3)], x_ss)

    def widen(block, gain):
        return (block.astype(F32) * gain).astype(BF16)

    def square_sums():
        for xx in range(NX):
            total = jnp.zeros((8, 128), F32)
            for gat in [gat[0] for gat in gat_a] + [gat_b]:
                block = gat[xx].reshape(128, -1).astype(F32)
                square = block * block
                high = square.astype(BF16)
                low = (square - high.astype(F32)).astype(BF16)
                ones = jnp.ones((8, block.shape[1]), BF16)
                total = total + dot_t(ones, high) + dot_t(ones, low)
            ssq_send[xx] = total[0:1]
        tp_others = [(2, True), (2, False), (1, True), (3, True), (1, False), (3, False), (0, True)]
        for n, (oy, flip) in enumerate(tp_others):
            send(ssq_send, ssq_recv.at[n], ssq_ss, ssq_rs, at(dy=oy, flip=flip))
        later(ssq_recv, ssq_ss)

    gain = gain_ref[...].reshape(1, WIDTH)

    for (first, width), (gat, _, _, _, x_rs) in zip(PARTS_A, gat_a):
        for ox in (0, 1, 3, 2):
            xx = (x + NX - ox) % NX
            if ox:
                wait_bytes(gat.at[xx], x_rs.at[ox - 1])
            act = widen(gat[xx].reshape(128, width), gain[:, first : first + width])
            act_v[pl.ds(xx * 2, 2), :, first : first + width] = act.reshape(2, 64, width)
    wait_bytes(gat_b.at[:, pl.ds(0, 7)], gbz_rs)
    for xx in range(NX):
        act = widen(gat_b[xx].reshape(128, WB), gain[:, FIRST_B:])
        act_v[2 * xx : 2 * xx + 2, :, FIRST_B:] = act.reshape(2, 64, WB)

    ways = (2, 1, 3, 0)

    def products(half, part):
        first, width = UNITS[part]
        act = jnp.concatenate([act_v[half * 4 + (y + oy) % NY] for oy in ways], axis=0)
        return dot(act, wt_v[:, 2 * first : 2 * (first + width)]).reshape(NY, 64, 2 * width)

    def start_part(part):
        _, to_core, from_core, core_ss, core_rs, *_ = units[part]
        to_core[...] = products(1 - c, part).astype(BF16)
        send(to_core, from_core, core_ss, core_rs, at(flip=True))
        later(to_core, core_ss)

    start_part(0)
    for part, (own, _, from_core, _, core_rs, to_y, from_y, y_ss, y_rs) in enumerate(units):
        own[...] = products(c, part)
        if part + 1 < len(units):
            start_part(part + 1)
        if part == 1:
            square_sums()
        wait_bytes(from_core, core_rs)
        for n in range(3):
            to_y[n] = (own[n] + from_core[n].astype(F32)).astype(BF16)
            send(to_y.at[n], from_y.at[n], y_ss, y_rs, at(dy=ways[n]))
        later(to_y, y_ss)
    wait_bytes(ssq_recv, ssq_rs)
    squares = ssq_send[...]
    for n in range(7):
        squares = squares + ssq_recv[n]
    row_id = lax.broadcasted_iota(I32, (64, 128), 0) + c * 256 + y * 64
    lane_id = lax.broadcasted_iota(I32, (64, 128), 1)
    mean = jnp.zeros((64, 1), F32)
    for n in range(NX):
        mean = mean + jnp.sum(
            jnp.where(row_id == lane_id + 128 * n, squares[n], 0.0), axis=1, keepdims=True
        )
    scale = lax.rsqrt(mean / D + EPSILON)
    for (_, width), (own, _, from_core, _, _, _, from_y, _, y_rs), (hid, hy_ss, hy_rs, hc_ss, hc_rs) in zip(
        UNITS, units, hids
    ):
        both = own[3] + from_core[3].astype(F32)
        wait_bytes(from_y, y_rs)
        for n in range(3):
            both = both + from_y[n].astype(F32)
        both = both * scale
        gate, up = both[:, :width], both[:, width:]
        hid[c, y] = (gate / (1.0 + jnp.exp(-gate)) * up).astype(BF16)
        for oy in FAR_Y:
            send(hid.at[c, y], hid.at[c, y], hy_ss, hy_rs.at[oy - 1], at(dy=oy))
        send(hid.at[c, y], hid.at[c, y], hc_ss, hc_rs, at(flip=True))
        later(hid.at[0, pl.ds(0, 3)], hy_ss)
        later(hid.at[0], hc_ss)
    for hid, _, hy_rs, hc_ss, hc_rs in hids:
        for oy in (1, 3, 2):
            yy = (y + NY - oy) % NY
            wait_bytes(hid.at[c, yy], hy_rs.at[oy - 1])
            send(hid.at[c, yy], hid.at[c, yy], hc_ss, hc_rs, at(flip=True))
    for hid, _, _, _, hc_rs in hids:
        wait_bytes(hid.at[1 - c], hc_rs)

    loads[4].wait()

    def out_a(part, lowered):
        first, width = PARTS_A[part]
        out_ref[:, first : first + width] = (gat_a[part][0][x, z].astype(F32) + lowered).astype(BF16)

    def out_b(lowered):
        out_ref[:, FIRST_B:] = (gat_b[x, z].astype(F32) + lowered).astype(BF16)

    sum_over_dp(
        lambda xx: jnp.concatenate(
            [hid[0][xx // 2, pl.ds((xx % 2) * 2, 2)].reshape(128, -1) for hid in hids], axis=1
        ),
        lambda: jnp.concatenate([hid[0][...].reshape(512, -1) for hid in hids], axis=1), wd_v,
        lambda zz: zz, sums[1], out_a, False, out_b,
    )
    for end in ends:
        end()


def per_device(
    queries, new_latent, residual, pool, page_owner, page_slot, lengths, resumed,
    value_up, out_proj, norm_gain, gate_weight, up_weight, down_weight,
):
    vmem = pl.BlockSpec(memory_space=pltpu.VMEM)
    anywhere = pl.BlockSpec(memory_space=pl.ANY)
    dma, V = pltpu.SemaphoreType.DMA, pltpu.VMEM
    one, n = dma, len(PARTS)
    def sum_scratch(gather_b):
        return [
            [
                [V((3, 128, w), BF16), V((3, 128, w), BF16), one, one,
                 V((NZ, REQ_D, w), F32), V((NZ, REQ_D, w), BF16), V((7, REQ_D, w), BF16), one, one]
                for _, w in PARTS_A
            ],
            [V((NX, NZ, REQ_D, WB), BF16), V((7, NX, REQ_D, WB), BF16), one, one,
             V((NX, REQ_D, WB), F32), V((NX, REQ_D, WB), BF16),
             V((NX, NX, REQ_D, WB) if gather_b else (3, REQ_D, WB), BF16), one, one],
        ]

    scratch = [
        V((256, COLS), BF16), V((TOK, COLS, 128), BF16), V((128, TOK, COLS), BF16), V((HEADS, KL, VH), BF16),
        V((512, WIDTH), BF16), V((2 * FFD, WIDTH), BF16), V((WIDTH, 2 * FFD), BF16), V((FFD, WIDTH), BF16), dma((5 + 2 * len(UNITS),)),
        V((1, 1, 128), I32), V((32, 1, 128), I32), pltpu.SMEM((32, 1, 128), I32),
        V((1, 1, 256), I32), pltpu.SMEM((1, 1, 256), I32), V((REQ_D, 256), F32), dma((2,)), one, one,
        [V((32, 16, w), BF16) for _, w in PARTS], [V((32, 16, w), BF16) for _, w in PARTS], dma((n,)), dma((n,)),
        [V((8, 256, w), BF16) for _, w in PARTS], dma((n,)), dma((n, 4)), dma((n,)), dma((n, 4)),
        V((256, COLS), BF16), V((8, 256, 256), F32),
        V((HEADS, 16, VH), BF16), V((16, 16, VH), BF16), one, one,
        V((NX, NC, 64, 512), BF16), one, dma((4,)), one, dma((4,)),
        [sum_scratch(True), sum_scratch(False)],
        [[V((NX, NZ, REQ_D, w), BF16), one, one, one, dma((3,))] for _, w in PARTS_A],
        V((NX, NZ, REQ_D, WB), BF16), one, one, V((NX, REQ_D, WB), BF16), one, one,
        V((8, 64, WIDTH), BF16), V((NX, 1, 128), F32), V((7, NX, 1, 128), F32), one, one,
        [
            [V((NY, 64, 2 * w), F32), V((NY, 64, 2 * w), BF16), V((NY, 64, 2 * w), BF16), one, one,
             V((3, 64, 2 * w), BF16), V((3, 64, 2 * w), BF16), one, one]
            for _, w in UNITS
        ],
        [[V((NC, NY, 64, w), BF16), one, dma((3,)), one, one] for _, w in UNITS],
    ]
    return pl.pallas_call(
        kernel,
        out_shape=jax.ShapeDtypeStruct((REQ_D, WIDTH), BF16),
        in_specs=[vmem] * 7 + [anywhere] * 7,
        out_specs=vmem,
        scratch_shapes=scratch,
        compiler_params=pltpu.CompilerParams(
            collective_id=0, has_side_effects=True, vmem_limit_bytes=56 * 1024 * 1024
        ),
        name="layer",
    )(
        page_owner.T, page_slot.T, lengths.reshape(1, REQ_D), resumed.reshape(1, REQ_D), new_latent, residual,
        norm_gain, queries.reshape(256, COLS), pool.transpose(1, 2, 0), value_up, out_proj,
        gate_weight.T, up_weight.T, down_weight,
    )


def solution(mesh):
    return jax.shard_map(
        per_device,
        mesh=mesh,
        in_specs=(
            P("dp", "tp", None), P("dp", None), P("dp", "tp"), P("dp", "tp", None), P("dp", None), P("dp", None),
            P("dp"), P("dp"), P("tp", None, None), P("dp", "tp"), P("tp"), P("tp", "dp"), P("tp", "dp"),
            P("dp", "tp"),
        ),
        out_specs=P("dp", "tp"),
        check_vma=False,
    )
```
